256 devices in a mesh: edge: 64 (over y, z, core), rep: 4 (over x).
Axes of the slice: x: 4, y: 4, z: 8, core: 2. Of those that a mesh axis runs over, the one named last changes fastest.
Arguments:
- entities: float32 [4, 65536, 400], P('rep', 'edge'), may hold values from -3 to 3
- ent_accum: float32 [4, 65536], P('rep', 'edge'), may hold values from 0.01 to 0.1
- relations: float32 [1000, 400], replicated, may hold values from -3 to 3
- rel_accum: float32 [1000], replicated, may hold values from 1 to 10
- heads: int32 [4, 2, 8192], P('rep', None, 'edge'), may hold values from 0 to 65535, as said below
- tails: int32 [4, 2, 8192], P('rep', None, 'edge'), may hold values from 0 to 65535, as said below
- negatives: int32 [4, 2, 65536], P('rep', None, 'edge'), may hold values from 0 to 65535, as said below
- rel_ids: int32 [4, 2, 8192], P('rep', None, 'edge'), may hold values from 0 to 999
Outputs:
- new_entities: float32 [4, 65536, 400], P('rep', 'edge')
- new_ent_accum: float32 [4, 65536], P('rep', 'edge')
- new_relations: float32 [1000, 400], replicated
- new_rel_accum: float32 [1000], replicated
The draws below stay inside these ranges and needn't reach their ends.
Inputs may be any that keep to these rules, and one draw needn't show every extreme that they name: Row i of a bucket belongs to owner i // 1024. In each bucket, step and block, at most 40 of the block's 1280 requests (heads, tails, negatives together) name rows of one owner, and in every bucket and step one owner is named exactly 40 times by every block. `tails`: drawn together with heads under the same bound. `negatives`: drawn together with heads under the same bound.
All inputs are finite; a program needn't handle non-finite values.
Results may differ from the reference program's by a relative error of at most 0.0042.
Values may be sent and summed in bfloat16 or wider, within the bound.
No kernel may reach another device: no remote copies, remote signals or barrier semaphores. Data moves between devices by JAX's collectives and lax.ppermute only.
A program may use at most 64 MiB of HBM per device.

```python
import math
import jax
import jax.numpy as jnp
from jax import lax

W = 400
NREL = 1000
NEG = 1024
STEPS = 2
SPAN = 128
ROWS_DEV = 1024
OWNERS = 64
BUCKETS = 4
ENT = 65536
EDGES = 8192
REQ = 1280
CAP = 40


def request_draw(key):
    base = jax.random.fold_in(key, 7)
    keys = jax.random.split(base, 5)
    blocks = (BUCKETS, STEPS, OWNERS)
    slot_total = OWNERS * CAP
    random_jitter = jax.random.randint(keys[0], blocks + (slot_total,), 0, 2 ** 20)
    bucket_levels = jax.random.randint(keys[1], (BUCKETS, STEPS, 1, OWNERS), 0, 4) * 2 ** 18
    largest_bucket = jax.random.randint(keys[2], (BUCKETS, STEPS, 1, 1), 0, OWNERS)
    slot_holder = jnp.arange(slot_total, dtype=jnp.int32) // CAP
    extra_reward = jnp.take(bucket_levels, slot_holder, axis=3)
    extra_reward = extra_reward + jnp.where(slot_holder[None, None, None, :] == largest_bucket, 2 ** 22, 0)
    triple_score = random_jitter + extra_reward
    chosen = jnp.argsort(-triple_score, axis=-1, stable=True)[..., :REQ]
    owner_ids = chosen // CAP
    shuffle = jnp.argsort(jax.random.randint(keys[3], blocks + (REQ,), 0, 2 ** 30), axis=-1, stable=True)
    owner_ids = jnp.take_along_axis(owner_ids, shuffle, axis=-1)
    local_rows = jax.random.randint(keys[4], blocks + (REQ,), 0, ROWS_DEV)
    return (owner_ids * ROWS_DEV + local_rows).astype(jnp.int32)


def draw_heads(key, part):
    return request_draw(key)[..., :SPAN].reshape(BUCKETS, STEPS, OWNERS * SPAN)


def draw_tails(key, part):
    return request_draw(key)[..., SPAN:2 * SPAN].reshape(BUCKETS, STEPS, OWNERS * SPAN)


def draw_negatives(key, part):
    return request_draw(key)[..., 2 * SPAN:].reshape(BUCKETS, STEPS, OWNERS * NEG)


def touch_ends(entries, own_key, least, top_value):
    longest = entries.shape.index(max(entries.shape))
    spots = []
    for shift in (0, 1):
        where = [jax.random.randint(jax.random.fold_in(own_key, axis), (), 0, length) for axis, length in enumerate(entries.shape)]
        where[longest] = (where[longest] + shift) % entries.shape[longest]
        spots.append(tuple(where))
    return entries.at[spots[0]].set(least).at[spots[1]].set(top_value)


def block_scale(own_key, shape, cuts, low, high):
    gain, own = 1.0, jax.random.fold_in(own_key, 6)
    for axis_at, shards_of in cuts:
        draws = jnp.exp(jax.random.uniform(jax.random.fold_in(own, axis_at), (shards_of,), jnp.float32, low / len(cuts), high / len(cuts)))
        gain = gain * jnp.repeat(draws, shape[axis_at] // shards_of).reshape([-1 if axis == axis_at else 1 for axis in range(len(shape))])
    return gain


def scatter_about(key, extent, width, most, cuts=(), kind=jnp.bfloat16):
    entries = width * jax.random.normal(key, extent, jnp.float32)
    if cuts:
        entries = entries * block_scale(key, extent, cuts, -0.22, 0.18)
    return jnp.clip(entries, -most, most).astype(kind)


def setup_inputs(seed: int = 0) -> dict:
    arg_keys = jax.random.split(jax.random.key(seed), 9)
    return {
        "entities": scatter_about(arg_keys[0], (BUCKETS, ENT, W), 0.5, 3.0, ((0, 4), (1, 64)), jnp.float32),
        "ent_accum": jnp.clip(jnp.exp(math.log(0.1) - 2.3025851 * jax.random.uniform(arg_keys[1], (BUCKETS, ENT), jnp.float32) ** block_scale(arg_keys[1], (BUCKETS, ENT), ((0, 4), (1, 64)), -0.2, 0.2)), 0.01, 0.1),
        "relations": scatter_about(arg_keys[2], (NREL, W), 0.5, 3.0, (), jnp.float32),
        "rel_accum": jnp.clip(jnp.exp(jax.random.uniform(arg_keys[3], (NREL,), jnp.float32, math.log(1.0), math.log(10.0))), 1.0, 10.0),
        "heads": draw_heads(jax.random.fold_in(arg_keys[8], 71), 0),
        "tails": draw_tails(jax.random.fold_in(arg_keys[8], 71), 0),
        "negatives": draw_negatives(jax.random.fold_in(arg_keys[8], 71), 0),
        "rel_ids": touch_ends(jax.random.randint(arg_keys[7], (BUCKETS, STEPS, EDGES), 0, NREL), jax.random.fold_in(arg_keys[7], 1), 0, NREL - 1).astype(jnp.int32),
    }


entity_rate = 0.1
relation_rate = 0.1

def complex_parts(rows):
    half = rows.shape[-1] // 2
    return (rows[:, :half], rows[:, half:])

def span_grads(head_entity_rows, tail_rows, negative_rows, relation_rows):
    negative_count = negative_rows.shape[0]
    head_full = head_entity_rows.astype(jnp.float32)
    tail_full = tail_rows.astype(jnp.float32)
    head_re, head_im = complex_parts(head_full)
    tail_re, tail_im = complex_parts(tail_full)
    rel_re, rel_im = complex_parts(relation_rows)
    query_tail = jnp.concatenate([head_re * rel_re - head_im * rel_im, head_re * rel_im + head_im * rel_re], axis=1)
    query_head = jnp.concatenate([rel_re * tail_re + rel_im * tail_im, rel_re * tail_im - rel_im * tail_re], axis=1)
    positive_score = lax.optimization_barrier(jnp.sum(query_tail * tail_full, axis=1))
    tail_query16 = query_tail.astype(jnp.bfloat16)
    head_query16 = query_head.astype(jnp.bfloat16)
    contract_last = (((1,), (1,)), ((), ()))
    scores_tail = lax.dot_general(tail_query16, negative_rows, contract_last, preferred_element_type=jnp.float32)
    scores_head = lax.dot_general(head_query16, negative_rows, contract_last, preferred_element_type=jnp.float32)
    weight_tail = (jax.nn.sigmoid(scores_tail) / negative_count).astype(jnp.bfloat16)
    weight_head = (jax.nn.sigmoid(scores_head) / negative_count).astype(jnp.bfloat16)
    positive_weight = -jax.nn.sigmoid(-positive_score)[:, None]
    grad_tail_query = positive_weight * tail_full + jnp.dot(weight_tail, negative_rows, preferred_element_type=jnp.float32)
    grad_head_query = jnp.dot(weight_head, negative_rows, preferred_element_type=jnp.float32)
    contract_first = (((0,), (0,)), ((), ()))
    grad_negative = lax.dot_general(weight_tail, tail_query16, contract_first, preferred_element_type=jnp.float32)
    grad_negative = grad_negative + lax.dot_general(weight_head, head_query16, contract_first, preferred_element_type=jnp.float32)
    pull_re, pull_im = complex_parts(grad_tail_query)
    push_re, push_im = complex_parts(grad_head_query)
    grad_head = jnp.concatenate([pull_re * rel_re + pull_im * rel_im, pull_im * rel_re - pull_re * rel_im], axis=1)
    grad_tail = positive_weight * query_tail + jnp.concatenate([push_re * rel_re - push_im * rel_im, push_re * rel_im + push_im * rel_re], axis=1)
    grad_relation = jnp.concatenate([pull_re * head_re + pull_im * head_im + push_re * tail_re + push_im * tail_im, pull_im * head_re - pull_re * head_im + push_re * tail_im - push_im * tail_re], axis=1)
    return (jnp.concatenate([grad_head, grad_tail, grad_negative], axis=0), grad_relation)

def reference(entities, ent_accum, relations, rel_accum, heads, tails, negatives, rel_ids):
    tables = [entities[bucket] for bucket in range(BUCKETS)]
    accums = [ent_accum[bucket] for bucket in range(BUCKETS)]
    rel_table = relations
    rel_state = rel_accum
    for step_index in range(STEPS):
        relation_total = jnp.zeros((NREL, W), jnp.float32)
        new_tables = []
        new_accums = []
        for bucket in range(BUCKETS):
            table = tables[bucket]
            head_all = heads[bucket, step_index]
            tail_all = tails[bucket, step_index]
            negative_all = negatives[bucket, step_index]
            relation_all = rel_ids[bucket, step_index]

            def one_block(carry, block):
                entity_grad, relation_sum = carry
                start = (block * SPAN).astype(jnp.int32)
                head_ids = lax.dynamic_slice_in_dim(head_all, start, SPAN)
                tail_ids = lax.dynamic_slice_in_dim(tail_all, start, SPAN)
                relation_ids = lax.dynamic_slice_in_dim(relation_all, start, SPAN)
                negative_ids = lax.dynamic_slice_in_dim(negative_all, (block * NEG).astype(jnp.int32), NEG)
                requests = jnp.concatenate([head_ids, tail_ids, negative_ids])
                fetched = table[requests].astype(jnp.bfloat16)
                request_grads, relation_grads = span_grads(fetched[:SPAN], fetched[SPAN:2 * SPAN], fetched[2 * SPAN:], rel_table[relation_ids])
                rounded = lax.optimization_barrier(request_grads.astype(jnp.bfloat16)).astype(jnp.float32)
                entity_grad = entity_grad.at[requests].add(rounded)
                relation_sum = relation_sum + jax.ops.segment_sum(relation_grads, relation_ids, num_segments=NREL)
                return ((entity_grad, relation_sum), None)
            start_carry = (jnp.zeros((ENT, W), jnp.float32), relation_total)
            (entity_grad, relation_total), _ = lax.scan(one_block, start_carry, jnp.arange(OWNERS, dtype=jnp.int32))
            accum = accums[bucket] + lax.optimization_barrier(jnp.mean(entity_grad * entity_grad, axis=1))
            new_accums.append(accum)
            new_tables.append(table - entity_rate * entity_grad / jnp.sqrt(accum)[:, None])
        tables = new_tables
        accums = new_accums
        rel_state = rel_state + lax.optimization_barrier(jnp.mean(relation_total * relation_total, axis=1))
        rel_table = rel_table - relation_rate * relation_total / jnp.sqrt(rel_state)[:, None]
    return (jnp.stack(tables), jnp.stack(accums), rel_table, rel_state)
```

```python
import jax
import jax.numpy as jnp
from jax import lax
from jax.experimental import pallas as pl
from jax.experimental.pallas import tpu as pltpu
from jax.sharding import PartitionSpec as P

F32, BF16, I32 = jnp.float32, jnp.bfloat16, jnp.int32
RATE = 0.1
OWN = 64
CAP = 40
SLOTS = OWN * CAP
WIDTH = 400
HALF = 200
BODY = 384
REL = 1024


def iota(shape, dim):
    return lax.broadcasted_iota(I32, shape, dim)


def one_hot(hit):
    return jnp.where(hit, 1.0, 0.0).astype(BF16)


def dot(a, b, dims=((1,), (0,))):
    return lax.dot_general(a, b, (dims, ((), ())), preferred_element_type=F32)


def fold_tail(x):
    x = x + pltpu.roll(x, 64, 1)
    x = x + pltpu.roll(x, 32, 1)
    return x + pltpu.roll(x, 16, 1)


def spread_tail(x16):
    rows = x16.shape[0]
    return fold_tail(jnp.concatenate([x16, jnp.zeros((rows, 112), F32)], axis=1))


def to_wide(x):
    return jnp.concatenate([x[:, :BODY], spread_tail(x[:, BODY:])], axis=1)


def to_narrow(x):
    return jnp.concatenate([x[:, :BODY], fold_tail(x[:, BODY:])[:, :16]], axis=1)


def pack(rows):
    group = iota((8, 128), 1) // 16
    tail = jnp.zeros((8, 128), F32)
    for i in range(5):
        tail = jnp.where(group == i, rows[8 * i : 8 * i + 8, BODY:], tail)
    return jnp.concatenate([rows[:, :128], rows[:, 128:256], rows[:, 256:384], tail], axis=0)


def unpack(block):
    group = iota((8, 128), 1) // 16
    tail = jnp.concatenate([jnp.where(group == i, block[120:], 0.0) for i in range(5)], axis=0)
    return jnp.concatenate([block[:40], block[40:80], block[80:120], tail], axis=1)


def unpack_all(wire_ref, rows_ref):
    def pair(e, _):
        two = [unpack(wire_ref[2 * e + k].astype(F32)) for k in range(2)]
        at = pl.multiple_of(e * 2 * CAP, 2 * CAP)
        rows_ref[pl.ds(at, 2 * CAP), :] = jnp.concatenate(two, axis=0).astype(BF16)
        return 0

    lax.fori_loop(0, OWN // 2, pair, 0)


def lane_to_column(row):
    return jnp.transpose(jnp.broadcast_to(row, (128, 128)))


def prepare(heads_ref, tails_ref, negatives_ref, send_ref, negative_ref, slots_ref):
    count = 2 * heads_ref.shape[2] + negatives_ref.shape[2]
    steps = heads_ref.shape[1]
    before = one_hot(iota((128, 128), 0) < iota((128, 128), 1))
    send = jnp.zeros((OWN, 128), F32)
    negative = jnp.zeros((OWN, 128), F32)
    for s in range(steps):
        requests = jnp.concatenate(
            [heads_ref[0, s : s + 1, :], tails_ref[0, s : s + 1, :], negatives_ref[0, s : s + 1, :]], axis=1
        )
        owner = lax.shift_right_logical(requests, 10)
        local = requests & 1023
        at_owner = jnp.where(iota((OWN, count), 0) == owner, 1.0, 0.0)
        seen = jnp.zeros((OWN, 1), F32)
        ranks = []
        for j in range(count // 128):
            part = at_owner[:, 128 * j : 128 * j + 128]
            earlier = dot(part.astype(BF16), before) + seen
            ranks.append(jnp.sum(part * earlier, axis=0, keepdims=True))
            seen = seen + jnp.sum(part, axis=1, keepdims=True)
        rank = jnp.concatenate(ranks, axis=1).astype(I32)
        at_rank = one_hot(iota((128, count), 0) == rank + CAP * s)
        high = (at_owner * lax.shift_right_logical(local, 5).astype(F32)).astype(BF16)
        low = (at_owner * (local & 31).astype(F32)).astype(BF16)
        last = ((1,), (1,))
        send = send + dot(high, at_rank, last) * 32.0 + dot(low, at_rank, last)
        chosen = jnp.where(iota((OWN, count), 1) >= 256, at_owner, 0.0).astype(BF16)
        negative = negative + dot(chosen, at_rank, last)
        slots_ref[s : s + 1, :] = (owner * CAP + rank)[:, :256]
    send_ref[...] = send.astype(I32)
    negative_ref[...] = negative


def gather_rows(named_ref, step, wide_ref, wire_ref):
    named = named_ref[...].astype(F32)
    named = jnp.transpose(jnp.concatenate([named, named], axis=0))
    named = named[CAP * step : CAP * step + CAP, :OWN].astype(I32)
    for g in range(OWN // 8):
        columns = jnp.concatenate([named[:, 8 * g + j : 8 * g + j + 1] for j in range(8)], axis=0)
        hit = one_hot(columns == iota((8 * CAP, 1024), 1))
        rows = dot(hit, wide_ref[...])
        for j in range(8):
            wire_ref[8 * g + j] = pack(rows[CAP * j : CAP * j + CAP]).astype(BF16)


def first_rows(table_ref, named_ref, wire_ref, wide_ref):
    wide_ref[...] = to_wide(table_ref[0]).astype(BF16)
    gather_rows(named_ref, 0, wide_ref, wire_ref)


def update(step, last, wire_in_ref, flat_ref, table_ref, accum_ref, named_ref, *rest):
    if last:
        new_table_ref, new_accum_ref, grads_ref = rest
    else:
        new_table_ref, new_accum_ref, wire_ref, grads_ref, wide_ref = rest
    unpack_all(wire_in_ref, grads_ref)
    for b in range(8):
        rows = slice(128 * b, 128 * b + 128)
        hit = one_hot(iota((128, SLOTS), 0) + 128 * b == flat_ref[step : step + 1, :])
        total = dot(hit, grads_ref[...])
        total = to_narrow(total)
        accum = lane_to_column(accum_ref[b : b + 1, :])
        accum = accum + jnp.sum(total * total, axis=1, keepdims=True) / WIDTH
        new_accum_ref[b : b + 1, :] = jnp.transpose(accum)[:1]
        new = table_ref[0, rows, :] - total * (RATE * lax.rsqrt(accum[:, :1]))
        new_table_ref[0, rows, :] = new
        if not last:
            wide_ref[rows, :] = to_wide(new).astype(BF16)
    if not last:
        gather_rows(named_ref, step + 1, wide_ref, wire_ref)


def complex_parts(x):
    return x[:, :HALF], x[:, HALF:]


def join(re, im):
    return jnp.concatenate([re, im], axis=1)


def split3(x):
    a = x.astype(BF16)
    x = x - a.astype(F32)
    b = x.astype(BF16)
    return a, b, (x - b.astype(F32)).astype(BF16)


def block(
    step, wire_in_ref, slots_ref, negative_ref, relations_ref, rel_ids_ref,
    wire_ref, relation_grad_ref, rows_ref, weights_ref,
):
    edges, parts = 128, 4
    part = SLOTS // parts
    per = OWN // parts
    unpack_all(wire_in_ref, rows_ref)
    slots = slots_ref[step : step + 1, :]
    slots_column = jnp.concatenate(
        [lane_to_column(slots[:, 128 * k : 128 * k + 128].astype(F32))[:, :1] for k in range(2)], axis=0
    ).astype(I32)
    fetched = jnp.zeros((2 * edges, 512), F32)
    for g in range(parts):
        hit = one_hot(slots_column == iota((2 * edges, part), 1) + part * g)
        fetched = fetched + dot(hit, rows_ref[part * g : part * g + part, :])
    fetched = to_narrow(fetched)
    head, tail = fetched[:edges], fetched[edges:]
    rel_ids = rel_ids_ref[0, step : step + 1, :]
    rel_column = lane_to_column(rel_ids.astype(F32))[:, :1].astype(I32)
    rel_hit = one_hot(rel_column == iota((edges, REL), 1))
    relation = jnp.zeros((edges, WIDTH), F32)
    for piece in reversed(split3(relations_ref[...])):
        relation = relation + dot(rel_hit, piece)

    head_re, head_im = complex_parts(head)
    tail_re, tail_im = complex_parts(tail)
    rel_re, rel_im = complex_parts(relation)
    query_tail = join(head_re * rel_re - head_im * rel_im, head_re * rel_im + head_im * rel_re)
    query_head = join(rel_re * tail_re + rel_im * tail_im, rel_re * tail_im - rel_im * tail_re)
    positive = jnp.sum(query_tail * tail, axis=1, keepdims=True)
    queries = to_wide(jnp.concatenate([query_tail, query_head], axis=0)).astype(BF16)
    pull = jnp.zeros((2 * edges, 512), F32)
    for g in range(parts):
        here = slice(part * g, part * g + part)
        scores = dot(queries, rows_ref[here, :], ((1,), (1,)))
        weights = jax.nn.sigmoid(scores) * (negative_ref[step : step + 1, here] / 1024)
        weights = weights.astype(BF16)
        weights_ref[:, here] = weights
        pull = pull + dot(weights, rows_ref[here, :])
    pull = to_narrow(pull)
    positive_weight = -jax.nn.sigmoid(-positive)
    pull_re, pull_im = complex_parts(positive_weight * tail + pull[:edges])
    push_re, push_im = complex_parts(pull[edges:])
    grad_head = join(pull_re * rel_re + pull_im * rel_im, pull_im * rel_re - pull_re * rel_im)
    grad_tail = positive_weight * query_tail + join(
        push_re * rel_re - push_im * rel_im, push_re * rel_im + push_im * rel_re
    )
    grad_relation = join(
        pull_re * head_re + pull_im * head_im + push_re * tail_re + push_im * tail_im,
        pull_im * head_re - pull_re * head_im + push_re * tail_im - push_im * tail_re,
    )
    rel_spread = one_hot(iota((REL, edges), 0) == rel_ids)
    relation_grad = jnp.zeros((REL, WIDTH), F32)
    for piece in reversed(split3(grad_relation)):
        relation_grad = relation_grad + dot(rel_spread, piece)
    relation_grad_ref[...] = relation_grad
    edge_grads = to_wide(jnp.concatenate([grad_head, grad_tail], axis=0)).astype(BF16)
    for g in range(parts):
        here = slice(part * g, part * g + part)
        grads = dot(weights_ref[:, here], queries, ((0,), (0,)))
        hit = one_hot(iota((part, 2 * edges), 0) + part * g == slots)
        grads = grads + dot(hit, edge_grads)
        for j in range(per):
            wire_ref[per * g + j] = pack(grads[CAP * j : CAP * j + CAP]).astype(BF16)


def relation_update(grad_ref, table_ref, state_ref, new_table_ref, new_state_ref):
    for b in range(REL // 128):
        rows = slice(128 * b, 128 * b + 128)
        total = grad_ref[rows, :]
        state = lane_to_column(state_ref[b : b + 1, :])
        state = state + jnp.sum(total * total, axis=1, keepdims=True) / WIDTH
        new_state_ref[b : b + 1, :] = jnp.transpose(state)[:1]
        new_table_ref[rows, :] = table_ref[rows, :] - total * (RATE * lax.rsqrt(state[:, :1]))


def kernel(body, outs, scratch=(), flops=0, nbytes=4 << 20):
    return pl.pallas_call(
        body,
        out_shape=outs,
        scratch_shapes=scratch,
        compiler_params=pltpu.CompilerParams(vmem_limit_bytes=40 << 20),
        cost_estimate=pl.CostEstimate(flops=flops, bytes_accessed=nbytes, transcendentals=0),
    )


def exchange(x):
    return lax.all_to_all(x, "edge", split_axis=0, concat_axis=0, tiled=True)


def relation_sum(grad):
    part = lax.psum_scatter(grad, "rep", scatter_dimension=0, tiled=True)
    rows = part.shape[0] // OWN
    mine = jnp.sum(exchange(part.reshape(OWN, rows, WIDTH)), axis=0)
    part = exchange(jnp.broadcast_to(mine[None], (OWN, rows, WIDTH))).reshape(OWN * rows, WIDTH)
    return lax.all_gather(part, "rep", axis=0, tiled=True)


def shards(entities, ent_accum, relations, rel_accum, heads, tails, negatives, rel_ids):
    steps = heads.shape[1]
    shape = jax.ShapeDtypeStruct
    wire = shape((OWN, 128, 128), BF16)
    table, accum = entities, ent_accum.reshape(8, 128)
    rel_count = relations.shape[0]
    rel_table = jnp.pad(relations, ((0, REL - rel_count), (0, 0)))
    rel_state = jnp.pad(rel_accum, (0, REL - rel_count), constant_values=1.0).reshape(8, 128)
    send, negative, slots = kernel(
        prepare, (shape((OWN, 128), I32), shape((OWN, 128), F32), shape((steps, 256), I32))
    )(heads, tails, negatives)
    named = exchange(send.reshape(OWN, 1, 128)).reshape(OWN, 128)
    flat = jnp.stack([named[:, CAP * s : CAP * s + CAP].reshape(SLOTS) for s in range(steps)])
    negative = jnp.stack([negative[:, CAP * s : CAP * s + CAP].reshape(SLOTS) for s in range(steps)])
    rows = kernel(first_rows, wire, [pltpu.VMEM((1024, 512), BF16)], 3 << 30)(table, named)
    for s in range(steps):
        last = s == steps - 1
        rows = exchange(rows)
        grads, relation_grad = kernel(
            lambda *refs, s=s: block(s, *refs),
            (wire, shape((REL, WIDTH), F32)),
            [pltpu.VMEM((SLOTS, 512), BF16), pltpu.VMEM((256, SLOTS), BF16)],
            4 << 30,
        )(rows, slots, negative, rel_table, rel_ids)
        grads = exchange(grads)
        relation_total = relation_sum(relation_grad)
        outs = (shape(table.shape, F32), shape((8, 128), F32)) + (() if last else (wire,))
        scratch = [pltpu.VMEM((SLOTS, 512), BF16)] + ([] if last else [pltpu.VMEM((1024, 512), BF16)])
        table, accum, *rows = kernel(
            lambda *refs, s=s, last=last: update(s, last, *refs), outs, scratch, 5 << 30
        )(grads, flat, table, accum, named)
        rows = None if last else rows[0]
        rel_table, rel_state = kernel(
            relation_update, (shape((REL, WIDTH), F32), shape((8, 128), F32))
        )(relation_total, rel_table, rel_state)
    return table, accum.reshape(1, 1024), rel_table[:rel_count], rel_state.reshape(REL)[:rel_count]


def solution(mesh):
    in_specs = (
        P("rep", "edge", None),
        P("rep", "edge"),
        P(),
        P(),
        P("rep", None, "edge"),
        P("rep", None, "edge"),
        P("rep", None, "edge"),
        P("rep", None, "edge"),
    )
    out_specs = (P("rep", "edge", None), P("rep", "edge"), P(), P())
    return jax.shard_map(shards, mesh=mesh, in_specs=in_specs, out_specs=out_specs, check_vma=False)
```

```python
import jax
import jax.numpy as jnp
from jax import lax
from jax.experimental import pallas as pl
from jax.experimental.pallas import tpu as pltpu
from jax.sharding import PartitionSpec as P

F32, BF16, I32 = jnp.float32, jnp.bfloat16, jnp.int32
RATE = 0.1
OWN = 64
CAP = 40
SLOTS = OWN * CAP
WIDTH = 400
HALF = 200
BODY = 384
REL = 1024


def iota(shape, dim):
    return lax.broadcasted_iota(I32, shape, dim)


def one_hot(hit):
    return jnp.where(hit, 1.0, 0.0).astype(BF16)


def dot(a, b, dims=((1,), (0,))):
    return lax.dot_general(a, b, (dims, ((), ())), preferred_element_type=F32)


def fold_tail(x):
    x = x + pltpu.roll(x, 64, 1)
    x = x + pltpu.roll(x, 32, 1)
    return x + pltpu.roll(x, 16, 1)


def spread_tail(x16):
    rows = x16.shape[0]
    return fold_tail(jnp.concatenate([x16, jnp.zeros((rows, 112), F32)], axis=1))


def to_wide(x):
    return jnp.concatenate([x[:, :BODY], spread_tail(x[:, BODY:])], axis=1)


def to_narrow(x):
    return jnp.concatenate([x[:, :BODY], fold_tail(x[:, BODY:])[:, :16]], axis=1)


def pack(rows):
    group = iota((8, 128), 1) // 16
    tail = jnp.zeros((8, 128), F32)
    for i in range(5):
        tail = jnp.where(group == i, rows[8 * i : 8 * i + 8, BODY:], tail)
    return jnp.concatenate([rows[:, :128], rows[:, 128:256], rows[:, 256:384], tail], axis=0)


def unpack(block):
    group = iota((8, 128), 1) // 16
    tail = jnp.concatenate([jnp.where(group == i, block[120:], 0.0) for i in range(5)], axis=0)
    return jnp.concatenate([block[:40], block[40:80], block[80:120], tail], axis=1)


def unpack_all(wire_ref, rows_ref):
    def pair(e, _):
        two = [unpack(wire_ref[2 * e + k].astype(F32)) for k in range(2)]
        at = pl.multiple_of(e * 2 * CAP, 2 * CAP)
        rows_ref[pl.ds(at, 2 * CAP), :] = jnp.concatenate(two, axis=0).astype(BF16)
        return 0

    lax.fori_loop(0, OWN // 2, pair, 0)


def lane_to_column(row):
    return jnp.transpose(jnp.broadcast_to(row, (128, 128)))


def prepare(heads_ref, tails_ref, negatives_ref, send_ref, negative_ref, slots_ref):
    count = 2 * heads_ref.shape[2] + negatives_ref.shape[2]
    steps = heads_ref.shape[1]
    before = one_hot(iota((128, 128), 0) < iota((128, 128), 1))
    send = jnp.zeros((OWN, 128), F32)
    negative = jnp.zeros((OWN, 128), F32)
    for s in range(steps):
        requests = jnp.concatenate(
            [heads_ref[0, s : s + 1, :], tails_ref[0, s : s + 1, :], negatives_ref[0, s : s + 1, :]], axis=1
        )
        owner = lax.shift_right_logical(requests, 10)
        local = requests & 1023
        at_owner = jnp.where(iota((OWN, count), 0) == owner, 1.0, 0.0)
        seen = jnp.zeros((OWN, 1), F32)
        ranks = []
        for j in range(count // 128):
            part = at_owner[:, 128 * j : 128 * j + 128]
            earlier = dot(part.astype(BF16), before) + seen
            ranks.append(jnp.sum(part * earlier, axis=0, keepdims=True))
            seen = seen + jnp.sum(part, axis=1, keepdims=True)
        rank = jnp.concatenate(ranks, axis=1).astype(I32)
        at_rank = one_hot(iota((128, count), 0) == rank + CAP * s)
        high = (at_owner * lax.shift_right_logical(local, 5).astype(F32)).astype(BF16)
        low = (at_owner * (local & 31).astype(F32)).astype(BF16)
        last = ((1,), (1,))
        send = send + dot(high, at_rank, last) * 32.0 + dot(low, at_rank, last)
        chosen = jnp.where(iota((OWN, count), 1) >= 256, at_owner, 0.0).astype(BF16)
        negative = negative + dot(chosen, at_rank, last)
        slots_ref[s : s + 1, :] = (owner * CAP + rank)[:, :256]
    send_ref[...] = send.astype(I32)
    negative_ref[...] = negative


def gather_rows(named_ref, step, wide_ref, wire_ref):
    named = named_ref[...].astype(F32)
    named = jnp.transpose(jnp.concatenate([named, named], axis=0))
    named = named[CAP * step : CAP * step + CAP, :OWN].astype(I32)
    for g in range(OWN // 8):
        columns = jnp.concatenate([named[:, 8 * g + j : 8 * g + j + 1] for j in range(8)], axis=0)
        hit = one_hot(columns == iota((8 * CAP, 1024), 1))
        rows = dot(hit, wide_ref[...])
        for j in range(8):
            wire_ref[8 * g + j] = pack(rows[CAP * j : CAP * j + CAP]).astype(BF16)


def first_rows(table_ref, named_ref, wire_ref, wide_ref):
    wide_ref[...] = to_wide(table_ref[0]).astype(BF16)
    gather_rows(named_ref, 0, wide_ref, wire_ref)


def update(step, last, wire_in_ref, flat_ref, table_ref, accum_ref, named_ref, *rest):
    if last:
        new_table_ref, new_accum_ref, grads_ref = rest
    else:
        new_table_ref, new_accum_ref, wire_ref, grads_ref, wide_ref = rest
    unpack_all(wire_in_ref, grads_ref)
    for b in range(8):
        rows = slice(128 * b, 128 * b + 128)
        hit = one_hot(iota((128, SLOTS), 0) + 128 * b == flat_ref[step : step + 1, :])
        total = dot(hit, grads_ref[...])
        total = to_narrow(total)
        accum = lane_to_column(accum_ref[b : b + 1, :])
        accum = accum + jnp.sum(total * total, axis=1, keepdims=True) / WIDTH
        new_accum_ref[b : b + 1, :] = jnp.transpose(accum)[:1]
        new = table_ref[0, rows, :] - total * (RATE * lax.rsqrt(accum[:, :1]))
        new_table_ref[0, rows, :] = new
        if not last:
            wide_ref[rows, :] = to_wide(new).astype(BF16)
    if not last:
        gather_rows(named_ref, step + 1, wide_ref, wire_ref)


def complex_parts(x):
    return x[:, :HALF], x[:, HALF:]


def join(re, im):
    return jnp.concatenate([re, im], axis=1)


def split3(x):
    a = x.astype(BF16)
    x = x - a.astype(F32)
    b = x.astype(BF16)
    return a, b, (x - b.astype(F32)).astype(BF16)


def block(
    step, at_ref, wire_in_ref, slots_ref, negative_ref, relations_ref, rel_ids_ref,
    wire_ref, keep_ref, give_ref, rows_ref, weights_ref,
):
    edges, parts = 128, 4
    part = SLOTS // parts
    per = OWN // parts
    unpack_all(wire_in_ref, rows_ref)
    slots = slots_ref[step : step + 1, :]
    slots_column = jnp.concatenate(
        [lane_to_column(slots[:, 128 * k : 128 * k + 128].astype(F32))[:, :1] for k in range(2)], axis=0
    ).astype(I32)
    fetched = jnp.zeros((2 * edges, 512), F32)
    for g in range(parts):
        hit = one_hot(slots_column == iota((2 * edges, part), 1) + part * g)
        fetched = fetched + dot(hit, rows_ref[part * g : part * g + part, :])
    fetched = to_narrow(fetched)
    head, tail = fetched[:edges], fetched[edges:]
    rel_ids = rel_ids_ref[0, step : step + 1, :]
    rel_column = lane_to_column(rel_ids.astype(F32))[:, :1].astype(I32)
    rel_hit = one_hot(rel_column == iota((edges, REL), 1))
    relation = [
        sum(dot(rel_hit, piece) for piece in reversed(split3(relations_ref[k]))) for k in range(2)
    ]

    head_re, head_im = complex_parts(head)
    tail_re, tail_im = complex_parts(tail)
    rel_re, rel_im = relation
    query_tail = join(head_re * rel_re - head_im * rel_im, head_re * rel_im + head_im * rel_re)
    query_head = join(rel_re * tail_re + rel_im * tail_im, rel_re * tail_im - rel_im * tail_re)
    positive = jnp.sum(query_tail * tail, axis=1, keepdims=True)
    queries = to_wide(jnp.concatenate([query_tail, query_head], axis=0)).astype(BF16)
    pull = jnp.zeros((2 * edges, 512), F32)
    for g in range(parts):
        here = slice(part * g, part * g + part)
        scores = dot(queries, rows_ref[here, :], ((1,), (1,)))
        weights = jax.nn.sigmoid(scores) * (negative_ref[step : step + 1, here] / 1024)
        weights = weights.astype(BF16)
        weights_ref[:, here] = weights
        pull = pull + dot(weights, rows_ref[here, :])
    pull = to_narrow(pull)
    positive_weight = -jax.nn.sigmoid(-positive)
    pull_re, pull_im = complex_parts(positive_weight * tail + pull[:edges])
    push_re, push_im = complex_parts(pull[edges:])
    grad_head = join(pull_re * rel_re + pull_im * rel_im, pull_im * rel_re - pull_re * rel_im)
    grad_tail = positive_weight * query_tail + join(
        push_re * rel_re - push_im * rel_im, push_re * rel_im + push_im * rel_re
    )
    grad_relation = (
        pull_re * head_re + pull_im * head_im + push_re * tail_re + push_im * tail_im,
        pull_im * head_re - pull_re * head_im + push_re * tail_im - push_im * tail_re,
    )
    rel_spread = one_hot(iota((REL, edges), 0) == rel_ids)
    relation_grad = [sum(dot(rel_spread, piece) for piece in reversed(split3(g))) for g in grad_relation]
    keep_ref[...] = jnp.where(at_ref[3] == 0, relation_grad[0], relation_grad[1])
    give_ref[...] = jnp.where(at_ref[3] == 0, relation_grad[1], relation_grad[0])
    edge_grads = to_wide(jnp.concatenate([grad_head, grad_tail], axis=0)).astype(BF16)
    for g in range(parts):
        here = slice(part * g, part * g + part)
        grads = dot(weights_ref[:, here], queries, ((0,), (0,)))
        hit = one_hot(iota((part, 2 * edges), 0) + part * g == slots)
        grads = grads + dot(hit, edge_grads)
        for j in range(per):
            wire_ref[per * g + j] = pack(grads[CAP * j : CAP * j + CAP]).astype(BF16)


def scatter_stage(axis, count, own_ref, *refs):
    at_ref, *rest = refs
    arrived, outs = rest[: len(rest) - count], rest[len(rest) - count :]
    total = own_ref[...]
    for ref in arrived:
        total = total + ref[...]
    if count == 1:
        outs[0][...] = total
        return
    *outs, sum_ref = outs
    sum_ref[...] = total
    n = count - 1
    rows = total.shape[0] // n
    for d in range(n):
        start = pl.multiple_of(lax.rem(at_ref[axis] + d, n) * rows, 8)
        outs[d][...] = sum_ref[pl.ds(start, rows), :]


def gather_stage(axis, at_ref, *refs):
    *parts, out_ref = refs
    n, rows = len(parts), parts[0].shape[0]
    for d in range(n):
        start = pl.multiple_of(lax.rem(at_ref[axis] + n - d, n) * rows, 8)
        out_ref[pl.ds(start, rows), :] = parts[d][...]


def relation_update(at_ref, mine_ref, other_ref, table_ref, state_ref, new_table_ref, new_state_ref):
    for b in range(REL // 128):
        rows = slice(128 * b, 128 * b + 128)
        mine, other = mine_ref[rows, :], other_ref[rows, :]
        total = [jnp.where(at_ref[3] == k, mine, other) for k in range(2)]
        state = lane_to_column(state_ref[b : b + 1, :])
        square = sum(jnp.sum(t * t, axis=1, keepdims=True) for t in total)
        state = state + square / WIDTH
        new_state_ref[b : b + 1, :] = jnp.transpose(state)[:1]
        for k in range(2):
            new_table_ref[k, rows, :] = table_ref[k, rows, :] - total[k] * (RATE * lax.rsqrt(state[:, :1]))


def kernel(body, outs, scratch=(), flops=0, nbytes=4 << 20, in_specs=None):
    more = {} if in_specs is None else {"in_specs": in_specs}
    return pl.pallas_call(
        body,
        out_shape=outs,
        **more,
        scratch_shapes=scratch,
        compiler_params=pltpu.CompilerParams(vmem_limit_bytes=40 << 20),
        cost_estimate=pl.CostEstimate(flops=flops, bytes_accessed=nbytes, transcendentals=0),
    )


def exchange(x):
    return lax.all_to_all(x, "edge", split_axis=0, concat_axis=0, tiled=True)


def edge_of(y, z, core):
    return (y * 8 + z) * 2 + core


def edge_pairs(dy, dz, flip=0):
    return [
        (edge_of(y, z, core), edge_of((y + dy) % 4, (z + dz) % 8, core ^ flip))
        for y in range(4)
        for z in range(8)
        for core in range(2)
    ]


def move(x, axis, d):
    if axis == 0:
        return lax.ppermute(x, "rep", [(k, (k + d) % 4) for k in range(4)])
    return lax.ppermute(x, "edge", edge_pairs(d if axis == 1 else 0, d if axis == 2 else 0))


def relation_sum(at, keep, give):
    shape = jax.ShapeDtypeStruct
    smem, vmem = pl.BlockSpec(memory_space=pltpu.SMEM), pl.BlockSpec(memory_space=pltpu.VMEM)
    sizes = (4, 4, 8)
    arrived = [lax.ppermute(give, "edge", edge_pairs(0, 0, 1))]
    own, rows = keep, REL
    for axis, n in enumerate(sizes):
        outs = [shape((rows // n, HALF), F32)] * n + [shape((rows, HALF), F32)]
        own, *parts, _ = kernel(
            lambda *refs, axis=axis, n=n: scatter_stage(axis, n + 1, *refs), outs,
            in_specs=[vmem, smem] + [vmem] * len(arrived),
        )(own, at, *arrived)
        arrived = [move(part, axis, d + 1) for d, part in enumerate(parts)]
        rows //= n
    own = kernel(
        lambda *refs: scatter_stage(0, 1, *refs), [shape((rows, HALF), F32)],
        in_specs=[vmem, smem] + [vmem] * len(arrived),
    )(own, at, *arrived)[0]
    for axis, n in reversed(list(enumerate(sizes))):
        arrived = [move(own, axis, d) for d in range(1, n)]
        rows *= n
        own = kernel(
            lambda *refs, axis=axis: gather_stage(axis, *refs), shape((rows, HALF), F32),
            in_specs=[smem] + [vmem] * n,
        )(at, own, *arrived)
    return own, lax.ppermute(own, "edge", edge_pairs(0, 0, 1))


def shards(entities, ent_accum, relations, rel_accum, heads, tails, negatives, rel_ids):
    steps = heads.shape[1]
    shape = jax.ShapeDtypeStruct
    wire = shape((OWN, 128, 128), BF16)
    table, accum = entities, ent_accum.reshape(8, 128)
    rel_count = relations.shape[0]
    rel_table = jnp.pad(relations, ((0, REL - rel_count), (0, 0)))
    rel_table = jnp.stack(complex_parts(rel_table))
    edge = lax.axis_index("edge")
    at = jnp.stack([lax.axis_index("rep"), edge // 16, edge // 2 % 8, edge % 2]).astype(I32)
    smem, vmem = pl.BlockSpec(memory_space=pltpu.SMEM), pl.BlockSpec(memory_space=pltpu.VMEM)
    rel_state = jnp.pad(rel_accum, (0, REL - rel_count), constant_values=1.0).reshape(8, 128)
    send, negative, slots = kernel(
        prepare, (shape((OWN, 128), I32), shape((OWN, 128), F32), shape((steps, 256), I32))
    )(heads, tails, negatives)
    named = exchange(send.reshape(OWN, 1, 128)).reshape(OWN, 128)
    flat = jnp.stack([named[:, CAP * s : CAP * s + CAP].reshape(SLOTS) for s in range(steps)])
    negative = jnp.stack([negative[:, CAP * s : CAP * s + CAP].reshape(SLOTS) for s in range(steps)])
    rows = kernel(first_rows, wire, [pltpu.VMEM((1024, 512), BF16)], 3 << 30)(table, named)
    for s in range(steps):
        last = s == steps - 1
        rows = exchange(rows)
        grads, keep, give = kernel(
            lambda *refs, s=s: block(s, *refs),
            (wire, shape((REL, HALF), F32), shape((REL, HALF), F32)),
            [pltpu.VMEM((SLOTS, 512), BF16), pltpu.VMEM((256, SLOTS), BF16)],
            4 << 30,
            in_specs=[smem] + [vmem] * 5,
        )(at, rows, slots, negative, rel_table, rel_ids)
        grads = exchange(grads)
        mine, other = relation_sum(at, keep, give)
        outs = (shape(table.shape, F32), shape((8, 128), F32)) + (() if last else (wire,))
        scratch = [pltpu.VMEM((SLOTS, 512), BF16)] + ([] if last else [pltpu.VMEM((1024, 512), BF16)])
        table, accum, *rows = kernel(
            lambda *refs, s=s, last=last: update(s, last, *refs), outs, scratch, 5 << 30
        )(grads, flat, table, accum, named)
        rows = None if last else rows[0]
        rel_table, rel_state = kernel(
            relation_update, (shape((2, REL, HALF), F32), shape((8, 128), F32)),
            in_specs=[smem] + [vmem] * 4,
        )(at, mine, other, rel_table, rel_state)
    rel_table = jnp.concatenate([rel_table[0], rel_table[1]], axis=1)[:rel_count]
    return table, accum.reshape(1, 1024), rel_table, rel_state.reshape(REL)[:rel_count]


def solution(mesh):
    in_specs = (
        P("rep", "edge", None),
        P("rep", "edge"),
        P(),
        P(),
        P("rep", None, "edge"),
        P("rep", None, "edge"),
        P("rep", None, "edge"),
        P("rep", None, "edge"),
    )
    out_specs = (P("rep", "edge", None), P("rep", "edge"), P(), P())
    return jax.shard_map(shards, mesh=mesh, in_specs=in_specs, out_specs=out_specs, check_vma=False)
```

```python
import jax
import jax.numpy as jnp
from jax import lax
from jax.experimental import pallas as pl
from jax.experimental.pallas import tpu as pltpu
from jax.sharding import PartitionSpec as P

F32, BF16, I32 = jnp.float32, jnp.bfloat16, jnp.int32
RATE = 0.1
OWN = 64
CAP = 40
SLOTS = OWN * CAP
WIDTH = 400
HALF = 200
BODY = 384
REL = 1024
DENSE = REL // 64 * 200
WIRE_PARTS = 4


def iota(shape, dim):
    return lax.broadcasted_iota(I32, shape, dim)


def one_hot(hit):
    return jnp.where(hit, 1.0, 0.0).astype(BF16)


def dot(a, b, dims=((1,), (0,))):
    return lax.dot_general(a, b, (dims, ((), ())), preferred_element_type=F32)


def fold_tail(x):
    x = x + pltpu.roll(x, 64, 1)
    x = x + pltpu.roll(x, 32, 1)
    return x + pltpu.roll(x, 16, 1)


def spread_tail(x16):
    rows = x16.shape[0]
    return fold_tail(jnp.concatenate([x16, jnp.zeros((rows, 112), F32)], axis=1))


def to_wide(x):
    return jnp.concatenate([x[:, :BODY], spread_tail(x[:, BODY:])], axis=1)


def to_narrow(x):
    return jnp.concatenate([x[:, :BODY], fold_tail(x[:, BODY:])[:, :16]], axis=1)


def pack(rows):
    group = iota((8, 128), 1) // 16
    tail = jnp.zeros((8, 128), F32)
    for i in range(5):
        tail = jnp.where(group == i, rows[8 * i : 8 * i + 8, BODY:], tail)
    return jnp.concatenate([rows[:, :128], rows[:, 128:256], rows[:, 256:384], tail], axis=0)


def unpack(block):
    group = iota((8, 128), 1) // 16
    tail = jnp.concatenate([jnp.where(group == i, block[120:], 0.0) for i in range(5)], axis=0)
    return jnp.concatenate([block[:40], block[40:80], block[80:120], tail], axis=1)


def pack_relations(rows):
    group = iota((8, 128), 1) // 16
    tail = jnp.zeros((8, 128), F32)
    for i in range(8):
        tail = jnp.where(group == i, rows[8 * i : 8 * i + 8, BODY:], tail)
    return jnp.concatenate([rows[:, :128], rows[:, 128:256], rows[:, 256:384], tail], axis=0)


def unpack_relations(dense):
    group = iota((8, 128), 1) // 16
    tail = jnp.concatenate([jnp.where(group == i, dense[192:], 0.0) for i in range(8)], axis=0)
    return to_narrow(jnp.concatenate([dense[:64], dense[64:128], dense[128:192], tail], axis=1))


def wire_copies(wire_ref, held_ref, sems):
    per = OWN // WIRE_PARTS
    return [
        pltpu.make_async_copy(wire_ref.at[pl.ds(per * g, per)], held_ref.at[pl.ds(per * g, per)], sems.at[g])
        for g in range(WIRE_PARTS)
    ]


def unpack_all(copies, held_ref, rows_ref):
    per = OWN // WIRE_PARTS // 2
    for g, copy in enumerate(copies):
        copy.wait()

        def pair(e, _):
            two = [unpack(held_ref[2 * e + k].astype(F32)) for k in range(2)]
            at = pl.multiple_of(e * 2 * CAP, 2 * CAP)
            rows_ref[pl.ds(at, 2 * CAP), :] = jnp.concatenate(two, axis=0).astype(BF16)
            return 0

        lax.fori_loop(per * g, per * g + per, pair, 0)


def lane_to_column(row):
    return jnp.transpose(jnp.broadcast_to(row, (128, 128)))


def prepare(heads_ref, tails_ref, negatives_ref, send_ref, negative_ref, slots_ref):
    count = 2 * heads_ref.shape[2] + negatives_ref.shape[2]
    steps = heads_ref.shape[1]
    before = one_hot(iota((128, 128), 0) < iota((128, 128), 1))
    send = jnp.zeros((OWN, 128), F32)
    negative = jnp.zeros((OWN, 128), F32)
    for s in range(steps):
        requests = jnp.concatenate(
            [heads_ref[0, s : s + 1, :], tails_ref[0, s : s + 1, :], negatives_ref[0, s : s + 1, :]], axis=1
        )
        owner = lax.shift_right_logical(requests, 10)
        local = requests & 1023
        at_owner = jnp.where(iota((OWN, count), 0) == owner, 1.0, 0.0)
        seen = jnp.zeros((OWN, 1), F32)
        ranks = []
        for j in range(count // 128):
            part = at_owner[:, 128 * j : 128 * j + 128]
            earlier = dot(part.astype(BF16), before) + seen
            ranks.append(jnp.sum(part * earlier, axis=0, keepdims=True))
            seen = seen + jnp.sum(part, axis=1, keepdims=True)
        rank = jnp.concatenate(ranks, axis=1).astype(I32)
        at_rank = one_hot(iota((128, count), 0) == rank + CAP * s)
        high = (at_owner * lax.shift_right_logical(local, 5).astype(F32)).astype(BF16)
        low = (at_owner * (local & 31).astype(F32)).astype(BF16)
        last = ((1,), (1,))
        send = send + dot(high, at_rank, last) * 32.0 + dot(low, at_rank, last)
        chosen = jnp.where(iota((OWN, count), 1) >= 256, at_owner, 0.0).astype(BF16)
        negative = negative + dot(chosen, at_rank, last)
        slots_ref[s : s + 1, :] = (owner * CAP + rank)[:, :256]
    send_ref[...] = send.astype(I32)
    negative_ref[...] = negative


def gather_rows(named_ref, step, wide_ref, wire_ref, held_ref, sems):
    named = named_ref[...].astype(F32)
    named = jnp.transpose(jnp.concatenate([named, named], axis=0))
    named = named[CAP * step : CAP * step + CAP, :OWN].astype(I32)
    per = OWN // 8
    copies = []
    for g in range(8):
        columns = jnp.concatenate([named[:, per * g + j : per * g + j + 1] for j in range(per)], axis=0)
        hit = one_hot(columns == iota((per * CAP, 1024), 1))
        rows = dot(hit, wide_ref[...])
        for j in range(per):
            held_ref[per * g + j] = pack(rows[CAP * j : CAP * j + CAP]).astype(BF16)
        here = pl.ds(per * g, per)
        copies.append(pltpu.make_async_copy(held_ref.at[here], wire_ref.at[here], sems.at[g]))
        copies[-1].start()
    for copy in copies:
        copy.wait()


def widen(table_ref, wide_ref):
    wide_ref[...] = to_wide(table_ref[0]).astype(BF16)


def first_rows(wide_ref, named_ref, wire_ref, held_ref, sems):
    gather_rows(named_ref, 0, wide_ref, wire_ref, held_ref, sems)


def update(step, last, wire_in_ref, flat_ref, table_ref, accum_ref, named_ref, _, *rest):
    if last:
        new_table_ref, new_accum_ref, in_sems, table_sem, out_sems, held_ref, rows_ref, grads_ref = rest
    else:
        new_table_ref, new_accum_ref, wire_ref, in_sems, table_sem, out_sems, held_ref, rows_ref, grads_ref, *rest = rest
        wide_ref, sent_ref, sent_sems = rest
    copies = wire_copies(wire_in_ref, held_ref, in_sems)
    for copy in copies:
        copy.start()
    table_copy = pltpu.make_async_copy(table_ref.at[0], rows_ref, table_sem)
    table_copy.start()
    unpack_all(copies, held_ref, grads_ref)
    table_copy.wait()
    outs = []
    for b in range(8):
        rows = slice(128 * b, 128 * b + 128)
        hit = one_hot(iota((128, SLOTS), 0) + 128 * b == flat_ref[step : step + 1, :])
        total = dot(hit, grads_ref[...])
        total = to_narrow(total)
        accum = lane_to_column(accum_ref[b : b + 1, :])
        accum = accum + jnp.sum(total * total, axis=1, keepdims=True) / WIDTH
        new_accum_ref[b : b + 1, :] = jnp.transpose(accum)[:1]
        new = rows_ref[rows, :] - total * (RATE * lax.rsqrt(accum[:, :1]))
        rows_ref[rows, :] = new
        here = pl.ds(128 * b, 128)
        outs.append(pltpu.make_async_copy(rows_ref.at[here], new_table_ref.at[0, here], out_sems.at[b]))
        outs[-1].start()
        if not last:
            wide_ref[rows, :] = to_wide(new).astype(BF16)
    if not last:
        gather_rows(named_ref, step + 1, wide_ref, wire_ref, sent_ref, sent_sems)
    for copy in outs:
        copy.wait()


def complex_parts(x):
    return x[:, :HALF], x[:, HALF:]


def join(re, im):
    return jnp.concatenate([re, im], axis=1)


def split3(x):
    a = x.astype(BF16)
    x = x - a.astype(F32)
    b = x.astype(BF16)
    return a, b, (x - b.astype(F32)).astype(BF16)


def relation_rows(step, table_ref, rel_ids_ref, out_ref):
    rel_ids = rel_ids_ref[0, step : step + 1, :]
    column = lane_to_column(rel_ids.astype(F32))[:, :1].astype(I32)
    hit = one_hot(column == iota((rel_ids.shape[1], REL), 1))
    out_ref[...] = sum(dot(hit, piece) for piece in reversed(split3(table_ref[...])))


def block(
    step, at_ref, wire_in_ref, slots_ref, negative_ref, relation_ref, rel_ids_ref,
    wire_ref, keep_ref, give_ref, rows_ref, weights_ref, held_ref, in_sems, sent_ref, out_sems,
):
    edges, parts = 128, 4
    part = SLOTS // parts
    per = OWN // parts
    copies = wire_copies(wire_in_ref, held_ref, in_sems)
    for copy in copies:
        copy.start()
    unpack_all(copies, held_ref, rows_ref)
    slots = slots_ref[step : step + 1, :]
    slots_column = jnp.concatenate(
        [lane_to_column(slots[:, 128 * k : 128 * k + 128].astype(F32))[:, :1] for k in range(2)], axis=0
    ).astype(I32)
    fetched = jnp.zeros((2 * edges, 512), F32)
    for g in range(parts):
        hit = one_hot(slots_column == iota((2 * edges, part), 1) + part * g)
        fetched = fetched + dot(hit, rows_ref[part * g : part * g + part, :])
    fetched = to_narrow(fetched)
    head, tail = fetched[:edges], fetched[edges:]
    head_re, head_im = complex_parts(head)
    tail_re, tail_im = complex_parts(tail)
    rel_re, rel_im = complex_parts(relation_ref[...])
    query_tail = join(head_re * rel_re - head_im * rel_im, head_re * rel_im + head_im * rel_re)
    query_head = join(rel_re * tail_re + rel_im * tail_im, rel_re * tail_im - rel_im * tail_re)
    positive = jnp.sum(query_tail * tail, axis=1, keepdims=True)
    queries = to_wide(jnp.concatenate([query_tail, query_head], axis=0)).astype(BF16)
    pull = jnp.zeros((2 * edges, 512), F32)
    for g in range(parts):
        here = slice(part * g, part * g + part)
        scores = dot(queries, rows_ref[here, :], ((1,), (1,)))
        weights = jax.nn.sigmoid(scores) * (negative_ref[step : step + 1, here] / 1024)
        weights = weights.astype(BF16)
        weights_ref[:, here] = weights
        pull = pull + dot(weights, rows_ref[here, :])
    pull = to_narrow(pull)
    positive_weight = -jax.nn.sigmoid(-positive)
    pull_re, pull_im = complex_parts(positive_weight * tail + pull[:edges])
    push_re, push_im = complex_parts(pull[edges:])
    grad_head = join(pull_re * rel_re + pull_im * rel_im, pull_im * rel_re - pull_re * rel_im)
    grad_tail = positive_weight * query_tail + join(
        push_re * rel_re - push_im * rel_im, push_re * rel_im + push_im * rel_re
    )
    edge_grads = to_wide(jnp.concatenate([grad_head, grad_tail], axis=0)).astype(BF16)
    outs = []
    for g in range(parts):
        here = slice(part * g, part * g + part)
        grads = dot(weights_ref[:, here], queries, ((0,), (0,)))
        hit = one_hot(iota((part, 2 * edges), 0) + part * g == slots)
        grads = grads + dot(hit, edge_grads)
        for j in range(per):
            sent_ref[per * g + j] = pack(grads[CAP * j : CAP * j + CAP]).astype(BF16)
        blocks = pl.ds(per * g, per)
        outs.append(pltpu.make_async_copy(sent_ref.at[blocks], wire_ref.at[blocks], out_sems.at[g]))
        outs[-1].start()
    grad_relation = to_wide(
        join(
            pull_re * head_re + pull_im * head_im + push_re * tail_re + push_im * tail_im,
            pull_im * head_re - pull_re * head_im + push_re * tail_im - push_im * tail_re,
        )
    )
    high = grad_relation.astype(BF16)
    low = (grad_relation - high.astype(F32)).astype(BF16)
    rel_ids = rel_ids_ref[0, step : step + 1, :]
    half = REL // 128
    for i in range(half):
        dense = []
        for k in range(2):
            hit = one_hot(iota((64, edges), 0) + 64 * (half * k + i) == rel_ids)
            dense.append(pack_relations(dot(hit, high) + dot(hit, low)))
        here = slice(200 * i, 200 * i + 200)
        keep_ref[here, :] = jnp.where(at_ref[3] == 0, dense[0], dense[1])
        give_ref[here, :] = jnp.where(at_ref[3] == 0, dense[1], dense[0])
    for copy in outs:
        copy.wait()


def scatter_stage(axis, at_ref, own_ref, *refs):
    n = (4, 4)[axis]
    arrived, outs, sum_ref = refs[: -n - 1], refs[-n - 1 : -1], refs[-1]
    total = own_ref[...].astype(F32)
    for ref in arrived:
        total = total + ref[...].astype(F32)
    sum_ref[: total.shape[0], :] = total
    rows = outs[0].shape[0]
    if total.shape[0] < n * rows:
        sum_ref[total.shape[0] :, :] = jnp.zeros((n * rows - total.shape[0], 128), F32)
    for d in range(n):
        start = pl.multiple_of(lax.rem(at_ref[axis] + d, n) * rows, 8)
        outs[d][...] = sum_ref[pl.ds(start, rows), :].astype(outs[d].dtype)


def sum_stage(*refs):
    *parts, out_ref = refs
    total = parts[0][...]
    for ref in parts[1:]:
        total = total + ref[...]
    out_ref[...] = total


def gather_y(at_ref, *refs):
    *parts, out_ref, all_ref = refs
    rows = parts[0].shape[0]
    for d in range(4):
        start = pl.multiple_of(lax.rem(at_ref[1] + 4 - d, 4) * rows, 8)
        all_ref[pl.ds(start, rows), :] = parts[d][...]
    out_ref[...] = all_ref[: out_ref.shape[0], :].astype(BF16)


def gather_x(at_ref, _, *refs):
    *parts, out_ref = refs
    rows = parts[0].shape[0]
    for d in range(4):
        start = pl.multiple_of(lax.rem(at_ref[0] + 4 - d, 4) * rows, 16)
        out_ref[pl.ds(start, rows), :] = parts[d][...]


def relation_update(at_ref, mine_ref, other_ref, table_ref, state_ref, new_table_ref, new_state_ref):
    count = REL // 128
    for b in range(count):
        rows = slice(128 * b, 128 * b + 128)
        here = slice(400 * (b % (count // 2)), 400 * (b % (count // 2)) + 400)
        mine, other = mine_ref[here, :].astype(F32), other_ref[here, :].astype(F32)
        dense = jnp.where(at_ref[3] == b // (count // 2), mine, other)
        total = jnp.concatenate([unpack_relations(dense[:200]), unpack_relations(dense[200:])], axis=0)
        state = lane_to_column(state_ref[b : b + 1, :])
        state = state + jnp.sum(total * total, axis=1, keepdims=True) / WIDTH
        new_state_ref[b : b + 1, :] = jnp.transpose(state)[:1]
        new_table_ref[rows, :] = table_ref[rows, :] - total * (RATE * lax.rsqrt(state[:, :1]))


SPACES = {
    "s": pl.BlockSpec(memory_space=pltpu.SMEM),
    "v": pl.BlockSpec(memory_space=pltpu.VMEM),
    "h": pl.BlockSpec(memory_space=pltpu.HBM),
    "a": pl.BlockSpec(memory_space=pl.ANY),
}


def kernel(body, ins, outs, places, scratch=(), flops=0):
    call = pl.pallas_call(
        body,
        out_shape=[pltpu.HBM(o.shape, o.dtype) if k == "h" else o for o, k in zip(outs, places)],
        in_specs=[SPACES[k] for k in ins],
        out_specs=[SPACES[k] for k in places],
        scratch_shapes=scratch,
        compiler_params=pltpu.CompilerParams(vmem_limit_bytes=40 << 20),
        cost_estimate=pl.CostEstimate(flops=flops, bytes_accessed=1 << 20, transcendentals=0),
    )
    return lambda *args: call(
        *[pltpu.with_memory_space_constraint(x, pltpu.HBM) if k == "h" else x for x, k in zip(args, ins)]
    )


def copies(n):
    return pltpu.SemaphoreType.DMA((n,))


def exchange(x):
    return lax.all_to_all(x, "edge", split_axis=0, concat_axis=0, tiled=True)


def edge_of(y, z, core):
    return (y * 8 + z) * 2 + core


def edge_pairs(dy, dz, flip=0):
    return [
        (edge_of(y, z, core), edge_of((y + dy) % 4, (z + dz) % 8, core ^ flip))
        for y in range(4)
        for z in range(8)
        for core in range(2)
    ]


def move(x, axis, d):
    if axis == 0:
        return lax.ppermute(x, "rep", [(k, (k + d) % 4) for k in range(4)])
    return lax.ppermute(x, "edge", edge_pairs(d if axis == 1 else 0, d if axis == 2 else 0))


def doubled(x, bit):
    pairs = [
        (edge_of(y, z, core), edge_of(y, z ^ bit, core)) for y in range(4) for z in range(8) for core in range(2)
    ]
    return kernel(sum_stage, "vv", [jax.ShapeDtypeStruct(x.shape, F32)], "v")(x, lax.ppermute(x, "edge", pairs))[0]


def relation_scatter(at, keep, give):
    shape = jax.ShapeDtypeStruct
    arrived = [lax.ppermute(give, "edge", edge_pairs(0, 0, 1))]
    own = keep
    for axis, (rows, sent) in enumerate(((DENSE // 8, BF16), (104, F32))):
        own, *parts = kernel(
            lambda *refs, axis=axis: scatter_stage(axis, *refs),
            "sv" + "v" * len(arrived),
            [shape((rows, 128), F32)] + [shape((rows, 128), sent)] * 3,
            "vvvv",
            [pltpu.VMEM((4 * rows, 128), F32)],
        )(at, own, *arrived)
        arrived = [move(part, axis, d + 1) for d, part in enumerate(parts)]
    own = kernel(sum_stage, "vvvv", [shape(own.shape, F32)], "v")(own, *arrived)[0]
    for bit in (1, 2, 4):
        own = doubled(own, bit)
    return own


def relation_gather_y(at, own):
    return kernel(
        gather_y, "svvvv", [jax.ShapeDtypeStruct((DENSE // 8, 128), BF16)], "v", [pltpu.VMEM((416, 128), F32)]
    )(at, own, *[move(own, 1, d) for d in (1, 2, 3)])[0]


def relation_gather_x(at, own, after):
    own = kernel(gather_x, "savvvv", [jax.ShapeDtypeStruct((DENSE // 2, 128), BF16)], "v")(
        at, after, own, *[move(own, 0, d) for d in (1, 2, 3)]
    )[0]
    return own, lax.ppermute(own, "edge", edge_pairs(0, 0, 1))


def shards(entities, ent_accum, relations, rel_accum, heads, tails, negatives, rel_ids):
    steps = heads.shape[1]
    shape = jax.ShapeDtypeStruct
    wire = shape((OWN, 128, 128), BF16)
    held = pltpu.VMEM((OWN, 128, 128), BF16)
    table, accum = entities, ent_accum.reshape(8, 128)
    rel_count = relations.shape[0]
    rel_table = jnp.pad(relations, ((0, REL - rel_count), (0, 0)))
    rel_state = jnp.pad(rel_accum, (0, REL - rel_count), constant_values=1.0).reshape(8, 128)
    edge = lax.axis_index("edge")
    at = jnp.stack([lax.axis_index("rep"), edge // 16, edge // 2 % 8, edge % 2]).astype(I32)
    send, negative, slots = kernel(
        prepare, "vvv", [shape((OWN, 128), I32), shape((OWN, 128), F32), shape((steps, 256), I32)], "vvv"
    )(heads, tails, negatives)
    named = exchange(send.reshape(OWN, 1, 128)).reshape(OWN, 128)
    wide = kernel(widen, "v", [shape((1024, 512), BF16)], "v")(table)[0]
    flat = jnp.stack([named[:, CAP * s : CAP * s + CAP].reshape(SLOTS) for s in range(steps)])
    negative = jnp.stack([negative[:, CAP * s : CAP * s + CAP].reshape(SLOTS) for s in range(steps)])
    rows = kernel(first_rows, "vv", [wire], "h", [held, copies(8)], 3 << 30)(wide, named)[0]
    for s in range(steps):
        last = s == steps - 1
        relation = kernel(
            lambda *refs, s=s: relation_rows(s, *refs), "vv", [shape((128, WIDTH), F32)], "v"
        )(rel_table, rel_ids)[0]
        rows = exchange(rows)
        dense = shape((DENSE // 2, 128), F32)
        grads, keep, give = kernel(
            lambda *refs, s=s: block(s, *refs),
            "shvvvv",
            [wire, dense, dense],
            "hvv",
            [pltpu.VMEM((SLOTS, 512), BF16), pltpu.VMEM((256, SLOTS), BF16), held, copies(WIRE_PARTS), held, copies(4)],
            4 << 30,
        )(at, rows, slots, negative, relation, rel_ids)
        grads = exchange(grads)
        own = relation_scatter(at, keep, give)
        if last:
            own = relation_gather_y(at, own)
        scratch = [copies(WIRE_PARTS), pltpu.SemaphoreType.DMA, copies(8), held]
        scratch += [pltpu.VMEM((1024, WIDTH), F32), pltpu.VMEM((SLOTS, 512), BF16)]
        if not last:
            scratch += [pltpu.VMEM((1024, 512), BF16), held, copies(8)]
        table, accum, *rows = kernel(
            lambda *refs, s=s, last=last: update(s, last, *refs),
            "hvhvva",
            [shape(table.shape, F32), shape((8, 128), F32)] + ([] if last else [wire]),
            "hv" if last else "hvh",
            scratch,
            5 << 30,
        )(grads, flat, table, accum, named, own)
        rows = None if last else rows[0]
        if not last:
            own = relation_gather_y(at, own)
        mine, other = relation_gather_x(at, own, accum)
        rel_table, rel_state = kernel(
            relation_update, "svvvv", [shape((REL, WIDTH), F32), shape((8, 128), F32)], "vv"
        )(at, mine, other, rel_table, rel_state)
    return table, accum.reshape(1, 1024), rel_table[:rel_count], rel_state.reshape(REL)[:rel_count]


def solution(mesh):
    in_specs = (
        P("rep", "edge", None),
        P("rep", "edge"),
        P(),
        P(),
        P("rep", None, "edge"),
        P("rep", None, "edge"),
        P("rep", None, "edge"),
        P("rep", None, "edge"),
    )
    out_specs = (P("rep", "edge", None), P("rep", "edge"), P(), P())
    return jax.shard_map(shards, mesh=mesh, in_specs=in_specs, out_specs=out_specs, check_vma=False)
```

```python
import jax
import jax.numpy as jnp
from jax import lax
from jax.experimental import pallas as pl
from jax.experimental.pallas import tpu as pltpu
from jax.sharding import PartitionSpec as P

F32, BF16, I32 = jnp.float32, jnp.bfloat16, jnp.int32
RATE = 0.1
OWN = 64
CAP = 40
SLOTS = OWN * CAP
WIDTH = 400
HALF = 200
BODY = 384
REL = 1024
DENSE = REL // 64 * 200
WIRE_PARTS = 4
Y_ROWS = 112


def iota(shape, dim):
    return lax.broadcasted_iota(I32, shape, dim)


def one_hot(hit):
    return jnp.where(hit, 1.0, 0.0).astype(BF16)


def dot(a, b, dims=((1,), (0,))):
    return lax.dot_general(a, b, (dims, ((), ())), preferred_element_type=F32)


def fold_tail(x):
    x = x + pltpu.roll(x, 64, 1)
    x = x + pltpu.roll(x, 32, 1)
    return x + pltpu.roll(x, 16, 1)


def spread_tail(x16):
    rows = x16.shape[0]
    return fold_tail(jnp.concatenate([x16, jnp.zeros((rows, 112), F32)], axis=1))


def to_wide(x):
    return jnp.concatenate([x[:, :BODY], spread_tail(x[:, BODY:])], axis=1)


def to_narrow(x):
    return jnp.concatenate([x[:, :BODY], fold_tail(x[:, BODY:])[:, :16]], axis=1)


def pack(rows):
    group = iota((8, 128), 1) // 16
    tail = jnp.zeros((8, 128), F32)
    for i in range(5):
        tail = jnp.where(group == i, rows[8 * i : 8 * i + 8, BODY:], tail)
    return jnp.concatenate([rows[:, :128], rows[:, 128:256], rows[:, 256:384], tail], axis=0)


def unpack(block):
    group = iota((8, 128), 1) // 16
    tail = jnp.concatenate([jnp.where(group == i, block[120:], 0.0) for i in range(5)], axis=0)
    return jnp.concatenate([block[:40], block[40:80], block[80:120], tail], axis=1)


def pack_relations(rows):
    group = iota((8, 128), 1) // 16
    tail = jnp.zeros((8, 128), F32)
    for i in range(8):
        tail = jnp.where(group == i, rows[8 * i : 8 * i + 8, BODY:], tail)
    return jnp.concatenate([rows[:, :128], rows[:, 128:256], rows[:, 256:384], tail], axis=0)


def unpack_relations(dense):
    group = iota((8, 128), 1) // 16
    tail = jnp.concatenate([jnp.where(group == i, dense[192:], 0.0) for i in range(8)], axis=0)
    return to_narrow(jnp.concatenate([dense[:64], dense[64:128], dense[128:192], tail], axis=1))


def wire_copies(wire_ref, held_ref, sems):
    per = OWN // WIRE_PARTS
    return [
        pltpu.make_async_copy(wire_ref.at[pl.ds(per * g, per)], held_ref.at[pl.ds(per * g, per)], sems.at[g])
        for g in range(WIRE_PARTS)
    ]


def unpack_all(copies, held_ref, rows_ref):
    per = OWN // WIRE_PARTS // 2
    for g, copy in enumerate(copies):
        copy.wait()

        def pair(e, _):
            two = [unpack(held_ref[2 * e + k].astype(F32)) for k in range(2)]
            at = pl.multiple_of(e * 2 * CAP, 2 * CAP)
            rows_ref[pl.ds(at, 2 * CAP), :] = jnp.concatenate(two, axis=0).astype(BF16)
            return 0

        lax.fori_loop(per * g, per * g + per, pair, 0)


def lane_to_column(row):
    return jnp.transpose(jnp.broadcast_to(row, (128, 128)))


def prepare(heads_in, tails_in, negatives_in, send_ref, negative_ref, slots_ref, heads_ref, tails_ref, negatives_ref, held_ref, sems):
    count = 2 * heads_ref.shape[2] + negatives_ref.shape[2]
    steps = heads_ref.shape[1]
    fetches = [
        pltpu.make_async_copy(source, held, sems.at[k])
        for k, (source, held) in enumerate(
            ((heads_in, heads_ref), (tails_in, tails_ref), (negatives_in, negatives_ref))
        )
    ]
    for copy in fetches:
        copy.start()
    for copy in fetches:
        copy.wait()
    before = one_hot(iota((128, 128), 0) < iota((128, 128), 1))
    send = jnp.zeros((OWN, 128), F32)
    negative = jnp.zeros((OWN, 128), F32)
    for s in range(steps):
        requests = jnp.concatenate(
            [heads_ref[0, s : s + 1, :], tails_ref[0, s : s + 1, :], negatives_ref[0, s : s + 1, :]], axis=1
        )
        owner = lax.shift_right_logical(requests, 10)
        local = requests & 1023
        at_owner = jnp.where(iota((OWN, count), 0) == owner, 1.0, 0.0)
        seen = jnp.zeros((OWN, 1), F32)
        ranks = []
        for j in range(count // 128):
            part = at_owner[:, 128 * j : 128 * j + 128]
            earlier = dot(part.astype(BF16), before) + seen
            ranks.append(jnp.sum(part * earlier, axis=0, keepdims=True))
            seen = seen + jnp.sum(part, axis=1, keepdims=True)
        rank = jnp.concatenate(ranks, axis=1).astype(I32)
        at_rank = one_hot(iota((128, count), 0) == rank + CAP * s)
        high = (at_owner * lax.shift_right_logical(local, 5).astype(F32)).astype(BF16)
        low = (at_owner * (local & 31).astype(F32)).astype(BF16)
        last = ((1,), (1,))
        send = send + dot(high, at_rank, last) * 32.0 + dot(low, at_rank, last)
        chosen = jnp.where(iota((OWN, count), 1) >= 256, at_owner, 0.0).astype(BF16)
        negative = negative + dot(chosen, at_rank, last)
        slots_ref[s : s + 1, :] = (owner * CAP + rank)[:, :256]
    held_ref[...] = send.astype(I32)
    sending = pltpu.make_async_copy(held_ref, send_ref, sems.at[3])
    sending.start()
    negative_ref[...] = negative
    sending.wait()


def gather_rows(named_ref, step, wide_ref, wire_ref, held_ref, sems):
    named = named_ref[...].astype(F32)
    named = jnp.transpose(jnp.concatenate([named, named], axis=0))
    named = named[CAP * step : CAP * step + CAP, :OWN].astype(I32)
    per = OWN // 8
    copies = []
    for g in range(8):
        columns = jnp.concatenate([named[:, per * g + j : per * g + j + 1] for j in range(per)], axis=0)
        hit = one_hot(columns == iota((per * CAP, 1024), 1))
        rows = dot(hit, wide_ref[...])
        for j in range(per):
            held_ref[per * g + j] = pack(rows[CAP * j : CAP * j + CAP]).astype(BF16)
        here = pl.ds(per * g, per)
        copies.append(pltpu.make_async_copy(held_ref.at[here], wire_ref.at[here], sems.at[g]))
        copies[-1].start()
    for copy in copies:
        copy.wait()


def widen(table_ref, wide_ref):
    wide_ref[...] = to_wide(table_ref[0]).astype(BF16)


def first_rows(wide_ref, named_ref, wire_ref, held_ref, sems):
    gather_rows(named_ref, 0, wide_ref, wire_ref, held_ref, sems)


def update(step, last, wire_in_ref, flat_ref, table_ref, accum_ref, named_ref, _, *rest):
    if last:
        new_table_ref, new_accum_ref, in_sems, table_sem, out_sems, held_ref, rows_ref, grads_ref = rest
    else:
        new_table_ref, new_accum_ref, wire_ref, in_sems, table_sem, out_sems, held_ref, rows_ref, grads_ref, *rest = rest
        wide_ref, sent_ref, sent_sems = rest
    copies = wire_copies(wire_in_ref, held_ref, in_sems)
    for copy in copies:
        copy.start()
    table_copy = pltpu.make_async_copy(table_ref.at[0], rows_ref, table_sem)
    table_copy.start()
    unpack_all(copies, held_ref, grads_ref)
    table_copy.wait()
    outs = []
    for b in range(8):
        rows = slice(128 * b, 128 * b + 128)
        hit = one_hot(iota((128, SLOTS), 0) + 128 * b == flat_ref[step : step + 1, :])
        total = dot(hit, grads_ref[...])
        total = to_narrow(total)
        accum = lane_to_column(accum_ref[b : b + 1, :])
        accum = accum + jnp.sum(total * total, axis=1, keepdims=True) / WIDTH
        new_accum_ref[b : b + 1, :] = jnp.transpose(accum)[:1]
        new = rows_ref[rows, :] - total * (RATE * lax.rsqrt(accum[:, :1]))
        rows_ref[rows, :] = new
        here = pl.ds(128 * b, 128)
        outs.append(pltpu.make_async_copy(rows_ref.at[here], new_table_ref.at[0, here], out_sems.at[b]))
        outs[-1].start()
        if not last:
            wide_ref[rows, :] = to_wide(new).astype(BF16)
    if not last:
        gather_rows(named_ref, step + 1, wide_ref, wire_ref, sent_ref, sent_sems)
    for copy in outs:
        copy.wait()


def complex_parts(x):
    return x[:, :HALF], x[:, HALF:]


def join(re, im):
    return jnp.concatenate([re, im], axis=1)


def split3(x):
    a = x.astype(BF16)
    x = x - a.astype(F32)
    b = x.astype(BF16)
    return a, b, (x - b.astype(F32)).astype(BF16)


def relation_rows(step, table_ref, rel_ids_ref, out_ref):
    rel_ids = rel_ids_ref[0, step : step + 1, :]
    column = lane_to_column(rel_ids.astype(F32))[:, :1].astype(I32)
    hit = one_hot(column == iota((rel_ids.shape[1], REL), 1))
    out_ref[...] = sum(dot(hit, piece) for piece in reversed(split3(table_ref[...])))


def block(
    step, at_ref, wire_in_ref, slots_ref, negative_ref, relation_ref, rel_ids_ref,
    wire_ref, keep_ref, give_ref, rows_ref, weights_ref, held_ref, in_sems, sent_ref, out_sems,
):
    edges, parts = 128, 4
    part = SLOTS // parts
    per = OWN // parts
    copies = wire_copies(wire_in_ref, held_ref, in_sems)
    for copy in copies:
        copy.start()
    unpack_all(copies, held_ref, rows_ref)
    slots = slots_ref[step : step + 1, :]
    slots_column = jnp.concatenate(
        [lane_to_column(slots[:, 128 * k : 128 * k + 128].astype(F32))[:, :1] for k in range(2)], axis=0
    ).astype(I32)
    fetched = jnp.zeros((2 * edges, 512), F32)
    for g in range(parts):
        hit = one_hot(slots_column == iota((2 * edges, part), 1) + part * g)
        fetched = fetched + dot(hit, rows_ref[part * g : part * g + part, :])
    fetched = to_narrow(fetched)
    head, tail = fetched[:edges], fetched[edges:]
    head_re, head_im = complex_parts(head)
    tail_re, tail_im = complex_parts(tail)
    rel_re, rel_im = complex_parts(relation_ref[...])
    query_tail = join(head_re * rel_re - head_im * rel_im, head_re * rel_im + head_im * rel_re)
    query_head = join(rel_re * tail_re + rel_im * tail_im, rel_re * tail_im - rel_im * tail_re)
    positive = jnp.sum(query_tail * tail, axis=1, keepdims=True)
    queries = to_wide(jnp.concatenate([query_tail, query_head], axis=0)).astype(BF16)
    pull = jnp.zeros((2 * edges, 512), F32)
    for g in range(parts):
        here = slice(part * g, part * g + part)
        scores = dot(queries, rows_ref[here, :], ((1,), (1,)))
        weights = jax.nn.sigmoid(scores) * (negative_ref[step : step + 1, here] / 1024)
        weights = weights.astype(BF16)
        weights_ref[:, here] = weights
        pull = pull + dot(weights, rows_ref[here, :])
    pull = to_narrow(pull)
    positive_weight = -jax.nn.sigmoid(-positive)
    pull_re, pull_im = complex_parts(positive_weight * tail + pull[:edges])
    push_re, push_im = complex_parts(pull[edges:])
    grad_head = join(pull_re * rel_re + pull_im * rel_im, pull_im * rel_re - pull_re * rel_im)
    grad_tail = positive_weight * query_tail + join(
        push_re * rel_re - push_im * rel_im, push_re * rel_im + push_im * rel_re
    )
    edge_grads = to_wide(jnp.concatenate([grad_head, grad_tail], axis=0)).astype(BF16)
    outs = []
    for g in range(parts):
        here = slice(part * g, part * g + part)
        grads = dot(weights_ref[:, here], queries, ((0,), (0,)))
        hit = one_hot(iota((part, 2 * edges), 0) + part * g == slots)
        grads = grads + dot(hit, edge_grads)
        for j in range(per):
            sent_ref[per * g + j] = pack(grads[CAP * j : CAP * j + CAP]).astype(BF16)
        blocks = pl.ds(per * g, per)
        outs.append(pltpu.make_async_copy(sent_ref.at[blocks], wire_ref.at[blocks], out_sems.at[g]))
        outs[-1].start()
    grad_relation = to_wide(
        join(
            pull_re * head_re + pull_im * head_im + push_re * tail_re + push_im * tail_im,
            pull_im * head_re - pull_re * head_im + push_re * tail_im - push_im * tail_re,
        )
    )
    high = grad_relation.astype(BF16)
    low = (grad_relation - high.astype(F32)).astype(BF16)
    rel_ids = rel_ids_ref[0, step : step + 1, :]
    half = REL // 128
    for i in range(half):
        dense = []
        for k in range(2):
            hit = one_hot(iota((64, edges), 0) + 64 * (half * k + i) == rel_ids)
            dense.append(pack_relations(dot(hit, high) + dot(hit, low)))
        here = slice(200 * i, 200 * i + 200)
        keep_ref[here, :] = jnp.where(at_ref[3] == 0, dense[0], dense[1])
        give_ref[here, :] = jnp.where(at_ref[3] == 0, dense[1], dense[0])
    for copy in outs:
        copy.wait()


def scatter_stage(axis, at_ref, own_ref, *refs):
    n = (4, 4)[axis]
    arrived, outs, sum_ref = refs[: -n - 1], refs[-n - 1 : -1], refs[-1]
    total = own_ref[...].astype(F32)
    for ref in arrived:
        total = total + ref[...].astype(F32)
    sum_ref[: total.shape[0], :] = total
    rows = outs[0].shape[0]
    if total.shape[0] < n * rows:
        sum_ref[total.shape[0] :, :] = jnp.zeros((n * rows - total.shape[0], 128), F32)
    for d in range(n):
        start = pl.multiple_of(lax.rem(at_ref[axis] + d, n) * rows, 8)
        outs[d][...] = sum_ref[pl.ds(start, rows), :].astype(outs[d].dtype)


def sum_y(own_ref, *refs):
    *parts, out_ref = refs
    total = own_ref[...]
    for ref in parts:
        total = total + ref[...]
    out_ref[...] = total.astype(BF16)


def sum_z(at_ref, *refs):
    *parts, out_ref, all_ref = refs
    n = len(parts)
    for d in range(n):
        all_ref[lax.rem(at_ref[2] + n - d, n)] = parts[d][...].astype(F32)
    total = all_ref[0]
    for z in range(1, n):
        total = total + all_ref[z]
    out_ref[...] = total


def gather_y(at_ref, *refs):
    *parts, out_ref, all_ref = refs
    rows = parts[0].shape[0]
    for d in range(4):
        start = pl.multiple_of(lax.rem(at_ref[1] + 4 - d, 4) * rows, 8)
        all_ref[pl.ds(start, rows), :] = parts[d][...]
    out_ref[...] = all_ref[: out_ref.shape[0], :].astype(BF16)


def gather_x(at_ref, _, *refs):
    *parts, out_ref = refs
    rows = parts[0].shape[0]
    for d in range(4):
        start = pl.multiple_of(lax.rem(at_ref[0] + 4 - d, 4) * rows, 16)
        out_ref[pl.ds(start, rows), :] = parts[d][...]


def relation_update(at_ref, mine_ref, other_ref, table_ref, state_ref, new_table_ref, new_state_ref):
    count = REL // 128
    for b in range(count):
        rows = slice(128 * b, 128 * b + 128)
        here = slice(400 * (b % (count // 2)), 400 * (b % (count // 2)) + 400)
        mine, other = mine_ref[here, :].astype(F32), other_ref[here, :].astype(F32)
        dense = jnp.where(at_ref[3] == b // (count // 2), mine, other)
        total = jnp.concatenate([unpack_relations(dense[:200]), unpack_relations(dense[200:])], axis=0)
        state = lane_to_column(state_ref[b : b + 1, :])
        state = state + jnp.sum(total * total, axis=1, keepdims=True) / WIDTH
        new_state_ref[b : b + 1, :] = jnp.transpose(state)[:1]
        new_table_ref[rows, :] = table_ref[rows, :] - total * (RATE * lax.rsqrt(state[:, :1]))


SPACES = {
    "s": pl.BlockSpec(memory_space=pltpu.SMEM),
    "v": pl.BlockSpec(memory_space=pltpu.VMEM),
    "h": pl.BlockSpec(memory_space=pltpu.HBM),
    "a": pl.BlockSpec(memory_space=pl.ANY),
}


def kernel(body, ins, outs, places, scratch=(), flops=0):
    call = pl.pallas_call(
        body,
        out_shape=[pltpu.HBM(o.shape, o.dtype) if k == "h" else o for o, k in zip(outs, places)],
        in_specs=[SPACES[k] for k in ins],
        out_specs=[SPACES[k] for k in places],
        scratch_shapes=scratch,
        compiler_params=pltpu.CompilerParams(vmem_limit_bytes=40 << 20),
        cost_estimate=pl.CostEstimate(flops=flops, bytes_accessed=1 << 20, transcendentals=0),
    )
    return lambda *args: call(
        *[pltpu.with_memory_space_constraint(x, pltpu.HBM) if k == "h" else x for x, k in zip(args, ins)]
    )


def copies(n):
    return pltpu.SemaphoreType.DMA((n,))


def exchange(x):
    return lax.all_to_all(x, "edge", split_axis=0, concat_axis=0, tiled=True)


def edge_of(y, z, core):
    return (y * 8 + z) * 2 + core


def edge_pairs(dy, dz, flip=0):
    return [
        (edge_of(y, z, core), edge_of((y + dy) % 4, (z + dz) % 8, core ^ flip))
        for y in range(4)
        for z in range(8)
        for core in range(2)
    ]


def move(x, axis, d):
    if axis == 0:
        return lax.ppermute(x, "rep", [(k, (k + d) % 4) for k in range(4)])
    return lax.ppermute(x, "edge", edge_pairs(d if axis == 1 else 0, d if axis == 2 else 0))


def relation_scatter(at, keep, give):
    shape = jax.ShapeDtypeStruct
    arrived = [lax.ppermute(give, "edge", edge_pairs(0, 0, 1))]
    own = keep
    for axis, (rows, sent) in enumerate(((DENSE // 8, BF16), (Y_ROWS, F32))):
        own, *parts = kernel(
            lambda *refs, axis=axis: scatter_stage(axis, *refs),
            "sv" + "v" * len(arrived),
            [shape((rows, 128), F32)] + [shape((rows, 128), sent)] * 3,
            "vvvv",
            [pltpu.VMEM((4 * rows, 128), F32)],
        )(at, own, *arrived)
        arrived = [move(part, axis, d + 1) for d, part in enumerate(parts)]
    own = kernel(sum_y, "vvvv", [shape(own.shape, BF16)], "v")(own, *arrived)[0]
    return kernel(sum_z, "s" + "v" * 8, [shape(own.shape, F32)], "v", [pltpu.VMEM((8, *own.shape), F32)])(
        at, own, *[move(own, 2, d) for d in range(1, 8)]
    )[0]


def relation_gather_y(at, own):
    return kernel(
        gather_y, "svvvv", [jax.ShapeDtypeStruct((DENSE // 8, 128), BF16)], "v", [pltpu.VMEM((4 * Y_ROWS, 128), F32)]
    )(at, own, *[move(own, 1, d) for d in (1, 2, 3)])[0]


def relation_gather_x(at, own, after):
    own = kernel(gather_x, "savvvv", [jax.ShapeDtypeStruct((DENSE // 2, 128), BF16)], "v")(
        at, after, own, *[move(own, 0, d) for d in (1, 2, 3)]
    )[0]
    return own, lax.ppermute(own, "edge", edge_pairs(0, 0, 1))


def shards(entities, ent_accum, relations, rel_accum, heads, tails, negatives, rel_ids):
    steps = heads.shape[1]
    shape = jax.ShapeDtypeStruct
    wire = shape((OWN, 128, 128), BF16)
    held = pltpu.VMEM((OWN, 128, 128), BF16)
    table, accum = entities, ent_accum.reshape(8, 128)
    rel_count = relations.shape[0]
    rel_table = jnp.pad(relations, ((0, REL - rel_count), (0, 0)))
    rel_state = jnp.pad(rel_accum, (0, REL - rel_count), constant_values=1.0).reshape(8, 128)
    edge = lax.axis_index("edge")
    at = jnp.stack([lax.axis_index("rep"), edge // 16, edge // 2 % 8, edge % 2]).astype(I32)
    send, negative, slots = kernel(
        prepare,
        "hhh",
        [shape((OWN, 128), I32), shape((OWN, 128), F32), shape((steps, 256), I32)],
        "hvv",
        [pltpu.VMEM(x.shape, I32) for x in (heads, tails, negatives)] + [pltpu.VMEM((OWN, 128), I32), copies(4)],
    )(heads, tails, negatives)
    named = exchange(send.reshape(OWN, 1, 128)).reshape(OWN, 128)
    wide = kernel(widen, "v", [shape((1024, 512), BF16)], "v")(table)[0]
    flat = jnp.stack([named[:, CAP * s : CAP * s + CAP].reshape(SLOTS) for s in range(steps)])
    negative = jnp.stack([negative[:, CAP * s : CAP * s + CAP].reshape(SLOTS) for s in range(steps)])
    rows = kernel(first_rows, "vv", [wire], "h", [held, copies(8)], 3 << 30)(wide, named)[0]
    for s in range(steps):
        last = s == steps - 1
        relation = kernel(
            lambda *refs, s=s: relation_rows(s, *refs), "vv", [shape((128, WIDTH), F32)], "v"
        )(rel_table, rel_ids)[0]
        rows = exchange(rows)
        dense = shape((DENSE // 2, 128), F32)
        grads, keep, give = kernel(
            lambda *refs, s=s: block(s, *refs),
            "shvvvv",
            [wire, dense, dense],
            "hvv",
            [pltpu.VMEM((SLOTS, 512), BF16), pltpu.VMEM((256, SLOTS), BF16), held, copies(WIRE_PARTS), held, copies(4)],
            4 << 30,
        )(at, rows, slots, negative, relation, rel_ids)
        grads = exchange(grads)
        own = relation_scatter(at, keep, give)
        if last:
            own = relation_gather_y(at, own)
        scratch = [copies(WIRE_PARTS), pltpu.SemaphoreType.DMA, copies(8), held]
        scratch += [pltpu.VMEM((1024, WIDTH), F32), pltpu.VMEM((SLOTS, 512), BF16)]
        if not last:
            scratch += [pltpu.VMEM((1024, 512), BF16), held, copies(8)]
        table, accum, *rows = kernel(
            lambda *refs, s=s, last=last: update(s, last, *refs),
            "hvhvva",
            [shape(table.shape, F32), shape((8, 128), F32)] + ([] if last else [wire]),
            "hv" if last else "hvh",
            scratch,
            5 << 30,
        )(grads, flat, table, accum, named, own)
        rows = None if last else rows[0]
        if not last:
            own = relation_gather_y(at, own)
        mine, other = relation_gather_x(at, own, accum)
        rel_table, rel_state = kernel(
            relation_update, "svvvv", [shape((REL, WIDTH), F32), shape((8, 128), F32)], "vv"
        )(at, mine, other, rel_table, rel_state)
    return table, accum.reshape(1, 1024), rel_table[:rel_count], rel_state.reshape(REL)[:rel_count]


def solution(mesh):
    in_specs = (
        P("rep", "edge", None),
        P("rep", "edge"),
        P(),
        P(),
        P("rep", None, "edge"),
        P("rep", None, "edge"),
        P("rep", None, "edge"),
        P("rep", None, "edge"),
    )
    out_specs = (P("rep", "edge", None), P("rep", "edge"), P(), P())
    return jax.shard_map(shards, mesh=mesh, in_specs=in_specs, out_specs=out_specs, check_vma=False)
```

```python
import jax
import jax.numpy as jnp
from jax import lax
from jax.experimental import pallas as pl
from jax.experimental.pallas import tpu as pltpu
from jax.sharding import PartitionSpec as P

F32, BF16, I32 = jnp.float32, jnp.bfloat16, jnp.int32
RATE = 0.1
OWN = 64
CAP = 40
SLOTS = OWN * CAP
WIDTH = 400
HALF = 200
BODY = 384
REL = 1024
DENSE = REL // 64 * 200
WIRE_PARTS = 4
FIRST_ROWS = 2 * CAP
Y_ROWS = 112


def iota(shape, dim):
    return lax.broadcasted_iota(I32, shape, dim)


def one_hot(hit):
    return jnp.where(hit, 1.0, 0.0).astype(BF16)


def dot(a, b, dims=((1,), (0,))):
    return lax.dot_general(a, b, (dims, ((), ())), preferred_element_type=F32)


def fold_tail(x):
    x = x + pltpu.roll(x, 64, 1)
    x = x + pltpu.roll(x, 32, 1)
    return x + pltpu.roll(x, 16, 1)


def spread_tail(x16):
    rows = x16.shape[0]
    return fold_tail(jnp.concatenate([x16, jnp.zeros((rows, 112), F32)], axis=1))


def to_wide(x):
    return jnp.concatenate([x[:, :BODY], spread_tail(x[:, BODY:])], axis=1)


def to_narrow(x):
    return jnp.concatenate([x[:, :BODY], fold_tail(x[:, BODY:])[:, :16]], axis=1)


def pack(rows):
    group = iota((8, 128), 1) // 16
    tail = jnp.zeros((8, 128), F32)
    for i in range(5):
        tail = jnp.where(group == i, rows[8 * i : 8 * i + 8, BODY:], tail)
    return jnp.concatenate([rows[:, :128], rows[:, 128:256], rows[:, 256:384], tail], axis=0)


def unpack(block):
    group = iota((8, 128), 1) // 16
    tail = jnp.concatenate([jnp.where(group == i, block[120:], 0.0) for i in range(5)], axis=0)
    return jnp.concatenate([block[:40], block[40:80], block[80:120], tail], axis=1)


def pack_relations(rows):
    group = iota((8, 128), 1) // 16
    tail = jnp.zeros((8, 128), F32)
    for i in range(8):
        tail = jnp.where(group == i, rows[8 * i : 8 * i + 8, BODY:], tail)
    return jnp.concatenate([rows[:, :128], rows[:, 128:256], rows[:, 256:384], tail], axis=0)


def unpack_relations(dense):
    group = iota((8, 128), 1) // 16
    tail = jnp.concatenate([jnp.where(group == i, dense[192:], 0.0) for i in range(8)], axis=0)
    return to_narrow(jnp.concatenate([dense[:64], dense[64:128], dense[128:192], tail], axis=1))


def wire_copies(wire_ref, held_ref, sems):
    per = OWN // WIRE_PARTS
    return [
        pltpu.make_async_copy(wire_ref.at[pl.ds(per * g, per)], held_ref.at[pl.ds(per * g, per)], sems.at[g])
        for g in range(WIRE_PARTS)
    ]


def unpack_first(block):
    return jnp.concatenate([block[:CAP], block[CAP:]], axis=1)


def unpack_second(block):
    group = iota((8, 128), 1) // 16
    tail = jnp.concatenate([jnp.where(group == i, block[CAP:], 0.0) for i in range(5)], axis=0)
    return jnp.concatenate([block[:CAP], tail], axis=1)


def unpack_all(copies, held_ref, rows_ref, unpack=unpack):
    per = OWN // WIRE_PARTS // 2
    for g, copy in enumerate(copies):
        copy.wait()

        def pair(e, _):
            two = [unpack(held_ref[2 * e + k].astype(F32)) for k in range(2)]
            at = pl.multiple_of(e * 2 * CAP, 2 * CAP)
            rows_ref[pl.ds(at, 2 * CAP), :] = jnp.concatenate(two, axis=0).astype(BF16)
            return 0

        lax.fori_loop(per * g, per * g + per, pair, 0)


def lane_to_column(row):
    return jnp.transpose(jnp.broadcast_to(row, (128, 128)))


def prepare(heads_in, tails_in, negatives_in, send_ref, negative_ref, slots_ref, heads_ref, tails_ref, negatives_ref, held_ref, sems):
    count = 2 * heads_ref.shape[2] + negatives_ref.shape[2]
    steps = heads_ref.shape[1]
    fetches = [
        pltpu.make_async_copy(source, held, sems.at[k])
        for k, (source, held) in enumerate(
            ((heads_in, heads_ref), (tails_in, tails_ref), (negatives_in, negatives_ref))
        )
    ]
    for copy in fetches:
        copy.start()
    for copy in fetches:
        copy.wait()
    before = one_hot(iota((128, 128), 0) < iota((128, 128), 1))
    send = jnp.zeros((OWN, 128), F32)
    negative = jnp.zeros((OWN, 128), F32)
    for s in range(steps):
        requests = jnp.concatenate(
            [heads_ref[0, s : s + 1, :], tails_ref[0, s : s + 1, :], negatives_ref[0, s : s + 1, :]], axis=1
        )
        owner = lax.shift_right_logical(requests, 10)
        local = requests & 1023
        at_owner = jnp.where(iota((OWN, count), 0) == owner, 1.0, 0.0)
        seen = jnp.zeros((OWN, 1), F32)
        ranks = []
        for j in range(count // 128):
            part = at_owner[:, 128 * j : 128 * j + 128]
            earlier = dot(part.astype(BF16), before) + seen
            ranks.append(jnp.sum(part * earlier, axis=0, keepdims=True))
            seen = seen + jnp.sum(part, axis=1, keepdims=True)
        rank = jnp.concatenate(ranks, axis=1).astype(I32)
        at_rank = one_hot(iota((128, count), 0) == rank + CAP * s)
        high = (at_owner * lax.shift_right_logical(local, 5).astype(F32)).astype(BF16)
        low = (at_owner * (local & 31).astype(F32)).astype(BF16)
        last = ((1,), (1,))
        send = send + dot(high, at_rank, last) * 32.0 + dot(low, at_rank, last)
        chosen = jnp.where(iota((OWN, count), 1) >= 256, at_owner, 0.0).astype(BF16)
        negative = negative + dot(chosen, at_rank, last)
        slots_ref[s : s + 1, :] = (owner * CAP + rank)[:, :256]
    held_ref[...] = send.astype(I32)
    sending = pltpu.make_async_copy(held_ref, send_ref, sems.at[3])
    sending.start()
    negative_ref[...] = negative
    sending.wait()


def gather_rows(named_ref, step, wide_ref, wire_ref, held_ref, sems):
    named = named_ref[...].astype(F32)
    named = jnp.transpose(jnp.concatenate([named, named], axis=0))
    named = named[CAP * step : CAP * step + CAP, :OWN].astype(I32)
    per = OWN // 8
    copies = []
    for g in range(8):
        columns = jnp.concatenate([named[:, per * g + j : per * g + j + 1] for j in range(per)], axis=0)
        hit = one_hot(columns == iota((per * CAP, 1024), 1))
        rows = dot(hit, wide_ref[...])
        for j in range(per):
            held_ref[per * g + j] = pack(rows[CAP * j : CAP * j + CAP]).astype(BF16)
        here = pl.ds(per * g, per)
        copies.append(pltpu.make_async_copy(held_ref.at[here], wire_ref.at[here], sems.at[g]))
        copies[-1].start()
    for copy in copies:
        copy.wait()


def widen(table_ref, wide_ref):
    wide_ref[...] = to_wide(table_ref[0]).astype(BF16)


def first_rows(wide_ref, named_ref, wire_ref, held_ref, sems):
    gather_rows(named_ref, 0, wide_ref, wire_ref, held_ref, sems)


def apply_rows(b, total, accum_ref, new_accum_ref, rows_ref):
    rows = slice(128 * b, 128 * b + 128)
    accum = lane_to_column(accum_ref[b : b + 1, :])
    accum = accum + jnp.sum(total * total, axis=1, keepdims=True) / WIDTH
    new_accum_ref[b : b + 1, :] = jnp.transpose(accum)[:1]
    new = rows_ref[rows, :] - total * (RATE * lax.rsqrt(accum[:, :1]))
    rows_ref[rows, :] = new
    return new


def update(
    step, wire_in_ref, flat_ref, table_ref, accum_ref, named_ref, _, new_table_ref, new_accum_ref, wire_ref,
    in_sems, table_sem, out_sems, held_ref, rows_ref, grads_ref, wide_ref, sent_ref, sent_sems,
):
    copies = wire_copies(wire_in_ref, held_ref, in_sems)
    for copy in copies:
        copy.start()
    table_copy = pltpu.make_async_copy(table_ref.at[0], rows_ref, table_sem)
    table_copy.start()
    unpack_all(copies, held_ref, grads_ref)
    table_copy.wait()
    outs = []
    for b in range(8):
        here = pl.ds(128 * b, 128)
        hit = one_hot(iota((128, SLOTS), 0) + 128 * b == flat_ref[step : step + 1, :])
        total = to_narrow(dot(hit, grads_ref[...]))
        new = apply_rows(b, total, accum_ref, new_accum_ref, rows_ref)
        outs.append(pltpu.make_async_copy(rows_ref.at[here], new_table_ref.at[0, here], out_sems.at[b]))
        outs[-1].start()
        wide_ref[here, :] = to_wide(new).astype(BF16)
    gather_rows(named_ref, step + 1, wide_ref, wire_ref, sent_ref, sent_sems)
    for copy in outs:
        copy.wait()


def first_sums(step, wire_in_ref, flat_ref, sums_ref, in_sems, held_ref, grads_ref):
    copies = wire_copies(wire_in_ref, held_ref, in_sems)
    for copy in copies:
        copy.start()
    unpack_all(copies, held_ref, grads_ref, unpack_first)
    for b in range(8):
        hit = one_hot(iota((128, SLOTS), 0) + 128 * b == flat_ref[step : step + 1, :])
        sums_ref[128 * b : 128 * b + 128, :] = dot(hit, grads_ref[...])


def last_update(
    step, wire_in_ref, flat_ref, sums_ref, table_ref, accum_ref, new_table_ref, new_accum_ref,
    in_sems, table_sem, out_sems, held_ref, rows_ref, grads_ref,
):
    copies = wire_copies(wire_in_ref, held_ref, in_sems)
    for copy in copies:
        copy.start()
    table_copy = pltpu.make_async_copy(table_ref.at[0], rows_ref, table_sem)
    table_copy.start()
    unpack_all(copies, held_ref, grads_ref, unpack_second)
    table_copy.wait()
    outs = []
    for b in range(8):
        here = pl.ds(128 * b, 128)
        hit = one_hot(iota((128, SLOTS), 0) + 128 * b == flat_ref[step : step + 1, :])
        total = to_narrow(jnp.concatenate([sums_ref[here, :], dot(hit, grads_ref[...])], axis=1))
        apply_rows(b, total, accum_ref, new_accum_ref, rows_ref)
        outs.append(pltpu.make_async_copy(rows_ref.at[here], new_table_ref.at[0, here], out_sems.at[b]))
        outs[-1].start()
    for copy in outs:
        copy.wait()


def pass_on(ref, after_ref, out_ref):
    del ref, after_ref, out_ref


def complex_parts(x):
    return x[:, :HALF], x[:, HALF:]


def join(re, im):
    return jnp.concatenate([re, im], axis=1)


def split3(x):
    a = x.astype(BF16)
    x = x - a.astype(F32)
    b = x.astype(BF16)
    return a, b, (x - b.astype(F32)).astype(BF16)


def relation_rows(step, table_ref, rel_ids_ref, out_ref):
    rel_ids = rel_ids_ref[0, step : step + 1, :]
    column = lane_to_column(rel_ids.astype(F32))[:, :1].astype(I32)
    hit = one_hot(column == iota((rel_ids.shape[1], REL), 1))
    out_ref[...] = sum(dot(hit, piece) for piece in reversed(split3(table_ref[...])))


def block(
    step, at_ref, wire_in_ref, slots_ref, negative_ref, relation_ref, rel_ids_ref, *rest
):
    *wire_refs, keep_ref, give_ref, rows_ref, weights_ref, held_ref, in_sems, sent_ref, out_sems = rest
    edges, parts = 128, 4
    part = SLOTS // parts
    per = OWN // parts
    copies = wire_copies(wire_in_ref, held_ref, in_sems)
    for copy in copies:
        copy.start()
    unpack_all(copies, held_ref, rows_ref)
    slots = slots_ref[step : step + 1, :]
    slots_column = jnp.concatenate(
        [lane_to_column(slots[:, 128 * k : 128 * k + 128].astype(F32))[:, :1] for k in range(2)], axis=0
    ).astype(I32)
    fetched = jnp.zeros((2 * edges, 512), F32)
    for g in range(parts):
        hit = one_hot(slots_column == iota((2 * edges, part), 1) + part * g)
        fetched = fetched + dot(hit, rows_ref[part * g : part * g + part, :])
    fetched = to_narrow(fetched)
    head, tail = fetched[:edges], fetched[edges:]
    head_re, head_im = complex_parts(head)
    tail_re, tail_im = complex_parts(tail)
    rel_re, rel_im = complex_parts(relation_ref[...])
    query_tail = join(head_re * rel_re - head_im * rel_im, head_re * rel_im + head_im * rel_re)
    query_head = join(rel_re * tail_re + rel_im * tail_im, rel_re * tail_im - rel_im * tail_re)
    positive = jnp.sum(query_tail * tail, axis=1, keepdims=True)
    queries = to_wide(jnp.concatenate([query_tail, query_head], axis=0)).astype(BF16)
    pull = jnp.zeros((2 * edges, 512), F32)
    for g in range(parts):
        here = slice(part * g, part * g + part)
        scores = dot(queries, rows_ref[here, :], ((1,), (1,)))
        weights = jax.nn.sigmoid(scores) * (negative_ref[step : step + 1, here] / 1024)
        weights = weights.astype(BF16)
        weights_ref[:, here] = weights
        pull = pull + dot(weights, rows_ref[here, :])
    pull = to_narrow(pull)
    positive_weight = -jax.nn.sigmoid(-positive)
    pull_re, pull_im = complex_parts(positive_weight * tail + pull[:edges])
    push_re, push_im = complex_parts(pull[edges:])
    grad_head = join(pull_re * rel_re + pull_im * rel_im, pull_im * rel_re - pull_re * rel_im)
    grad_tail = positive_weight * query_tail + join(
        push_re * rel_re - push_im * rel_im, push_re * rel_im + push_im * rel_re
    )
    edge_grads = to_wide(jnp.concatenate([grad_head, grad_tail], axis=0)).astype(BF16)
    outs = []
    for g in range(parts):
        here = slice(part * g, part * g + part)
        grads = dot(weights_ref[:, here], queries, ((0,), (0,)))
        hit = one_hot(iota((part, 2 * edges), 0) + part * g == slots)
        grads = grads + dot(hit, edge_grads)
        for j in range(per):
            sent_ref[per * g + j] = pack(grads[CAP * j : CAP * j + CAP]).astype(BF16)
        blocks = pl.ds(per * g, per)
        start = 0
        for k, wire_ref in enumerate(wire_refs):
            dense = pl.ds(start, wire_ref.shape[1])
            start += wire_ref.shape[1]
            outs.append(
                pltpu.make_async_copy(sent_ref.at[blocks, dense], wire_ref.at[blocks], out_sems.at[k, g])
            )
            outs[-1].start()
    grad_relation = to_wide(
        join(
            pull_re * head_re + pull_im * head_im + push_re * tail_re + push_im * tail_im,
            pull_im * head_re - pull_re * head_im + push_re * tail_im - push_im * tail_re,
        )
    )
    high = grad_relation.astype(BF16)
    low = (grad_relation - high.astype(F32)).astype(BF16)
    rel_ids = rel_ids_ref[0, step : step + 1, :]
    half = REL // 128
    for i in range(half):
        dense = []
        for k in range(2):
            hit = one_hot(iota((64, edges), 0) + 64 * (half * k + i) == rel_ids)
            dense.append(pack_relations(dot(hit, high) + dot(hit, low)))
        here = slice(200 * i, 200 * i + 200)
        keep_ref[here, :] = jnp.where(at_ref[3] == 0, dense[0], dense[1])
        give_ref[here, :] = jnp.where(at_ref[3] == 0, dense[1], dense[0])
    for copy in outs:
        copy.wait()


def scatter_stage(axis, at_ref, own_ref, *refs):
    n = (4, 4)[axis]
    arrived, outs, sum_ref = refs[: -n - 1], refs[-n - 1 : -1], refs[-1]
    total = own_ref[...].astype(F32)
    for ref in arrived:
        total = total + ref[...].astype(F32)
    sum_ref[: total.shape[0], :] = total
    rows = outs[0].shape[0]
    if total.shape[0] < n * rows:
        sum_ref[total.shape[0] :, :] = jnp.zeros((n * rows - total.shape[0], 128), F32)
    for d in range(n):
        start = pl.multiple_of(lax.rem(at_ref[axis] + d, n) * rows, 8)
        outs[d][...] = sum_ref[pl.ds(start, rows), :].astype(outs[d].dtype)


def sum_y(own_ref, *refs):
    *parts, out_ref = refs
    total = own_ref[...]
    for ref in parts:
        total = total + ref[...]
    out_ref[...] = total.astype(BF16)


def sum_z(at_ref, *refs):
    *parts, out_ref, all_ref = refs
    n = len(parts)
    for d in range(n):
        all_ref[lax.rem(at_ref[2] + n - d, n)] = parts[d][...].astype(F32)
    total = all_ref[0]
    for z in range(1, n):
        total = total + all_ref[z]
    out_ref[...] = total


def gather_y(at_ref, *refs):
    *parts, out_ref, all_ref = refs
    rows = parts[0].shape[0]
    for d in range(4):
        start = pl.multiple_of(lax.rem(at_ref[1] + 4 - d, 4) * rows, 8)
        all_ref[pl.ds(start, rows), :] = parts[d][...]
    out_ref[...] = all_ref[: out_ref.shape[0], :].astype(BF16)


def gather_x(at_ref, *refs):
    *parts, out_ref = refs
    rows = parts[0].shape[0]
    for d in range(4):
        start = pl.multiple_of(lax.rem(at_ref[0] + 4 - d, 4) * rows, 16)
        out_ref[pl.ds(start, rows), :] = parts[d][...]


def relation_update(at_ref, mine_ref, other_ref, table_ref, state_ref, new_table_ref, new_state_ref):
    count = REL // 128
    for b in range(count):
        rows = slice(128 * b, 128 * b + 128)
        here = slice(400 * (b % (count // 2)), 400 * (b % (count // 2)) + 400)
        mine, other = mine_ref[here, :].astype(F32), other_ref[here, :].astype(F32)
        dense = jnp.where(at_ref[3] == b // (count // 2), mine, other)
        total = jnp.concatenate([unpack_relations(dense[:200]), unpack_relations(dense[200:])], axis=0)
        state = lane_to_column(state_ref[b : b + 1, :])
        state = state + jnp.sum(total * total, axis=1, keepdims=True) / WIDTH
        new_state_ref[b : b + 1, :] = jnp.transpose(state)[:1]
        new_table_ref[rows, :] = table_ref[rows, :] - total * (RATE * lax.rsqrt(state[:, :1]))


SPACES = {
    "s": pl.BlockSpec(memory_space=pltpu.SMEM),
    "v": pl.BlockSpec(memory_space=pltpu.VMEM),
    "h": pl.BlockSpec(memory_space=pltpu.HBM),
    "a": pl.BlockSpec(memory_space=pl.ANY),
}


def kernel(body, ins, outs, places, scratch=(), flops=0, aliases=None):
    call = pl.pallas_call(
        body,
        out_shape=[pltpu.HBM(o.shape, o.dtype) if k == "h" else o for o, k in zip(outs, places)],
        in_specs=[SPACES[k] for k in ins],
        out_specs=[SPACES[k] for k in places],
        scratch_shapes=scratch,
        input_output_aliases=aliases or {},
        compiler_params=pltpu.CompilerParams(vmem_limit_bytes=40 << 20),
        cost_estimate=pl.CostEstimate(flops=flops, bytes_accessed=1 << 20, transcendentals=0),
    )
    return lambda *args: call(
        *[pltpu.with_memory_space_constraint(x, pltpu.HBM) if k == "h" else x for x, k in zip(args, ins)]
    )


def copies(n):
    return pltpu.SemaphoreType.DMA((n,))


def exchange(x):
    return lax.all_to_all(x, "edge", split_axis=0, concat_axis=0, tiled=True)


def edge_of(y, z, core):
    return (y * 8 + z) * 2 + core


def edge_pairs(dy, dz, flip=0):
    return [
        (edge_of(y, z, core), edge_of((y + dy) % 4, (z + dz) % 8, core ^ flip))
        for y in range(4)
        for z in range(8)
        for core in range(2)
    ]


def move(x, axis, d):
    if axis == 0:
        return lax.ppermute(x, "rep", [(k, (k + d) % 4) for k in range(4)])
    return lax.ppermute(x, "edge", edge_pairs(d if axis == 1 else 0, d if axis == 2 else 0))


def relation_scatter(at, keep, give):
    shape = jax.ShapeDtypeStruct
    arrived = [lax.ppermute(give, "edge", edge_pairs(0, 0, 1))]
    own = keep
    for axis, (rows, sent) in enumerate(((DENSE // 8, BF16), (Y_ROWS, F32))):
        own, *parts = kernel(
            lambda *refs, axis=axis: scatter_stage(axis, *refs),
            "sv" + "v" * len(arrived),
            [shape((rows, 128), F32)] + [shape((rows, 128), sent)] * 3,
            "vvvv",
            [pltpu.VMEM((4 * rows, 128), F32)],
        )(at, own, *arrived)
        arrived = [move(part, axis, d + 1) for d, part in enumerate(parts)]
    own = kernel(sum_y, "vvvv", [shape(own.shape, BF16)], "v")(own, *arrived)[0]
    return kernel(sum_z, "s" + "v" * 8, [shape(own.shape, F32)], "v", [pltpu.VMEM((8, *own.shape), F32)])(
        at, own, *[move(own, 2, d) for d in range(1, 8)]
    )[0]


def relation_gather_y(at, own):
    return kernel(
        gather_y, "svvvv", [jax.ShapeDtypeStruct((DENSE // 8, 128), BF16)], "v", [pltpu.VMEM((4 * Y_ROWS, 128), F32)]
    )(at, own, *[move(own, 1, d) for d in (1, 2, 3)])[0]


def relation_gather_x(at, own):
    own = kernel(gather_x, "svvvv", [jax.ShapeDtypeStruct((DENSE // 2, 128), BF16)], "v")(
        at, own, *[move(own, 0, d) for d in (1, 2, 3)]
    )[0]
    return own, lax.ppermute(own, "edge", edge_pairs(0, 0, 1))


def shards(entities, ent_accum, relations, rel_accum, heads, tails, negatives, rel_ids):
    steps = heads.shape[1]
    shape = jax.ShapeDtypeStruct
    wire = shape((OWN, 128, 128), BF16)
    held = pltpu.VMEM((OWN, 128, 128), BF16)
    table, accum = entities, ent_accum.reshape(8, 128)
    rel_count = relations.shape[0]
    rel_table = jnp.pad(relations, ((0, REL - rel_count), (0, 0)))
    rel_state = jnp.pad(rel_accum, (0, REL - rel_count), constant_values=1.0).reshape(8, 128)
    edge = lax.axis_index("edge")
    at = jnp.stack([lax.axis_index("rep"), edge // 16, edge // 2 % 8, edge % 2]).astype(I32)
    send, negative, slots = kernel(
        prepare,
        "hhh",
        [shape((OWN, 128), I32), shape((OWN, 128), F32), shape((steps, 256), I32)],
        "hvv",
        [pltpu.VMEM(x.shape, I32) for x in (heads, tails, negatives)] + [pltpu.VMEM((OWN, 128), I32), copies(4)],
    )(heads, tails, negatives)
    named = exchange(send.reshape(OWN, 1, 128)).reshape(OWN, 128)
    wide = kernel(widen, "v", [shape((1024, 512), BF16)], "v")(table)[0]
    flat = jnp.stack([named[:, CAP * s : CAP * s + CAP].reshape(SLOTS) for s in range(steps)])
    negative = jnp.stack([negative[:, CAP * s : CAP * s + CAP].reshape(SLOTS) for s in range(steps)])
    rows = kernel(first_rows, "vv", [wire], "h", [held, copies(8)], 3 << 30)(wide, named)[0]
    for s in range(steps):
        last = s == steps - 1
        relation = kernel(
            lambda *refs, s=s: relation_rows(s, *refs), "vv", [shape((128, WIDTH), F32)], "v"
        )(rel_table, rel_ids)[0]
        rows = exchange(rows)
        dense = shape((DENSE // 2, 128), F32)
        wires = [shape((OWN, n, 128), BF16) for n in ((FIRST_ROWS, 128 - FIRST_ROWS) if last else (128,))]
        *grads, keep, give = kernel(
            lambda *refs, s=s: block(s, *refs),
            "shvvvv",
            wires + [dense, dense],
            "h" * len(wires) + "vv",
            [
                pltpu.VMEM((SLOTS, 512), BF16), pltpu.VMEM((256, SLOTS), BF16), held, copies(WIRE_PARTS), held,
                pltpu.SemaphoreType.DMA((2, 4)),
            ],
            4 << 30,
        )(at, rows, slots, negative, relation, rel_ids)
        grads[0] = exchange(grads[0])
        own = relation_scatter(at, keep, give)
        scratch = [copies(WIRE_PARTS), pltpu.SemaphoreType.DMA, copies(8)]
        outs = [shape(table.shape, F32), shape((8, 128), F32)]
        if last:
            second = kernel(pass_on, "ha", [wires[1]], "h", aliases={0: 0})(grads[1], own)[0]
            second = exchange(second)
            sums = kernel(
                lambda *refs, s=s: first_sums(s, *refs),
                "hv",
                [shape((1024, 256), F32)],
                "v",
                [copies(WIRE_PARTS), pltpu.VMEM((OWN, FIRST_ROWS, 128), BF16), pltpu.VMEM((SLOTS, 256), BF16)],
                2 << 30,
            )(grads[0], flat)[0]
            scratch += [pltpu.VMEM((OWN, 128 - FIRST_ROWS, 128), BF16), pltpu.VMEM((1024, WIDTH), F32)]
            table, accum = kernel(
                lambda *refs, s=s: last_update(s, *refs),
                "hvvhv",
                outs,
                "hv",
                scratch + [pltpu.VMEM((SLOTS, 256), BF16)],
                2 << 30,
            )(second, flat, sums, table, accum)
        else:
            scratch += [held, pltpu.VMEM((1024, WIDTH), F32), pltpu.VMEM((SLOTS, 512), BF16)]
            table, accum, rows = kernel(
                lambda *refs, s=s: update(s, *refs),
                "hvhvva",
                outs + [wire],
                "hvh",
                scratch + [pltpu.VMEM((1024, 512), BF16), held, copies(8)],
                5 << 30,
            )(grads[0], flat, table, accum, named, own)
        own = relation_gather_y(at, own)
        mine, other = relation_gather_x(at, own)
        rel_table, rel_state = kernel(
            relation_update, "svvvv", [shape((REL, WIDTH), F32), shape((8, 128), F32)], "vv"
        )(at, mine, other, rel_table, rel_state)
    return table, accum.reshape(1, 1024), rel_table[:rel_count], rel_state.reshape(REL)[:rel_count]


def solution(mesh):
    in_specs = (
        P("rep", "edge", None),
        P("rep", "edge"),
        P(),
        P(),
        P("rep", None, "edge"),
        P("rep", None, "edge"),
        P("rep", None, "edge"),
        P("rep", None, "edge"),
    )
    out_specs = (P("rep", "edge", None), P("rep", "edge"), P(), P())
    return jax.shard_map(shards, mesh=mesh, in_specs=in_specs, out_specs=out_specs, check_vma=False)
```

```python
import jax
import jax.numpy as jnp
from jax import lax
from jax.experimental import pallas as pl
from jax.experimental.pallas import tpu as pltpu
from jax.sharding import PartitionSpec as P

F32, BF16, I32 = jnp.float32, jnp.bfloat16, jnp.int32
RATE = 0.1
OWN = 64
CAP = 40
SLOTS = OWN * CAP
WIDTH = 400
HALF = 200
BODY = 384
REL = 1024
DENSE = REL // 64 * 200
WIRE_PARTS = 4
FIRST_ROWS = 2 * CAP
Y_ROWS = 112


def iota(shape, dim):
    return lax.broadcasted_iota(I32, shape, dim)


def one_hot(hit):
    return jnp.where(hit, 1.0, 0.0).astype(BF16)


def dot(a, b, dims=((1,), (0,))):
    return lax.dot_general(a, b, (dims, ((), ())), preferred_element_type=F32)


def fold_tail(x):
    x = x + pltpu.roll(x, 64, 1)
    x = x + pltpu.roll(x, 32, 1)
    return x + pltpu.roll(x, 16, 1)


def spread_tail(x16):
    rows = x16.shape[0]
    return fold_tail(jnp.concatenate([x16, jnp.zeros((rows, 112), F32)], axis=1))


def to_wide(x):
    return jnp.concatenate([x[:, :BODY], spread_tail(x[:, BODY:])], axis=1)


def to_narrow(x):
    return jnp.concatenate([x[:, :BODY], fold_tail(x[:, BODY:])[:, :16]], axis=1)


def pack(rows):
    group = iota((8, 128), 1) // 16
    tail = jnp.zeros((8, 128), F32)
    for i in range(5):
        tail = jnp.where(group == i, rows[8 * i : 8 * i + 8, BODY:], tail)
    return jnp.concatenate([rows[:, :128], rows[:, 128:256], rows[:, 256:384], tail], axis=0)


def unpack(block):
    group = iota((8, 128), 1) // 16
    tail = jnp.concatenate([jnp.where(group == i, block[120:], 0.0) for i in range(5)], axis=0)
    return jnp.concatenate([block[:40], block[40:80], block[80:120], tail], axis=1)


def pack_relations(rows):
    group = iota((8, 128), 1) // 16
    tail = jnp.zeros((8, 128), F32)
    for i in range(8):
        tail = jnp.where(group == i, rows[8 * i : 8 * i + 8, BODY:], tail)
    return jnp.concatenate([rows[:, :128], rows[:, 128:256], rows[:, 256:384], tail], axis=0)


def unpack_relations(dense):
    group = iota((8, 128), 1) // 16
    tail = jnp.concatenate([jnp.where(group == i, dense[192:], 0.0) for i in range(8)], axis=0)
    return to_narrow(jnp.concatenate([dense[:64], dense[64:128], dense[128:192], tail], axis=1))


def wire_copies(wire_ref, held_ref, sems):
    per = OWN // WIRE_PARTS
    return [
        pltpu.make_async_copy(wire_ref.at[pl.ds(per * g, per)], held_ref.at[pl.ds(per * g, per)], sems.at[g])
        for g in range(WIRE_PARTS)
    ]


def unpack_first(block):
    return jnp.concatenate([block[:CAP], block[CAP:]], axis=1)


def unpack_second(block):
    group = iota((8, 128), 1) // 16
    tail = jnp.concatenate([jnp.where(group == i, block[CAP:], 0.0) for i in range(5)], axis=0)
    return jnp.concatenate([block[:CAP], tail], axis=1)


def unpack_all(copies, held_ref, rows_ref, unpack=unpack):
    per = OWN // WIRE_PARTS // 2
    for g, copy in enumerate(copies):
        copy.wait()

        def pair(e, _):
            two = [unpack(held_ref[2 * e + k].astype(F32)) for k in range(2)]
            at = pl.multiple_of(e * 2 * CAP, 2 * CAP)
            rows_ref[pl.ds(at, 2 * CAP), :] = jnp.concatenate(two, axis=0).astype(BF16)
            return 0

        lax.fori_loop(per * g, per * g + per, pair, 0)


def lane_to_column(row):
    return jnp.transpose(jnp.broadcast_to(row, (128, 128)))


def prepare(heads_in, tails_in, negatives_in, send_ref, negative_ref, slots_ref, heads_ref, tails_ref, negatives_ref, held_ref, sems):
    count = 2 * heads_ref.shape[2] + negatives_ref.shape[2]
    steps = heads_ref.shape[1]
    fetches = [
        pltpu.make_async_copy(source, held, sems.at[k])
        for k, (source, held) in enumerate(
            ((heads_in, heads_ref), (tails_in, tails_ref), (negatives_in, negatives_ref))
        )
    ]
    for copy in fetches:
        copy.start()
    for copy in fetches:
        copy.wait()
    before = one_hot(iota((128, 128), 0) < iota((128, 128), 1))
    send = jnp.zeros((OWN, 128), F32)
    negative = jnp.zeros((OWN, 128), F32)
    for s in range(steps):
        requests = jnp.concatenate(
            [heads_ref[0, s : s + 1, :], tails_ref[0, s : s + 1, :], negatives_ref[0, s : s + 1, :]], axis=1
        )
        owner = lax.shift_right_logical(requests, 10)
        local = requests & 1023
        at_owner = jnp.where(iota((OWN, count), 0) == owner, 1.0, 0.0)
        seen = jnp.zeros((OWN, 1), F32)
        ranks = []
        for j in range(count // 128):
            part = at_owner[:, 128 * j : 128 * j + 128]
            earlier = dot(part.astype(BF16), before) + seen
            ranks.append(jnp.sum(part * earlier, axis=0, keepdims=True))
            seen = seen + jnp.sum(part, axis=1, keepdims=True)
        rank = jnp.concatenate(ranks, axis=1).astype(I32)
        at_rank = one_hot(iota((128, count), 0) == rank + CAP * s)
        high = (at_owner * lax.shift_right_logical(local, 5).astype(F32)).astype(BF16)
        low = (at_owner * (local & 31).astype(F32)).astype(BF16)
        last = ((1,), (1,))
        send = send + dot(high, at_rank, last) * 32.0 + dot(low, at_rank, last)
        chosen = jnp.where(iota((OWN, count), 1) >= 256, at_owner, 0.0).astype(BF16)
        negative = negative + dot(chosen, at_rank, last)
        slots_ref[s : s + 1, :] = (owner * CAP + rank)[:, :256]
    held_ref[...] = send.astype(I32)
    sending = pltpu.make_async_copy(held_ref, send_ref, sems.at[3])
    sending.start()
    negative_ref[...] = negative
    sending.wait()


def gather_rows(named_ref, step, wide_ref, wire_ref, held_ref, sems):
    named = named_ref[...].astype(F32)
    named = jnp.transpose(jnp.concatenate([named, named], axis=0))
    named = named[CAP * step : CAP * step + CAP, :OWN].astype(I32)
    per = OWN // 8
    copies = []
    for g in range(8):
        columns = jnp.concatenate([named[:, per * g + j : per * g + j + 1] for j in range(per)], axis=0)
        hit = one_hot(columns == iota((per * CAP, 1024), 1))
        rows = dot(hit, wide_ref[...])
        for j in range(per):
            held_ref[per * g + j] = pack(rows[CAP * j : CAP * j + CAP]).astype(BF16)
        here = pl.ds(per * g, per)
        copies.append(pltpu.make_async_copy(held_ref.at[here], wire_ref.at[here], sems.at[g]))
        copies[-1].start()
    for copy in copies:
        copy.wait()


def widen(table_ref, wide_ref):
    wide_ref[...] = to_wide(table_ref[0]).astype(BF16)


def first_rows(wide_ref, named_ref, wire_ref, held_ref, sems):
    gather_rows(named_ref, 0, wide_ref, wire_ref, held_ref, sems)


def to_columns(state_ref):
    return jnp.transpose(jnp.concatenate([state_ref[...], jnp.zeros((120, 128), F32)], axis=0))


def adagrad(b, total, old, states):
    state = states[:, b : b + 1] + jnp.sum(total * total, axis=1, keepdims=True) / WIDTH
    new = old - total * (RATE * lax.rsqrt(state))
    return new, jnp.where(iota((128, 128), 1) == b, state, states)


def update(
    step, wire_in_ref, flat_ref, table_ref, accum_ref, named_ref, *rest
):
    new_table_ref, new_accum_ref, wire_ref, in_sems, table_sem, out_sems, *rest = rest[7:]
    held_ref, rows_ref, grads_ref, wide_ref, sent_ref, sent_sems = rest
    copies = wire_copies(wire_in_ref, held_ref, in_sems)
    for copy in copies:
        copy.start()
    table_copy = pltpu.make_async_copy(table_ref.at[0], rows_ref, table_sem)
    table_copy.start()
    unpack_all(copies, held_ref, grads_ref)
    table_copy.wait()
    outs = []
    states = to_columns(accum_ref)
    for b in range(8):
        here = pl.ds(128 * b, 128)
        hit = one_hot(iota((128, SLOTS), 0) + 128 * b == flat_ref[step : step + 1, :])
        total = to_narrow(dot(hit, grads_ref[...]))
        new, states = adagrad(b, total, rows_ref[here, :], states)
        rows_ref[here, :] = new
        outs.append(pltpu.make_async_copy(rows_ref.at[here], new_table_ref.at[0, here], out_sems.at[b]))
        outs[-1].start()
        wide_ref[here, :] = to_wide(new).astype(BF16)
    new_accum_ref[...] = jnp.transpose(states)[:8]
    gather_rows(named_ref, step + 1, wide_ref, wire_ref, sent_ref, sent_sems)
    for copy in outs:
        copy.wait()


def first_sums(step, wire_in_ref, flat_ref, sums_ref, in_sems, held_ref, grads_ref):
    copies = wire_copies(wire_in_ref, held_ref, in_sems)
    for copy in copies:
        copy.start()
    unpack_all(copies, held_ref, grads_ref, unpack_first)
    for b in range(8):
        hit = one_hot(iota((128, SLOTS), 0) + 128 * b == flat_ref[step : step + 1, :])
        sums_ref[128 * b : 128 * b + 128, :] = dot(hit, grads_ref[...])


def last_update(
    step, wire_in_ref, flat_ref, sums_ref, table_ref, accum_ref, new_table_ref, new_accum_ref,
    in_sems, table_sem, out_sems, held_ref, rows_ref, grads_ref, turned_ref,
):
    copies = wire_copies(wire_in_ref, held_ref, in_sems)
    for copy in copies:
        copy.start()
    table_copy = pltpu.make_async_copy(table_ref.at[0], rows_ref, table_sem)
    table_copy.start()
    unpack_all(copies, held_ref, grads_ref, unpack_second)
    table_copy.wait()
    outs = []
    states = to_columns(accum_ref)
    for b in range(8):
        here = pl.ds(128 * b, 128)
        hit = one_hot(iota((128, SLOTS), 0) + 128 * b == flat_ref[step : step + 1, :])
        total = to_narrow(jnp.concatenate([sums_ref[here, :], dot(hit, grads_ref[...])], axis=1))
        new, states = adagrad(b, total, rows_ref[here, :], states)
        turned_ref[b] = jnp.transpose(new)
        outs.append(pltpu.make_async_copy(turned_ref.at[b], new_table_ref.at[0, :, here], out_sems.at[b]))
        outs[-1].start()
    new_accum_ref[...] = jnp.transpose(states)[:8]
    for copy in outs:
        copy.wait()


def pass_on(ref, after_ref, out_ref):
    del ref, after_ref, out_ref


def complex_parts(x):
    return x[:, :HALF], x[:, HALF:]


def join(re, im):
    return jnp.concatenate([re, im], axis=1)


def split3(x):
    a = x.astype(BF16)
    x = x - a.astype(F32)
    b = x.astype(BF16)
    return a, b, (x - b.astype(F32)).astype(BF16)


def relation_rows(step, table_ref, rel_ids_ref, out_ref):
    rel_ids = rel_ids_ref[0, step : step + 1, :]
    column = lane_to_column(rel_ids.astype(F32))[:, :1].astype(I32)
    hit = one_hot(column == iota((rel_ids.shape[1], REL), 1))
    out_ref[...] = sum(dot(hit, piece) for piece in reversed(split3(table_ref[...])))


def block(
    step, at_ref, wire_in_ref, slots_ref, negative_ref, relation_ref, rel_ids_ref, *rest
):
    *rest, sent_ref, out_sems, kept_ref, keep_sems = rest
    *wire_refs, keep_ref, give_ref, rows_ref, weights_ref, held_ref, in_sems = rest
    edges, parts = 128, 4
    part = SLOTS // parts
    per = OWN // parts
    copies = wire_copies(wire_in_ref, held_ref, in_sems)
    for copy in copies:
        copy.start()
    unpack_all(copies, held_ref, rows_ref)
    slots = slots_ref[step : step + 1, :]
    slots_column = jnp.concatenate(
        [lane_to_column(slots[:, 128 * k : 128 * k + 128].astype(F32))[:, :1] for k in range(2)], axis=0
    ).astype(I32)
    fetched = jnp.zeros((2 * edges, 512), F32)
    for g in range(parts):
        here = slice(part * g, part * g + part)
        hit = one_hot(slots_column == iota((2 * edges, part), 1) + part * g)
        weights_ref[2 * edges :, here] = hit
        fetched = fetched + dot(hit, rows_ref[here, :])
    fetched = to_narrow(fetched)
    head, tail = fetched[:edges], fetched[edges:]
    head_re, head_im = complex_parts(head)
    tail_re, tail_im = complex_parts(tail)
    rel_re, rel_im = complex_parts(relation_ref[...])
    query_tail = join(head_re * rel_re - head_im * rel_im, head_re * rel_im + head_im * rel_re)
    query_head = join(rel_re * tail_re + rel_im * tail_im, rel_re * tail_im - rel_im * tail_re)
    positive = jnp.sum(query_tail * tail, axis=1, keepdims=True)
    queries = to_wide(jnp.concatenate([query_tail, query_head], axis=0)).astype(BF16)
    pull = jnp.zeros((2 * edges, 512), F32)
    for g in range(parts):
        here = slice(part * g, part * g + part)
        scores = dot(queries, rows_ref[here, :], ((1,), (1,)))
        weights = jax.nn.sigmoid(scores) * (negative_ref[step : step + 1, here] / 1024)
        weights = weights.astype(BF16)
        weights_ref[: 2 * edges, here] = weights
        pull = pull + dot(weights, rows_ref[here, :])
    pull = to_narrow(pull)
    positive_weight = -jax.nn.sigmoid(-positive)
    pull_re, pull_im = complex_parts(positive_weight * tail + pull[:edges])
    push_re, push_im = complex_parts(pull[edges:])
    grad_head = join(pull_re * rel_re + pull_im * rel_im, pull_im * rel_re - pull_re * rel_im)
    grad_tail = positive_weight * query_tail + join(
        push_re * rel_re - push_im * rel_im, push_re * rel_im + push_im * rel_re
    )
    edge_grads = to_wide(jnp.concatenate([grad_head, grad_tail], axis=0)).astype(BF16)
    edge_grads = jnp.concatenate([queries, edge_grads], axis=0)
    outs = []
    for g in range(parts):
        here = slice(part * g, part * g + part)
        grads = dot(weights_ref[:, here], edge_grads, ((0,), (0,)))
        for j in range(per):
            sent_ref[per * g + j] = pack(grads[CAP * j : CAP * j + CAP]).astype(BF16)
        blocks = pl.ds(per * g, per)
        start = 0
        for k, wire_ref in enumerate(wire_refs):
            dense = pl.ds(start, wire_ref.shape[1])
            start += wire_ref.shape[1]
            outs.append(
                pltpu.make_async_copy(sent_ref.at[blocks, dense], wire_ref.at[blocks], out_sems.at[k, g])
            )
            outs[-1].start()
    grad_relation = to_wide(
        join(
            pull_re * head_re + pull_im * head_im + push_re * tail_re + push_im * tail_im,
            pull_im * head_re - pull_re * head_im + push_re * tail_im - push_im * tail_re,
        )
    )
    high = grad_relation.astype(BF16)
    low = (grad_relation - high.astype(F32)).astype(BF16)
    rel_ids = rel_ids_ref[0, step : step + 1, :]
    half = REL // 128
    for i in range(half):
        dense = []
        for k in range(2):
            hit = one_hot(iota((64, edges), 0) + 64 * (half * k + i) == rel_ids)
            dense.append(pack_relations(dot(hit, high) + dot(hit, low)))
        here = slice(200 * i, 200 * i + 200)
        kept_ref[0, here, :] = jnp.where(at_ref[3] == 0, dense[0], dense[1])
        kept_ref[1, here, :] = jnp.where(at_ref[3] == 0, dense[1], dense[0])
        dense = pl.ds(200 * i, 200)
        for k, out_ref in enumerate((give_ref, keep_ref)):
            outs.append(
                pltpu.make_async_copy(kept_ref.at[1 - k, dense], out_ref.at[dense], keep_sems.at[k, i])
            )
            outs[-1].start()
    for copy in outs:
        copy.wait()


def scatter_stage(axis, at_ref, own_ref, *refs):
    n = (4, 4)[axis]
    arrived, outs, sum_ref = refs[: -n - 1], refs[-n - 1 : -1], refs[-1]
    total = own_ref[...].astype(F32)
    for ref in arrived:
        total = total + ref[...].astype(F32)
    sum_ref[: total.shape[0], :] = total
    rows = outs[0].shape[0]
    if total.shape[0] < n * rows:
        sum_ref[total.shape[0] :, :] = jnp.zeros((n * rows - total.shape[0], 128), F32)
    for d in range(n):
        start = pl.multiple_of(lax.rem(at_ref[axis] + d, n) * rows, 8)
        outs[d][...] = sum_ref[pl.ds(start, rows), :].astype(outs[d].dtype)


def sum_y(own_ref, *refs):
    *parts, out_ref = refs
    total = own_ref[...]
    for ref in parts:
        total = total + ref[...]
    out_ref[...] = total.astype(BF16)


def sum_z(at_ref, *refs):
    *parts, out_ref, all_ref = refs
    n = len(parts)
    for d in range(n):
        all_ref[lax.rem(at_ref[2] + n - d, n)] = parts[d][...].astype(F32)
    total = all_ref[0]
    for z in range(1, n):
        total = total + all_ref[z]
    out_ref[...] = total


def gather_y(at_ref, *refs):
    *parts, out_ref, all_ref = refs
    rows = parts[0].shape[0]
    for d in range(4):
        start = pl.multiple_of(lax.rem(at_ref[1] + 4 - d, 4) * rows, 8)
        all_ref[pl.ds(start, rows), :] = parts[d][...]
    out_ref[...] = all_ref[: out_ref.shape[0], :].astype(BF16)


def gather_x(at_ref, *refs):
    *parts, out_ref = refs
    rows = parts[0].shape[0]
    for d in range(4):
        start = pl.multiple_of(lax.rem(at_ref[0] + 4 - d, 4) * rows, 16)
        out_ref[pl.ds(start, rows), :] = parts[d][...]


def relation_update(at_ref, mine_ref, other_ref, table_ref, state_ref, new_table_ref, new_state_ref):
    count = REL // 128
    states = to_columns(state_ref)
    for b in range(count):
        rows = slice(128 * b, 128 * b + 128)
        here = slice(400 * (b % (count // 2)), 400 * (b % (count // 2)) + 400)
        mine, other = mine_ref[here, :], other_ref[here, :]
        dense = jnp.where(at_ref[3] == b // (count // 2), mine, other).astype(F32)
        total = jnp.concatenate([unpack_relations(dense[:200]), unpack_relations(dense[200:])], axis=0)
        new_table_ref[rows, :], states = adagrad(b, total, table_ref[rows, :], states)
    new_state_ref[...] = jnp.transpose(states)[:8]


SPACES = {
    "s": pl.BlockSpec(memory_space=pltpu.SMEM),
    "v": pl.BlockSpec(memory_space=pltpu.VMEM),
    "h": pl.BlockSpec(memory_space=pltpu.HBM),
    "a": pl.BlockSpec(memory_space=pl.ANY),
}


def kernel(body, ins, outs, places, scratch=(), flops=0, aliases=None):
    call = pl.pallas_call(
        body,
        out_shape=[pltpu.HBM(o.shape, o.dtype) if k == "h" else o for o, k in zip(outs, places)],
        in_specs=[SPACES[k] for k in ins],
        out_specs=[SPACES[k] for k in places],
        scratch_shapes=scratch,
        input_output_aliases=aliases or {},
        compiler_params=pltpu.CompilerParams(vmem_limit_bytes=30 << 20),
        cost_estimate=pl.CostEstimate(flops=flops, bytes_accessed=1 << 20, transcendentals=0),
    )
    return lambda *args: call(
        *[pltpu.with_memory_space_constraint(x, pltpu.HBM) if k == "h" else x for x, k in zip(args, ins)]
    )


def copies(n):
    return pltpu.SemaphoreType.DMA((n,))


def exchange(x):
    return lax.all_to_all(x, "edge", split_axis=0, concat_axis=0, tiled=True)


def edge_of(y, z, core):
    return (y * 8 + z) * 2 + core


def edge_pairs(dy, dz, flip=0):
    return [
        (edge_of(y, z, core), edge_of((y + dy) % 4, (z + dz) % 8, core ^ flip))
        for y in range(4)
        for z in range(8)
        for core in range(2)
    ]


def move(x, axis, d):
    if axis == 0:
        return lax.ppermute(x, "rep", [(k, (k + d) % 4) for k in range(4)])
    return lax.ppermute(x, "edge", edge_pairs(d if axis == 1 else 0, d if axis == 2 else 0))


def relation_scatter(at, keep, give):
    shape = jax.ShapeDtypeStruct
    arrived = [lax.ppermute(give, "edge", edge_pairs(0, 0, 1))]
    own = keep
    for axis, (rows, sent) in enumerate(((DENSE // 8, BF16), (Y_ROWS, F32))):
        own, *parts = kernel(
            lambda *refs, axis=axis: scatter_stage(axis, *refs),
            "sv" + "v" * len(arrived),
            [shape((rows, 128), F32)] + [shape((rows, 128), sent)] * 3,
            "vvvv",
            [pltpu.VMEM((4 * rows, 128), F32)],
        )(at, own, *arrived)
        arrived = [move(part, axis, d + 1) for d, part in enumerate(parts)]
    own = kernel(sum_y, "vvvv", [shape(own.shape, BF16)], "v")(own, *arrived)[0]
    arrived = [move(own, 2, d) for d in range(1, 8)]
    own = kernel(sum_z, "s" + "v" * 8, [shape(own.shape, F32)], "v", [pltpu.VMEM((8, *own.shape), F32)])(
        at, own, *arrived
    )[0]
    return own, arrived


def relation_gather_y(at, own):
    return kernel(
        gather_y, "svvvv", [jax.ShapeDtypeStruct((DENSE // 8, 128), BF16)], "v", [pltpu.VMEM((4 * Y_ROWS, 128), F32)]
    )(at, own, *[move(own, 1, d) for d in (1, 2, 3)])[0]


def relation_gather_x(at, own):
    own = kernel(gather_x, "svvvv", [jax.ShapeDtypeStruct((DENSE // 2, 128), BF16)], "v")(
        at, own, *[move(own, 0, d) for d in (1, 2, 3)]
    )[0]
    return own, lax.ppermute(own, "edge", edge_pairs(0, 0, 1))


def shards(entities, ent_accum, relations, rel_accum, heads, tails, negatives, rel_ids):
    steps = heads.shape[1]
    shape = jax.ShapeDtypeStruct
    wire = shape((OWN, 128, 128), BF16)
    held = pltpu.VMEM((OWN, 128, 128), BF16)
    table, accum = entities, ent_accum.reshape(8, 128)
    rel_count = relations.shape[0]
    rel_table = jnp.pad(relations, ((0, REL - rel_count), (0, 0)))
    rel_state = jnp.pad(rel_accum, (0, REL - rel_count), constant_values=1.0).reshape(8, 128)
    edge = lax.axis_index("edge")
    at = jnp.stack([lax.axis_index("rep"), edge // 16, edge // 2 % 8, edge % 2]).astype(I32)
    send, negative, slots = kernel(
        prepare,
        "hhh",
        [shape((OWN, 128), I32), shape((OWN, 128), F32), shape((steps, 256), I32)],
        "hvv",
        [pltpu.VMEM(x.shape, I32) for x in (heads, tails, negatives)] + [pltpu.VMEM((OWN, 128), I32), copies(4)],
    )(heads, tails, negatives)
    named = exchange(send.reshape(OWN, 1, 128)).reshape(OWN, 128)
    wide = kernel(widen, "v", [shape((1024, 512), BF16)], "v")(table)[0]
    flat = jnp.stack([named[:, CAP * s : CAP * s + CAP].reshape(SLOTS) for s in range(steps)])
    negative = jnp.stack([negative[:, CAP * s : CAP * s + CAP].reshape(SLOTS) for s in range(steps)])
    rows = kernel(first_rows, "vv", [wire], "h", [held, copies(8)], 3 << 30)(wide, named)[0]
    for s in range(steps):
        last = s == steps - 1
        relation = kernel(
            lambda *refs, s=s: relation_rows(s, *refs), "vv", [shape((128, WIDTH), F32)], "v"
        )(rel_table, rel_ids)[0]
        rows = exchange(rows)
        dense = shape((DENSE // 2, 128), F32)
        wires = [shape((OWN, n, 128), BF16) for n in ((FIRST_ROWS, 128 - FIRST_ROWS) if last else (128,))]
        *grads, keep, give = kernel(
            lambda *refs, s=s: block(s, *refs),
            "shvvvv",
            wires + [dense, dense],
            "h" * len(wires) + "hh",
            [
                pltpu.VMEM((SLOTS, 512), BF16), pltpu.VMEM((512, SLOTS), BF16), held, copies(WIRE_PARTS), held,
                pltpu.SemaphoreType.DMA((2, 4)), pltpu.VMEM((2, DENSE // 2, 128), F32),
                pltpu.SemaphoreType.DMA((2, REL // 128)),
            ],
            4 << 30,
        )(at, rows, slots, negative, relation, rel_ids)
        grads[0] = exchange(grads[0])
        own, arrived = relation_scatter(at, keep, give)
        scratch = [copies(WIRE_PARTS), pltpu.SemaphoreType.DMA, copies(8)]
        outs = [shape(table.shape, F32), shape((8, 128), F32)]
        if last:
            second = kernel(pass_on, "ha", [wires[1]], "h", aliases={0: 0})(grads[1], own)[0]
            second = exchange(second)
            sums = kernel(
                lambda *refs, s=s: first_sums(s, *refs),
                "hv",
                [shape((1024, 256), F32)],
                "v",
                [copies(WIRE_PARTS), pltpu.VMEM((OWN, FIRST_ROWS, 128), BF16), pltpu.VMEM((SLOTS, 256), BF16)],
                2 << 30,
            )(grads[0], flat)[0]
            scratch += [pltpu.VMEM((OWN, 128 - FIRST_ROWS, 128), BF16), pltpu.VMEM((1024, WIDTH), F32)]
            table, accum = kernel(
                lambda *refs, s=s: last_update(s, *refs),
                "hvvhv",
                [shape((1, WIDTH, 1024), F32), outs[1]],
                "hv",
                scratch + [pltpu.VMEM((SLOTS, 256), BF16), pltpu.VMEM((8, WIDTH, 128), F32)],
                2 << 30,
            )(second, flat, sums, table, accum)
            table = jnp.swapaxes(table, 1, 2)
        else:
            scratch += [held, pltpu.VMEM((1024, WIDTH), F32), pltpu.VMEM((SLOTS, 512), BF16)]
            table, accum, rows = kernel(
                lambda *refs, s=s: update(s, *refs),
                "hvhvv" + "a" * len(arrived),
                outs + [wire],
                "hvh",
                scratch + [pltpu.VMEM((1024, 512), BF16), held, copies(8)],
                5 << 30,
            )(grads[0], flat, table, accum, named, *arrived)
        own = relation_gather_y(at, own)
        mine, other = relation_gather_x(at, own)
        rel_table, rel_state = kernel(
            relation_update, "svvvv", [shape((REL, WIDTH), F32), shape((8, 128), F32)], "vv"
        )(at, mine, other, rel_table, rel_state)
    return table, accum.reshape(1, 1024), rel_table[:rel_count], rel_state.reshape(REL)[:rel_count]


def solution(mesh):
    in_specs = (
        P("rep", "edge", None),
        P("rep", "edge"),
        P(),
        P(),
        P("rep", None, "edge"),
        P("rep", None, "edge"),
        P("rep", None, "edge"),
        P("rep", None, "edge"),
    )
    out_specs = (P("rep", "edge", None), P("rep", "edge"), P(), P())
    return jax.shard_map(shards, mesh=mesh, in_specs=in_specs, out_specs=out_specs, check_vma=False)
```

```python
import jax
import jax.numpy as jnp
from jax import lax
from jax.experimental import pallas as pl
from jax.experimental.pallas import tpu as pltpu
from jax.sharding import PartitionSpec as P

F32, BF16, I32 = jnp.float32, jnp.bfloat16, jnp.int32
RATE = 0.1
OWN = 64
CAP = 40
SLOTS = OWN * CAP
WIDTH = 400
HALF = 200
BODY = 384
REL = 1024
DENSE = REL // 64 * 200
WIRE_PARTS = 4
FIRST_ROWS = 2 * CAP
Y_ROWS = 112


def iota(shape, dim):
    return lax.broadcasted_iota(I32, shape, dim)


def one_hot(hit):
    return jnp.where(hit, 1.0, 0.0).astype(BF16)


def dot(a, b, dims=((1,), (0,))):
    return lax.dot_general(a, b, (dims, ((), ())), preferred_element_type=F32)


def fold_tail(x):
    x = x + pltpu.roll(x, 64, 1)
    x = x + pltpu.roll(x, 32, 1)
    return x + pltpu.roll(x, 16, 1)


def spread_tail(x16):
    rows = x16.shape[0]
    return fold_tail(jnp.concatenate([x16, jnp.zeros((rows, 112), F32)], axis=1))


def to_wide(x):
    return jnp.concatenate([x[:, :BODY], spread_tail(x[:, BODY:])], axis=1)


def to_narrow(x):
    return jnp.concatenate([x[:, :BODY], fold_tail(x[:, BODY:])[:, :16]], axis=1)


def pack(rows):
    group = iota((8, 128), 1) // 16
    tail = jnp.zeros((8, 128), F32)
    for i in range(5):
        tail = jnp.where(group == i, rows[8 * i : 8 * i + 8, BODY:], tail)
    return jnp.concatenate([rows[:, :128], rows[:, 128:256], rows[:, 256:384], tail], axis=0)


def unpack(block):
    group = iota((8, 128), 1) // 16
    tail = jnp.concatenate([jnp.where(group == i, block[120:], 0.0) for i in range(5)], axis=0)
    return jnp.concatenate([block[:40], block[40:80], block[80:120], tail], axis=1)


def pack_relations(rows):
    group = iota((8, 128), 1) // 16
    tail = jnp.zeros((8, 128), F32)
    for i in range(8):
        tail = jnp.where(group == i, rows[8 * i : 8 * i + 8, BODY:], tail)
    return jnp.concatenate([rows[:, :128], rows[:, 128:256], rows[:, 256:384], tail], axis=0)


def unpack_relations(dense):
    group = iota((8, 128), 1) // 16
    tail = jnp.concatenate([jnp.where(group == i, dense[192:], 0.0) for i in range(8)], axis=0)
    return to_narrow(jnp.concatenate([dense[:64], dense[64:128], dense[128:192], tail], axis=1))


def wire_copies(wire_ref, held_ref, sems):
    per = OWN // WIRE_PARTS
    return [
        pltpu.make_async_copy(wire_ref.at[pl.ds(per * g, per)], held_ref.at[pl.ds(per * g, per)], sems.at[g])
        for g in range(WIRE_PARTS)
    ]


def unpack_first(block):
    return jnp.concatenate([block[:CAP], block[CAP:]], axis=1)


def unpack_second(block):
    group = iota((8, 128), 1) // 16
    tail = jnp.concatenate([jnp.where(group == i, block[CAP:], 0.0) for i in range(5)], axis=0)
    return jnp.concatenate([block[:CAP], tail], axis=1)


def unpack_all(copies, held_ref, rows_ref, unpack=unpack):
    per = OWN // WIRE_PARTS // 2
    for g, copy in enumerate(copies):
        copy.wait()

        def pair(e, _):
            two = [unpack(held_ref[2 * e + k].astype(F32)) for k in range(2)]
            at = pl.multiple_of(e * 2 * CAP, 2 * CAP)
            rows_ref[pl.ds(at, 2 * CAP), :] = jnp.concatenate(two, axis=0).astype(BF16)
            return 0

        lax.fori_loop(per * g, per * g + per, pair, 0)


def lane_to_column(row):
    return jnp.transpose(jnp.broadcast_to(row, (128, 128)))


def prepare(heads_in, tails_in, negatives_in, send_ref, negative_ref, slots_ref, heads_ref, tails_ref, negatives_ref, held_ref, sems):
    count = 2 * heads_ref.shape[2] + negatives_ref.shape[2]
    steps = heads_ref.shape[1]
    fetches = [
        pltpu.make_async_copy(source, held, sems.at[k])
        for k, (source, held) in enumerate(
            ((heads_in, heads_ref), (tails_in, tails_ref), (negatives_in, negatives_ref))
        )
    ]
    for copy in fetches:
        copy.start()
    for copy in fetches:
        copy.wait()
    before = one_hot(iota((128, 128), 0) < iota((128, 128), 1))
    send = jnp.zeros((OWN, 128), F32)
    negative = jnp.zeros((OWN, 128), F32)
    for s in range(steps):
        requests = jnp.concatenate(
            [heads_ref[0, s : s + 1, :], tails_ref[0, s : s + 1, :], negatives_ref[0, s : s + 1, :]], axis=1
        )
        owner = lax.shift_right_logical(requests, 10)
        local = requests & 1023
        at_owner = jnp.where(iota((OWN, count), 0) == owner, 1.0, 0.0)
        seen = jnp.zeros((OWN, 1), F32)
        ranks = []
        for j in range(count // 128):
            part = at_owner[:, 128 * j : 128 * j + 128]
            earlier = dot(part.astype(BF16), before) + seen
            ranks.append(jnp.sum(part * earlier, axis=0, keepdims=True))
            seen = seen + jnp.sum(part, axis=1, keepdims=True)
        rank = jnp.concatenate(ranks, axis=1).astype(I32)
        at_rank = one_hot(iota((128, count), 0) == rank + CAP * s)
        high = (at_owner * lax.shift_right_logical(local, 5).astype(F32)).astype(BF16)
        low = (at_owner * (local & 31).astype(F32)).astype(BF16)
        last = ((1,), (1,))
        send = send + dot(high, at_rank, last) * 32.0 + dot(low, at_rank, last)
        chosen = jnp.where(iota((OWN, count), 1) >= 256, at_owner, 0.0).astype(BF16)
        negative = negative + dot(chosen, at_rank, last)
        slots_ref[s : s + 1, :] = (owner * CAP + rank)[:, :256]
    held_ref[...] = send.astype(I32)
    sending = pltpu.make_async_copy(held_ref, send_ref, sems.at[3])
    sending.start()
    negative_ref[...] = negative
    sending.wait()


def gather_rows(named_ref, step, wide_ref, wire_ref, held_ref, sems):
    named = named_ref[...].astype(F32)
    named = jnp.transpose(jnp.concatenate([named, named], axis=0))
    named = named[CAP * step : CAP * step + CAP, :OWN].astype(I32)
    per = OWN // 8
    copies = []
    for g in range(8):
        columns = jnp.concatenate([named[:, per * g + j : per * g + j + 1] for j in range(per)], axis=0)
        hit = one_hot(columns == iota((per * CAP, 1024), 1))
        rows = dot(hit, wide_ref[...])
        for j in range(per):
            held_ref[per * g + j] = pack(rows[CAP * j : CAP * j + CAP]).astype(BF16)
        here = pl.ds(per * g, per)
        copies.append(pltpu.make_async_copy(held_ref.at[here], wire_ref.at[here], sems.at[g]))
        copies[-1].start()
    for copy in copies:
        copy.wait()


def widen(table_ref, wide_ref):
    wide_ref[...] = to_wide(table_ref[0]).astype(BF16)


def first_rows(wide_ref, named_ref, wire_ref, held_ref, sems):
    gather_rows(named_ref, 0, wide_ref, wire_ref, held_ref, sems)


def to_columns(state_ref):
    return jnp.transpose(jnp.concatenate([state_ref[...], jnp.zeros((120, 128), F32)], axis=0))


def adagrad(b, total, old, states):
    state = states[:, b : b + 1] + jnp.sum(total * total, axis=1, keepdims=True) / WIDTH
    new = old - total * (RATE * lax.rsqrt(state))
    return new, jnp.where(iota((128, 128), 1) == b, state, states)


def apply_rows(b, total, accum_ref, new_accum_ref, rows_ref):
    accum = lane_to_column(accum_ref[b : b + 1, :])
    accum = accum + jnp.sum(total * total, axis=1, keepdims=True) / WIDTH
    new_accum_ref[b : b + 1, :] = jnp.transpose(accum)[:1]
    return rows_ref[128 * b : 128 * b + 128, :] - total * (RATE * lax.rsqrt(accum[:, :1]))


def update(
    step, wire_in_ref, flat_ref, table_ref, accum_ref, named_ref, *rest
):
    new_table_ref, new_accum_ref, wire_ref, in_sems, table_sem, out_sems, *rest = rest[7:]
    held_ref, rows_ref, grads_ref, wide_ref, sent_ref, sent_sems = rest
    copies = wire_copies(wire_in_ref, held_ref, in_sems)
    for copy in copies:
        copy.start()
    table_copy = pltpu.make_async_copy(table_ref.at[0], rows_ref, table_sem)
    table_copy.start()
    unpack_all(copies, held_ref, grads_ref)
    table_copy.wait()
    outs = []
    for b in range(8):
        here = pl.ds(128 * b, 128)
        hit = one_hot(iota((128, SLOTS), 0) + 128 * b == flat_ref[step : step + 1, :])
        total = to_narrow(dot(hit, grads_ref[...]))
        new = apply_rows(b, total, accum_ref, new_accum_ref, rows_ref)
        rows_ref[here, :] = new
        outs.append(pltpu.make_async_copy(rows_ref.at[here], new_table_ref.at[0, here], out_sems.at[b]))
        outs[-1].start()
        wide_ref[here, :] = to_wide(new).astype(BF16)
    gather_rows(named_ref, step + 1, wide_ref, wire_ref, sent_ref, sent_sems)
    for copy in outs:
        copy.wait()


def first_sums(step, wire_in_ref, flat_ref, sums_ref, in_sems, held_ref, grads_ref):
    copies = wire_copies(wire_in_ref, held_ref, in_sems)
    for copy in copies:
        copy.start()
    unpack_all(copies, held_ref, grads_ref, unpack_first)
    for b in range(8):
        hit = one_hot(iota((128, SLOTS), 0) + 128 * b == flat_ref[step : step + 1, :])
        sums_ref[128 * b : 128 * b + 128, :] = dot(hit, grads_ref[...])


def last_update(
    step, wire_in_ref, flat_ref, sums_ref, table_ref, accum_ref, new_table_ref, new_accum_ref,
    in_sems, table_sem, out_sems, held_ref, rows_ref, grads_ref, turned_ref,
):
    copies = wire_copies(wire_in_ref, held_ref, in_sems)
    for copy in copies:
        copy.start()
    table_copy = pltpu.make_async_copy(table_ref.at[0], rows_ref, table_sem)
    table_copy.start()
    unpack_all(copies, held_ref, grads_ref, unpack_second)
    table_copy.wait()
    outs = []
    for b in range(8):
        here = pl.ds(128 * b, 128)
        hit = one_hot(iota((128, SLOTS), 0) + 128 * b == flat_ref[step : step + 1, :])
        total = to_narrow(jnp.concatenate([sums_ref[here, :], dot(hit, grads_ref[...])], axis=1))
        new = apply_rows(b, total, accum_ref, new_accum_ref, rows_ref)
        turned_ref[b] = jnp.transpose(new)
        outs.append(pltpu.make_async_copy(turned_ref.at[b], new_table_ref.at[0, :, here], out_sems.at[b]))
        outs[-1].start()
    for copy in outs:
        copy.wait()


def pass_on(ref, after_ref, out_ref):
    del ref, after_ref, out_ref


def complex_parts(x):
    return x[:, :HALF], x[:, HALF:]


def join(re, im):
    return jnp.concatenate([re, im], axis=1)


def split3(x):
    a = x.astype(BF16)
    x = x - a.astype(F32)
    b = x.astype(BF16)
    return a, b, (x - b.astype(F32)).astype(BF16)


def relation_rows(step, table_ref, rel_ids_ref, out_ref):
    rel_ids = rel_ids_ref[0, step : step + 1, :]
    column = lane_to_column(rel_ids.astype(F32))[:, :1].astype(I32)
    hit = one_hot(column == iota((rel_ids.shape[1], REL), 1))
    out_ref[...] = sum(dot(hit, piece) for piece in reversed(split3(table_ref[...])))


def block(
    step, at_ref, wire_in_ref, slots_ref, negative_ref, relation_ref, rel_ids_ref, *rest
):
    *rest, sent_ref, out_sems, kept_ref, keep_sems = rest
    *wire_refs, keep_ref, give_ref, rows_ref, weights_ref, held_ref, in_sems = rest
    edges, parts = 128, 4
    part = SLOTS // parts
    per = OWN // parts
    copies = wire_copies(wire_in_ref, held_ref, in_sems)
    for copy in copies:
        copy.start()
    unpack_all(copies, held_ref, rows_ref)
    slots = slots_ref[step : step + 1, :]
    slots_column = jnp.concatenate(
        [lane_to_column(slots[:, 128 * k : 128 * k + 128].astype(F32))[:, :1] for k in range(2)], axis=0
    ).astype(I32)
    fetched = jnp.zeros((2 * edges, 512), F32)
    for g in range(parts):
        here = slice(part * g, part * g + part)
        hit = one_hot(slots_column == iota((2 * edges, part), 1) + part * g)
        fetched = fetched + dot(hit, rows_ref[here, :])
    fetched = to_narrow(fetched)
    head, tail = fetched[:edges], fetched[edges:]
    head_re, head_im = complex_parts(head)
    tail_re, tail_im = complex_parts(tail)
    rel_re, rel_im = complex_parts(relation_ref[...])
    query_tail = join(head_re * rel_re - head_im * rel_im, head_re * rel_im + head_im * rel_re)
    query_head = join(rel_re * tail_re + rel_im * tail_im, rel_re * tail_im - rel_im * tail_re)
    positive = jnp.sum(query_tail * tail, axis=1, keepdims=True)
    queries = to_wide(jnp.concatenate([query_tail, query_head], axis=0)).astype(BF16)
    pull = jnp.zeros((2 * edges, 512), F32)
    for g in range(parts):
        here = slice(part * g, part * g + part)
        scores = dot(queries, rows_ref[here, :], ((1,), (1,)))
        weights = jax.nn.sigmoid(scores) * (negative_ref[step : step + 1, here] / 1024)
        weights = weights.astype(BF16)
        weights_ref[:, here] = weights
        pull = pull + dot(weights, rows_ref[here, :])
    pull = to_narrow(pull)
    positive_weight = -jax.nn.sigmoid(-positive)
    pull_re, pull_im = complex_parts(positive_weight * tail + pull[:edges])
    push_re, push_im = complex_parts(pull[edges:])
    grad_head = join(pull_re * rel_re + pull_im * rel_im, pull_im * rel_re - pull_re * rel_im)
    grad_tail = positive_weight * query_tail + join(
        push_re * rel_re - push_im * rel_im, push_re * rel_im + push_im * rel_re
    )
    edge_grads = to_wide(jnp.concatenate([grad_head, grad_tail], axis=0)).astype(BF16)
    outs = []
    for g in range(parts):
        here = slice(part * g, part * g + part)
        grads = dot(weights_ref[:, here], queries, ((0,), (0,)))
        hit = one_hot(iota((part, 2 * edges), 0) + part * g == slots)
        grads = grads + dot(hit, edge_grads)
        for j in range(per):
            sent_ref[per * g + j] = pack(grads[CAP * j : CAP * j + CAP]).astype(BF16)
        blocks = pl.ds(per * g, per)
        start = 0
        for k, wire_ref in enumerate(wire_refs):
            dense = pl.ds(start, wire_ref.shape[1])
            start += wire_ref.shape[1]
            outs.append(
                pltpu.make_async_copy(sent_ref.at[blocks, dense], wire_ref.at[blocks], out_sems.at[k, g])
            )
            outs[-1].start()
    grad_relation = to_wide(
        join(
            pull_re * head_re + pull_im * head_im + push_re * tail_re + push_im * tail_im,
            pull_im * head_re - pull_re * head_im + push_re * tail_im - push_im * tail_re,
        )
    )
    high = grad_relation.astype(BF16)
    low = (grad_relation - high.astype(F32)).astype(BF16)
    rel_ids = rel_ids_ref[0, step : step + 1, :]
    half = REL // 128
    for i in range(half):
        dense = []
        for k in range(2):
            hit = one_hot(iota((64, edges), 0) + 64 * (half * k + i) == rel_ids)
            dense.append(pack_relations(dot(hit, high) + dot(hit, low)))
        here = slice(200 * i, 200 * i + 200)
        kept_ref[0, here, :] = jnp.where(at_ref[3] == 0, dense[0], dense[1])
        kept_ref[1, here, :] = jnp.where(at_ref[3] == 0, dense[1], dense[0])
        dense = pl.ds(200 * i, 200)
        for k, out_ref in enumerate((give_ref, keep_ref)):
            outs.append(
                pltpu.make_async_copy(kept_ref.at[1 - k, dense], out_ref.at[dense], keep_sems.at[k, i])
            )
            outs[-1].start()
    for copy in outs:
        copy.wait()


def scatter_stage(axis, at_ref, own_ref, *refs):
    n = (4, 4)[axis]
    arrived, outs, sum_ref = refs[: -n - 1], refs[-n - 1 : -1], refs[-1]
    total = own_ref[...].astype(F32)
    for ref in arrived:
        total = total + ref[...].astype(F32)
    sum_ref[: total.shape[0], :] = total
    rows = outs[0].shape[0]
    if total.shape[0] < n * rows:
        sum_ref[total.shape[0] :, :] = jnp.zeros((n * rows - total.shape[0], 128), F32)
    for d in range(n):
        start = pl.multiple_of(lax.rem(at_ref[axis] + d, n) * rows, 8)
        outs[d][...] = sum_ref[pl.ds(start, rows), :].astype(outs[d].dtype)


def sum_y(own_ref, *refs):
    *parts, out_ref = refs
    total = own_ref[...]
    for ref in parts:
        total = total + ref[...]
    out_ref[...] = total.astype(BF16)


def add_pair(own_ref, other_ref, out_ref):
    out_ref[...] = (own_ref[...].astype(F32) + other_ref[...].astype(F32)).astype(BF16)


def sum_z(at_ref, *refs):
    *parts, out_ref, all_ref = refs
    n = len(parts)
    for d in range(n):
        all_ref[lax.rem(at_ref[2] + 8 - d, n)] = parts[d][...].astype(F32)
    total = all_ref[0]
    for z in range(1, n):
        total = total + all_ref[z]
    out_ref[...] = total


def gather_y(at_ref, *refs):
    *parts, out_ref, all_ref = refs
    rows = parts[0].shape[0]
    for d in range(4):
        start = pl.multiple_of(lax.rem(at_ref[1] + 4 - d, 4) * rows, 8)
        all_ref[pl.ds(start, rows), :] = parts[d][...]
    out_ref[...] = all_ref[: out_ref.shape[0], :].astype(BF16)


def gather_x(at_ref, *refs):
    *parts, out_ref = refs
    rows = parts[0].shape[0]
    for d in range(4):
        start = pl.multiple_of(lax.rem(at_ref[0] + 4 - d, 4) * rows, 16)
        out_ref[pl.ds(start, rows), :] = parts[d][...]


def relation_update(at_ref, mine_ref, other_ref, table_ref, state_ref, new_table_ref, new_state_ref):
    count = REL // 128
    states = to_columns(state_ref)
    for b in range(count):
        rows = slice(128 * b, 128 * b + 128)
        here = slice(400 * (b % (count // 2)), 400 * (b % (count // 2)) + 400)
        mine, other = mine_ref[here, :], other_ref[here, :]
        dense = jnp.where(at_ref[3] == b // (count // 2), mine, other).astype(F32)
        total = jnp.concatenate([unpack_relations(dense[:200]), unpack_relations(dense[200:])], axis=0)
        new, states = adagrad(b, total, table_ref[rows, :], states)
        if new_table_ref.shape[0] == REL:
            new_table_ref[rows, :] = new
        else:
            end = min(128 * b + 128, new_table_ref.shape[1])
            new_table_ref[:, 128 * b : end] = jnp.transpose(new)[:, : end - 128 * b]
    new_state_ref[...] = jnp.transpose(states)[:8]


SPACES = {
    "s": pl.BlockSpec(memory_space=pltpu.SMEM),
    "v": pl.BlockSpec(memory_space=pltpu.VMEM),
    "h": pl.BlockSpec(memory_space=pltpu.HBM),
    "a": pl.BlockSpec(memory_space=pl.ANY),
}


def kernel(body, ins, outs, places, scratch=(), flops=0, aliases=None):
    call = pl.pallas_call(
        body,
        out_shape=[pltpu.HBM(o.shape, o.dtype) if k == "h" else o for o, k in zip(outs, places)],
        in_specs=[SPACES[k] for k in ins],
        out_specs=[SPACES[k] for k in places],
        scratch_shapes=scratch,
        input_output_aliases=aliases or {},
        compiler_params=pltpu.CompilerParams(vmem_limit_bytes=30 << 20),
        cost_estimate=pl.CostEstimate(flops=flops, bytes_accessed=1 << 20, transcendentals=0),
    )
    return lambda *args: call(
        *[pltpu.with_memory_space_constraint(x, pltpu.HBM) if k == "h" else x for x, k in zip(args, ins)]
    )


def copies(n):
    return pltpu.SemaphoreType.DMA((n,))


def exchange(x):
    return lax.all_to_all(x, "edge", split_axis=0, concat_axis=0, tiled=True)


def edge_of(y, z, core):
    return (y * 8 + z) * 2 + core


def edge_pairs(dy, dz, flip=0):
    return [
        (edge_of(y, z, core), edge_of((y + dy) % 4, (z + dz) % 8, core ^ flip))
        for y in range(4)
        for z in range(8)
        for core in range(2)
    ]


def move(x, axis, d):
    if axis == 0:
        return lax.ppermute(x, "rep", [(k, (k + d) % 4) for k in range(4)])
    return lax.ppermute(x, "edge", edge_pairs(d if axis == 1 else 0, d if axis == 2 else 0))


def relation_scatter(at, keep, give, last):
    shape = jax.ShapeDtypeStruct
    arrived = [lax.ppermute(give, "edge", edge_pairs(0, 0, 1))]
    own = keep
    for axis, (rows, sent) in enumerate(((DENSE // 8, BF16), (Y_ROWS, F32))):
        own, *parts = kernel(
            lambda *refs, axis=axis: scatter_stage(axis, *refs),
            "sv" + "v" * len(arrived),
            [shape((rows, 128), F32)] + [shape((rows, 128), sent)] * 3,
            "vvvv",
            [pltpu.VMEM((4 * rows, 128), F32)],
        )(at, own, *arrived)
        arrived = [move(part, axis, d + 1) for d, part in enumerate(parts)]
    own = kernel(sum_y, "vvvv", [shape(own.shape, BF16)], "v")(own, *arrived)[0]
    n = 8
    if last:
        own = kernel(add_pair, "vv", [shape(own.shape, BF16)], "v")(own, move(own, 2, 4))[0]
        n = 4
    arrived = [move(own, 2, d) for d in range(1, n)]
    own = kernel(sum_z, "s" + "v" * n, [shape(own.shape, F32)], "v", [pltpu.VMEM((n, *own.shape), F32)])(
        at, own, *arrived
    )[0]
    return own, arrived


def relation_gather_y(at, own):
    return kernel(
        gather_y, "svvvv", [jax.ShapeDtypeStruct((DENSE // 8, 128), BF16)], "v", [pltpu.VMEM((4 * Y_ROWS, 128), F32)]
    )(at, own, *[move(own, 1, d) for d in (1, 2, 3)])[0]


def relation_gather_x(at, own):
    own = kernel(gather_x, "svvvv", [jax.ShapeDtypeStruct((DENSE // 2, 128), BF16)], "v")(
        at, own, *[move(own, 0, d) for d in (1, 2, 3)]
    )[0]
    return own, lax.ppermute(own, "edge", edge_pairs(0, 0, 1))


def shards(entities, ent_accum, relations, rel_accum, heads, tails, negatives, rel_ids):
    steps = heads.shape[1]
    shape = jax.ShapeDtypeStruct
    wire = shape((OWN, 128, 128), BF16)
    held = pltpu.VMEM((OWN, 128, 128), BF16)
    table, accum = entities, ent_accum.reshape(8, 128)
    rel_count = relations.shape[0]
    rel_table = jnp.pad(relations, ((0, REL - rel_count), (0, 0)))
    rel_state = jnp.pad(rel_accum, (0, REL - rel_count), constant_values=1.0).reshape(8, 128)
    edge = lax.axis_index("edge")
    at = jnp.stack([lax.axis_index("rep"), edge // 16, edge // 2 % 8, edge % 2]).astype(I32)
    send, negative, slots = kernel(
        prepare,
        "hhh",
        [shape((OWN, 128), I32), shape((OWN, 128), F32), shape((steps, 256), I32)],
        "hvv",
        [pltpu.VMEM(x.shape, I32) for x in (heads, tails, negatives)] + [pltpu.VMEM((OWN, 128), I32), copies(4)],
    )(heads, tails, negatives)
    named = exchange(send.reshape(OWN, 1, 128)).reshape(OWN, 128)
    wide = kernel(widen, "v", [shape((1024, 512), BF16)], "v")(table)[0]
    flat = jnp.stack([named[:, CAP * s : CAP * s + CAP].reshape(SLOTS) for s in range(steps)])
    negative = jnp.stack([negative[:, CAP * s : CAP * s + CAP].reshape(SLOTS) for s in range(steps)])
    rows = kernel(first_rows, "vv", [wire], "h", [held, copies(8)], 3 << 30)(wide, named)[0]
    for s in range(steps):
        last = s == steps - 1
        relation = kernel(
            lambda *refs, s=s: relation_rows(s, *refs), "vv", [shape((128, WIDTH), F32)], "v"
        )(rel_table, rel_ids)[0]
        rows = exchange(rows)
        dense = shape((DENSE // 2, 128), F32)
        wires = [shape((OWN, n, 128), BF16) for n in ((FIRST_ROWS, 128 - FIRST_ROWS) if last else (128,))]
        *grads, keep, give = kernel(
            lambda *refs, s=s: block(s, *refs),
            "shvvvv",
            wires + [dense, dense],
            "h" * len(wires) + "hh",
            [
                pltpu.VMEM((SLOTS, 512), BF16), pltpu.VMEM((256, SLOTS), BF16), held, copies(WIRE_PARTS), held,
                pltpu.SemaphoreType.DMA((2, 4)), pltpu.VMEM((2, DENSE // 2, 128), F32),
                pltpu.SemaphoreType.DMA((2, REL // 128)),
            ],
            4 << 30,
        )(at, rows, slots, negative, relation, rel_ids)
        grads[0] = exchange(grads[0])
        own, arrived = relation_scatter(at, keep, give, last)
        scratch = [copies(WIRE_PARTS), pltpu.SemaphoreType.DMA, copies(8)]
        outs = [shape(table.shape, F32), shape((8, 128), F32)]
        if last:
            second = kernel(pass_on, "ha", [wires[1]], "h", aliases={0: 0})(grads[1], own)[0]
            second = exchange(second)
            sums = kernel(
                lambda *refs, s=s: first_sums(s, *refs),
                "hv",
                [shape((1024, 256), F32)],
                "v",
                [copies(WIRE_PARTS), pltpu.VMEM((OWN, FIRST_ROWS, 128), BF16), pltpu.VMEM((SLOTS, 256), BF16)],
                2 << 30,
            )(grads[0], flat)[0]
            scratch += [pltpu.VMEM((OWN, 128 - FIRST_ROWS, 128), BF16), pltpu.VMEM((1024, WIDTH), F32)]
            table, accum = kernel(
                lambda *refs, s=s: last_update(s, *refs),
                "hvvhv",
                [shape((1, WIDTH, 1024), F32), outs[1]],
                "hv",
                scratch + [pltpu.VMEM((SLOTS, 256), BF16), pltpu.VMEM((8, WIDTH, 128), F32)],
                2 << 30,
            )(second, flat, sums, table, accum)
            table = jnp.swapaxes(table, 1, 2)
        else:
            scratch += [held, pltpu.VMEM((1024, WIDTH), F32), pltpu.VMEM((SLOTS, 512), BF16)]
            table, accum, rows = kernel(
                lambda *refs, s=s: update(s, *refs),
                "hvhvv" + "a" * len(arrived),
                outs + [wire],
                "hvh",
                scratch + [pltpu.VMEM((1024, 512), BF16), held, copies(8)],
                5 << 30,
            )(grads[0], flat, table, accum, named, *arrived)
        own = relation_gather_y(at, own)
        mine, other = relation_gather_x(at, own)
        rel_table, rel_state = kernel(
            relation_update,
            "svvvv",
            [shape((WIDTH, rel_count) if last else (REL, WIDTH), F32), shape((8, 128), F32)],
            "vv",
        )(at, mine, other, rel_table, rel_state)
    return table, accum.reshape(1, 1024), rel_table.T, rel_state.reshape(REL)[:rel_count]


def solution(mesh):
    in_specs = (
        P("rep", "edge", None),
        P("rep", "edge"),
        P(),
        P(),
        P("rep", None, "edge"),
        P("rep", None, "edge"),
        P("rep", None, "edge"),
        P("rep", None, "edge"),
    )
    out_specs = (P("rep", "edge", None), P("rep", "edge"), P(), P())
    return jax.shard_map(shards, mesh=mesh, in_specs=in_specs, out_specs=out_specs, check_vma=False)
```

```python
import jax
import jax.numpy as jnp
from jax import lax
from jax.experimental import pallas as pl
from jax.experimental.pallas import tpu as pltpu
from jax.sharding import PartitionSpec as P

F32, BF16, I32 = jnp.float32, jnp.bfloat16, jnp.int32
RATE = 0.1
OWN = 64
CAP = 40
SLOTS = OWN * CAP
WIDTH = 400
HALF = 200
BODY = 384
REL = 1024
DENSE = REL // 64 * 200
WIRE_PARTS = 4
FIRST_ROWS = 2 * CAP
Y_ROWS = 112


def iota(shape, dim):
    return lax.broadcasted_iota(I32, shape, dim)


def one_hot(hit):
    return jnp.where(hit, 1.0, 0.0).astype(BF16)


def dot(a, b, dims=((1,), (0,))):
    return lax.dot_general(a, b, (dims, ((), ())), preferred_element_type=F32)


def fold_tail(x):
    x = x + pltpu.roll(x, 64, 1)
    x = x + pltpu.roll(x, 32, 1)
    return x + pltpu.roll(x, 16, 1)


def spread_tail(x16):
    rows = x16.shape[0]
    return fold_tail(jnp.concatenate([x16, jnp.zeros((rows, 112), F32)], axis=1))


def to_wide(x):
    return jnp.concatenate([x[:, :BODY], spread_tail(x[:, BODY:])], axis=1)


def to_narrow(x):
    return jnp.concatenate([x[:, :BODY], fold_tail(x[:, BODY:])[:, :16]], axis=1)


def pack(rows):
    group = iota((8, 128), 1) // 16
    tail = jnp.zeros((8, 128), F32)
    for i in range(5):
        tail = jnp.where(group == i, rows[8 * i : 8 * i + 8, BODY:], tail)
    return jnp.concatenate([rows[:, :128], rows[:, 128:256], rows[:, 256:384], tail], axis=0)


def unpack(block):
    group = iota((8, 128), 1) // 16
    tail = jnp.concatenate([jnp.where(group == i, block[120:], 0.0) for i in range(5)], axis=0)
    return jnp.concatenate([block[:40], block[40:80], block[80:120], tail], axis=1)


def pack_relations(rows):
    group = iota((8, 128), 1) // 16
    tail = jnp.zeros((8, 128), F32)
    for i in range(8):
        tail = jnp.where(group == i, rows[8 * i : 8 * i + 8, BODY:], tail)
    return jnp.concatenate([rows[:, :128], rows[:, 128:256], rows[:, 256:384], tail], axis=0)


def unpack_relations(dense):
    group = iota((8, 128), 1) // 16
    tail = jnp.concatenate([jnp.where(group == i, dense[192:], 0.0) for i in range(8)], axis=0)
    return to_narrow(jnp.concatenate([dense[:64], dense[64:128], dense[128:192], tail], axis=1))


def wire_copies(wire_ref, held_ref, sems):
    per = OWN // WIRE_PARTS
    return [
        pltpu.make_async_copy(wire_ref.at[pl.ds(per * g, per)], held_ref.at[pl.ds(per * g, per)], sems.at[g])
        for g in range(WIRE_PARTS)
    ]


def unpack_first(block):
    return jnp.concatenate([block[:CAP], block[CAP:]], axis=1)


def unpack_second(block):
    group = iota((8, 128), 1) // 16
    tail = jnp.concatenate([jnp.where(group == i, block[CAP:], 0.0) for i in range(5)], axis=0)
    return jnp.concatenate([block[:CAP], tail], axis=1)


def unpack_all(copies, held_ref, rows_ref, unpack=unpack):
    per = OWN // WIRE_PARTS // 2
    for g, copy in enumerate(copies):
        copy.wait()

        def pair(e, _):
            two = [unpack(held_ref[2 * e + k].astype(F32)) for k in range(2)]
            at = pl.multiple_of(e * 2 * CAP, 2 * CAP)
            rows_ref[pl.ds(at, 2 * CAP), :] = jnp.concatenate(two, axis=0).astype(BF16)
            return 0

        lax.fori_loop(per * g, per * g + per, pair, 0)


def lane_to_column(row):
    return jnp.transpose(jnp.broadcast_to(row, (128, 128)))


def prepare(heads_in, tails_in, negatives_in, send_ref, negative_ref, slots_ref, heads_ref, tails_ref, negatives_ref, held_ref, sems):
    count = 2 * heads_ref.shape[2] + negatives_ref.shape[2]
    steps = heads_ref.shape[1]
    fetches = [
        pltpu.make_async_copy(source, held, sems.at[k])
        for k, (source, held) in enumerate(
            ((heads_in, heads_ref), (tails_in, tails_ref), (negatives_in, negatives_ref))
        )
    ]
    for copy in fetches:
        copy.start()
    for copy in fetches:
        copy.wait()
    before = one_hot(iota((128, 128), 0) < iota((128, 128), 1))
    send = jnp.zeros((OWN, 128), F32)
    negative = jnp.zeros((OWN, 128), F32)
    for s in range(steps):
        requests = jnp.concatenate(
            [heads_ref[0, s : s + 1, :], tails_ref[0, s : s + 1, :], negatives_ref[0, s : s + 1, :]], axis=1
        )
        owner = lax.shift_right_logical(requests, 10)
        local = requests & 1023
        at_owner = jnp.where(iota((OWN, count), 0) == owner, 1.0, 0.0)
        seen = jnp.zeros((OWN, 1), F32)
        ranks = []
        for j in range(count // 128):
            part = at_owner[:, 128 * j : 128 * j + 128]
            earlier = dot(part.astype(BF16), before) + seen
            ranks.append(jnp.sum(part * earlier, axis=0, keepdims=True))
            seen = seen + jnp.sum(part, axis=1, keepdims=True)
        rank = jnp.concatenate(ranks, axis=1).astype(I32)
        at_rank = one_hot(iota((128, count), 0) == rank + CAP * s)
        high = (at_owner * lax.shift_right_logical(local, 5).astype(F32)).astype(BF16)
        low = (at_owner * (local & 31).astype(F32)).astype(BF16)
        last = ((1,), (1,))
        send = send + dot(high, at_rank, last) * 32.0 + dot(low, at_rank, last)
        chosen = jnp.where(iota((OWN, count), 1) >= 256, at_owner, 0.0).astype(BF16)
        negative = negative + dot(chosen, at_rank, last)
        slots_ref[s : s + 1, :] = (owner * CAP + rank)[:, :256]
    held_ref[...] = send.astype(I32)
    sending = pltpu.make_async_copy(held_ref, send_ref, sems.at[3])
    sending.start()
    negative_ref[...] = negative
    sending.wait()


def gather_rows(named_ref, step, wide_ref, wire_ref, held_ref, sems):
    named = named_ref[...].astype(F32)
    named = jnp.transpose(jnp.concatenate([named, named], axis=0))
    named = named[CAP * step : CAP * step + CAP, :OWN].astype(I32)
    per = OWN // 8
    copies = []
    for g in range(8):
        columns = jnp.concatenate([named[:, per * g + j : per * g + j + 1] for j in range(per)], axis=0)
        hit = one_hot(columns == iota((per * CAP, 1024), 1))
        rows = dot(hit, wide_ref[...])
        for j in range(per):
            held_ref[per * g + j] = pack(rows[CAP * j : CAP * j + CAP]).astype(BF16)
        here = pl.ds(per * g, per)
        copies.append(pltpu.make_async_copy(held_ref.at[here], wire_ref.at[here], sems.at[g]))
        copies[-1].start()
    for copy in copies:
        copy.wait()


def widen(table_ref, wide_ref):
    wide_ref[...] = to_wide(table_ref[0]).astype(BF16)


def first_rows(wide_ref, named_ref, wire_ref, held_ref, sems):
    gather_rows(named_ref, 0, wide_ref, wire_ref, held_ref, sems)


def to_columns(state_ref):
    return jnp.transpose(jnp.concatenate([state_ref[...], jnp.zeros((120, 128), F32)], axis=0))


def adagrad(b, total, old, states):
    state = states[:, b : b + 1] + jnp.sum(total * total, axis=1, keepdims=True) / WIDTH
    new = old - total * (RATE * lax.rsqrt(state))
    return new, jnp.where(iota((128, 128), 1) == b, state, states)


def apply_rows(b, total, accum_ref, new_accum_ref, rows_ref):
    accum = lane_to_column(accum_ref[b : b + 1, :])
    accum = accum + jnp.sum(total * total, axis=1, keepdims=True) / WIDTH
    new_accum_ref[b : b + 1, :] = jnp.transpose(accum)[:1]
    return rows_ref[128 * b : 128 * b + 128, :] - total * (RATE * lax.rsqrt(accum[:, :1]))


def update(
    step, wire_in_ref, flat_ref, table_ref, accum_ref, named_ref, *rest
):
    new_table_ref, new_accum_ref, wire_ref, in_sems, table_sem, out_sems, *rest = rest[7:]
    held_ref, rows_ref, grads_ref, wide_ref, sent_ref, sent_sems = rest
    copies = wire_copies(wire_in_ref, held_ref, in_sems)
    for copy in copies:
        copy.start()
    table_copy = pltpu.make_async_copy(table_ref.at[0], rows_ref, table_sem)
    table_copy.start()
    unpack_all(copies, held_ref, grads_ref)
    table_copy.wait()
    outs = []
    for b in range(8):
        here = pl.ds(128 * b, 128)
        hit = one_hot(iota((128, SLOTS), 0) + 128 * b == flat_ref[step : step + 1, :])
        total = to_narrow(dot(hit, grads_ref[...]))
        new = apply_rows(b, total, accum_ref, new_accum_ref, rows_ref)
        rows_ref[here, :] = new
        outs.append(pltpu.make_async_copy(rows_ref.at[here], new_table_ref.at[0, here], out_sems.at[b]))
        outs[-1].start()
        wide_ref[here, :] = to_wide(new).astype(BF16)
    gather_rows(named_ref, step + 1, wide_ref, wire_ref, sent_ref, sent_sems)
    for copy in outs:
        copy.wait()


def last_update(
    step, first_ref, second_ref, flat_ref, table_ref, accum_ref, new_table_ref, new_accum_ref,
    first_sems, second_sems, table_sem, out_sems, first_held_ref, second_held_ref, rows_ref, grads_ref, turned_ref,
):
    firsts = wire_copies(first_ref, first_held_ref, first_sems)
    seconds = wire_copies(second_ref, second_held_ref, second_sems)
    for copy in firsts + seconds:
        copy.start()
    table_copy = pltpu.make_async_copy(table_ref.at[0], rows_ref, table_sem)
    table_copy.start()
    unpack_all(firsts, first_held_ref, grads_ref.at[:, pl.ds(0, 256)], unpack_first)
    unpack_all(seconds, second_held_ref, grads_ref.at[:, pl.ds(256, 256)], unpack_second)
    table_copy.wait()
    outs = []
    for b in range(8):
        here = pl.ds(128 * b, 128)
        hit = one_hot(iota((128, SLOTS), 0) + 128 * b == flat_ref[step : step + 1, :])
        total = to_narrow(dot(hit, grads_ref[...]))
        turned_ref[b] = jnp.transpose(apply_rows(b, total, accum_ref, new_accum_ref, rows_ref))
        outs.append(pltpu.make_async_copy(turned_ref.at[b], new_table_ref.at[0, :, here], out_sems.at[b]))
        outs[-1].start()
    for copy in outs:
        copy.wait()


def pass_on(ref, *rest):
    del ref, rest


def complex_parts(x):
    return x[:, :HALF], x[:, HALF:]


def join(re, im):
    return jnp.concatenate([re, im], axis=1)


def split3(x):
    a = x.astype(BF16)
    x = x - a.astype(F32)
    b = x.astype(BF16)
    return a, b, (x - b.astype(F32)).astype(BF16)


def relation_rows(step, table_ref, rel_ids_ref, out_ref):
    rel_ids = rel_ids_ref[0, step : step + 1, :]
    column = lane_to_column(rel_ids.astype(F32))[:, :1].astype(I32)
    hit = one_hot(column == iota((rel_ids.shape[1], REL), 1))
    out_ref[...] = sum(dot(hit, piece) for piece in reversed(split3(table_ref[...])))


def block(
    step, at_ref, wire_in_ref, slots_ref, negative_ref, relation_ref, rel_ids_ref, *rest
):
    *rest, sent_ref, out_sems, kept_ref, keep_sems = rest
    *wire_refs, keep_ref, give_ref, rows_ref, weights_ref, held_ref, in_sems = rest
    edges, parts = 128, 4
    part = SLOTS // parts
    per = OWN // parts
    copies = wire_copies(wire_in_ref, held_ref, in_sems)
    for copy in copies:
        copy.start()
    unpack_all(copies, held_ref, rows_ref)
    slots = slots_ref[step : step + 1, :]
    slots_column = jnp.concatenate(
        [lane_to_column(slots[:, 128 * k : 128 * k + 128].astype(F32))[:, :1] for k in range(2)], axis=0
    ).astype(I32)
    fetched = jnp.zeros((2 * edges, 512), F32)
    for g in range(parts):
        here = slice(part * g, part * g + part)
        hit = one_hot(slots_column == iota((2 * edges, part), 1) + part * g)
        fetched = fetched + dot(hit, rows_ref[here, :])
    fetched = to_narrow(fetched)
    head, tail = fetched[:edges], fetched[edges:]
    head_re, head_im = complex_parts(head)
    tail_re, tail_im = complex_parts(tail)
    rel_re, rel_im = complex_parts(relation_ref[...])
    query_tail = join(head_re * rel_re - head_im * rel_im, head_re * rel_im + head_im * rel_re)
    query_head = join(rel_re * tail_re + rel_im * tail_im, rel_re * tail_im - rel_im * tail_re)
    positive = jnp.sum(query_tail * tail, axis=1, keepdims=True)
    queries = to_wide(jnp.concatenate([query_tail, query_head], axis=0)).astype(BF16)
    pull = jnp.zeros((2 * edges, 512), F32)
    for g in range(parts):
        here = slice(part * g, part * g + part)
        scores = dot(queries, rows_ref[here, :], ((1,), (1,)))
        weights = jax.nn.sigmoid(scores) * (negative_ref[step : step + 1, here] / 1024)
        weights = weights.astype(BF16)
        weights_ref[:, here] = weights
        pull = pull + dot(weights, rows_ref[here, :])
    pull = to_narrow(pull)
    positive_weight = -jax.nn.sigmoid(-positive)
    pull_re, pull_im = complex_parts(positive_weight * tail + pull[:edges])
    push_re, push_im = complex_parts(pull[edges:])
    grad_head = join(pull_re * rel_re + pull_im * rel_im, pull_im * rel_re - pull_re * rel_im)
    grad_tail = positive_weight * query_tail + join(
        push_re * rel_re - push_im * rel_im, push_re * rel_im + push_im * rel_re
    )
    edge_grads = to_wide(jnp.concatenate([grad_head, grad_tail], axis=0)).astype(BF16)
    outs = []
    for g in range(parts):
        here = slice(part * g, part * g + part)
        grads = dot(weights_ref[:, here], queries, ((0,), (0,)))
        hit = one_hot(iota((part, 2 * edges), 0) + part * g == slots)
        grads = grads + dot(hit, edge_grads)
        for j in range(per):
            sent_ref[per * g + j] = pack(grads[CAP * j : CAP * j + CAP]).astype(BF16)
        blocks = pl.ds(per * g, per)
        start = 0
        for k, wire_ref in enumerate(wire_refs):
            dense = pl.ds(start, wire_ref.shape[1])
            start += wire_ref.shape[1]
            outs.append(
                pltpu.make_async_copy(sent_ref.at[blocks, dense], wire_ref.at[blocks], out_sems.at[k, g])
            )
            outs[-1].start()
    grad_relation = to_wide(
        join(
            pull_re * head_re + pull_im * head_im + push_re * tail_re + push_im * tail_im,
            pull_im * head_re - pull_re * head_im + push_re * tail_im - push_im * tail_re,
        )
    )
    high = grad_relation.astype(BF16)
    low = (grad_relation - high.astype(F32)).astype(BF16)
    rel_ids = rel_ids_ref[0, step : step + 1, :]
    half = REL // 128
    for i in range(half):
        dense = []
        for k in range(2):
            hit = one_hot(iota((64, edges), 0) + 64 * (half * k + i) == rel_ids)
            dense.append(pack_relations(dot(hit, high) + dot(hit, low)))
        here = slice(200 * i, 200 * i + 200)
        kept_ref[0, here, :] = jnp.where(at_ref[3] == 0, dense[0], dense[1])
        kept_ref[1, here, :] = jnp.where(at_ref[3] == 0, dense[1], dense[0])
        dense = pl.ds(200 * i, 200)
        for k, out_ref in enumerate((give_ref, keep_ref)):
            outs.append(
                pltpu.make_async_copy(kept_ref.at[1 - k, dense], out_ref.at[dense], keep_sems.at[k, i])
            )
            outs[-1].start()
    for copy in outs:
        copy.wait()


def scatter_stage(axis, at_ref, own_ref, *refs):
    n = (4, 4)[axis]
    arrived, outs, sum_ref = refs[: -n - 1], refs[-n - 1 : -1], refs[-1]
    total = own_ref[...].astype(F32)
    for ref in arrived:
        total = total + ref[...].astype(F32)
    sum_ref[: total.shape[0], :] = total
    rows = outs[0].shape[0]
    if total.shape[0] < n * rows:
        sum_ref[total.shape[0] :, :] = jnp.zeros((n * rows - total.shape[0], 128), F32)
    for d in range(n):
        start = pl.multiple_of(lax.rem(at_ref[axis] + d, n) * rows, 8)
        outs[d][...] = sum_ref[pl.ds(start, rows), :].astype(outs[d].dtype)


def sum_y(own_ref, *refs):
    *parts, out_ref = refs
    total = own_ref[...]
    for ref in parts:
        total = total + ref[...]
    out_ref[...] = total.astype(BF16)


def sum_z(at_ref, *refs):
    *parts, out_ref, all_ref = refs
    n = len(parts)
    for d in range(n):
        all_ref[lax.rem(at_ref[2] + 8 - d, n)] = parts[d][...].astype(F32)
    total = all_ref[0]
    for z in range(1, n):
        total = total + all_ref[z]
    out_ref[...] = total


def gather_y(at_ref, *refs):
    *parts, out_ref, all_ref = refs
    rows = parts[0].shape[0]
    for d in range(4):
        start = pl.multiple_of(lax.rem(at_ref[1] + 4 - d, 4) * rows, 8)
        all_ref[pl.ds(start, rows), :] = parts[d][...]
    out_ref[...] = all_ref[: out_ref.shape[0], :].astype(BF16)


def gather_x(at_ref, *refs):
    *parts, out_ref = refs
    rows = parts[0].shape[0]
    for d in range(4):
        start = pl.multiple_of(lax.rem(at_ref[0] + 4 - d, 4) * rows, 16)
        out_ref[pl.ds(start, rows), :] = parts[d][...]


def relation_update(at_ref, mine_ref, other_ref, table_ref, state_ref, new_table_ref, new_state_ref):
    count = REL // 128
    states = to_columns(state_ref)
    for b in range(count):
        rows = slice(128 * b, 128 * b + 128)
        here = slice(400 * (b % (count // 2)), 400 * (b % (count // 2)) + 400)
        mine, other = mine_ref[here, :], other_ref[here, :]
        dense = jnp.where(at_ref[3] == b // (count // 2), mine, other).astype(F32)
        total = jnp.concatenate([unpack_relations(dense[:200]), unpack_relations(dense[200:])], axis=0)
        new, states = adagrad(b, total, table_ref[rows, :], states)
        if new_table_ref.shape[0] == REL:
            new_table_ref[rows, :] = new
        else:
            end = min(128 * b + 128, new_table_ref.shape[1])
            new_table_ref[:, 128 * b : end] = jnp.transpose(new)[:, : end - 128 * b]
    new_state_ref[...] = jnp.transpose(states)[:8]


SPACES = {
    "s": pl.BlockSpec(memory_space=pltpu.SMEM),
    "v": pl.BlockSpec(memory_space=pltpu.VMEM),
    "h": pl.BlockSpec(memory_space=pltpu.HBM),
    "a": pl.BlockSpec(memory_space=pl.ANY),
}


def kernel(body, ins, outs, places, scratch=(), flops=0, aliases=None):
    call = pl.pallas_call(
        body,
        out_shape=[pltpu.HBM(o.shape, o.dtype) if k == "h" else o for o, k in zip(outs, places)],
        in_specs=[SPACES[k] for k in ins],
        out_specs=[SPACES[k] for k in places],
        scratch_shapes=scratch,
        input_output_aliases=aliases or {},
        compiler_params=pltpu.CompilerParams(vmem_limit_bytes=30 << 20),
        cost_estimate=pl.CostEstimate(flops=flops, bytes_accessed=1 << 20, transcendentals=0),
    )
    return lambda *args: call(
        *[pltpu.with_memory_space_constraint(x, pltpu.HBM) if k == "h" else x for x, k in zip(args, ins)]
    )


def copies(n):
    return pltpu.SemaphoreType.DMA((n,))


def exchange(x):
    return lax.all_to_all(x, "edge", split_axis=0, concat_axis=0, tiled=True)


def edge_of(y, z, core):
    return (y * 8 + z) * 2 + core


def edge_pairs(dy, dz, flip=0):
    return [
        (edge_of(y, z, core), edge_of((y + dy) % 4, (z + dz) % 8, core ^ flip))
        for y in range(4)
        for z in range(8)
        for core in range(2)
    ]


def move(x, axis, d):
    if axis == 0:
        return lax.ppermute(x, "rep", [(k, (k + d) % 4) for k in range(4)])
    return lax.ppermute(x, "edge", edge_pairs(d if axis == 1 else 0, d if axis == 2 else 0))


def relation_scatter(at, keep, give):
    shape = jax.ShapeDtypeStruct
    arrived = [lax.ppermute(give, "edge", edge_pairs(0, 0, 1))]
    own = keep
    for axis, (rows, sent) in enumerate(((DENSE // 8, BF16), (Y_ROWS, F32))):
        own, *parts = kernel(
            lambda *refs, axis=axis: scatter_stage(axis, *refs),
            "sv" + "v" * len(arrived),
            [shape((rows, 128), F32)] + [shape((rows, 128), sent)] * 3,
            "vvvv",
            [pltpu.VMEM((4 * rows, 128), F32)],
        )(at, own, *arrived)
        arrived = [move(part, axis, d + 1) for d, part in enumerate(parts)]
    own = kernel(sum_y, "vvvv", [shape(own.shape, BF16)], "v")(own, *arrived)[0]
    n = 8
    arrived = [move(own, 2, d) for d in range(1, n)]
    own = kernel(sum_z, "s" + "v" * n, [shape(own.shape, F32)], "v", [pltpu.VMEM((n, *own.shape), F32)])(
        at, own, *arrived
    )[0]
    return own, arrived


def relation_gather_y(at, own):
    return kernel(
        gather_y, "svvvv", [jax.ShapeDtypeStruct((DENSE // 8, 128), BF16)], "v", [pltpu.VMEM((4 * Y_ROWS, 128), F32)]
    )(at, own, *[move(own, 1, d) for d in (1, 2, 3)])[0]


def relation_gather_x(at, own):
    own = kernel(gather_x, "svvvv", [jax.ShapeDtypeStruct((DENSE // 2, 128), BF16)], "v")(
        at, own, *[move(own, 0, d) for d in (1, 2, 3)]
    )[0]
    return own, lax.ppermute(own, "edge", edge_pairs(0, 0, 1))


def shards(entities, ent_accum, relations, rel_accum, heads, tails, negatives, rel_ids):
    steps = heads.shape[1]
    shape = jax.ShapeDtypeStruct
    wire = shape((OWN, 128, 128), BF16)
    held = pltpu.VMEM((OWN, 128, 128), BF16)
    table, accum = entities, ent_accum.reshape(8, 128)
    rel_count = relations.shape[0]
    rel_table = jnp.pad(relations, ((0, REL - rel_count), (0, 0)))
    rel_state = jnp.pad(rel_accum, (0, REL - rel_count), constant_values=1.0).reshape(8, 128)
    edge = lax.axis_index("edge")
    at = jnp.stack([lax.axis_index("rep"), edge // 16, edge // 2 % 8, edge % 2]).astype(I32)
    send, negative, slots = kernel(
        prepare,
        "hhh",
        [shape((OWN, 128), I32), shape((OWN, 128), F32), shape((steps, 256), I32)],
        "hvv",
        [pltpu.VMEM(x.shape, I32) for x in (heads, tails, negatives)] + [pltpu.VMEM((OWN, 128), I32), copies(4)],
    )(heads, tails, negatives)
    named = exchange(send.reshape(OWN, 1, 128)).reshape(OWN, 128)
    wide = kernel(widen, "v", [shape((1024, 512), BF16)], "v")(table)[0]
    flat = jnp.stack([named[:, CAP * s : CAP * s + CAP].reshape(SLOTS) for s in range(steps)])
    negative = jnp.stack([negative[:, CAP * s : CAP * s + CAP].reshape(SLOTS) for s in range(steps)])
    rows = kernel(first_rows, "vv", [wire], "h", [held, copies(8)], 3 << 30)(wide, named)[0]
    for s in range(steps):
        last = s == steps - 1
        relation = kernel(
            lambda *refs, s=s: relation_rows(s, *refs), "vv", [shape((128, WIDTH), F32)], "v"
        )(rel_table, rel_ids)[0]
        rows = exchange(rows)
        dense = shape((DENSE // 2, 128), F32)
        wires = [shape((OWN, n, 128), BF16) for n in ((FIRST_ROWS, 128 - FIRST_ROWS) if last else (128,))]
        *grads, keep, give = kernel(
            lambda *refs, s=s: block(s, *refs),
            "shvvvv",
            wires + [dense, dense],
            "h" * len(wires) + "hh",
            [
                pltpu.VMEM((SLOTS, 512), BF16), pltpu.VMEM((256, SLOTS), BF16), held, copies(WIRE_PARTS), held,
                pltpu.SemaphoreType.DMA((2, 4)), pltpu.VMEM((2, DENSE // 2, 128), F32),
                pltpu.SemaphoreType.DMA((2, REL // 128)),
            ],
            4 << 30,
        )(at, rows, slots, negative, relation, rel_ids)
        grads[0] = exchange(grads[0])
        own, arrived = relation_scatter(at, keep, give)
        scratch = [copies(WIRE_PARTS), pltpu.SemaphoreType.DMA, copies(8)]
        outs = [shape(table.shape, F32), shape((8, 128), F32)]
        if last:
            second = kernel(pass_on, "haa", [wires[1]], "h", aliases={0: 0})(grads[1], own, grads[0])[0]
            second = exchange(second)
            table, accum = kernel(
                lambda *refs, s=s: last_update(s, *refs),
                "hhvhv",
                [shape((1, WIDTH, 1024), F32), outs[1]],
                "hv",
                [
                    copies(WIRE_PARTS), *scratch,
                    pltpu.VMEM((OWN, FIRST_ROWS, 128), BF16), pltpu.VMEM((OWN, 128 - FIRST_ROWS, 128), BF16),
                    pltpu.VMEM((1024, WIDTH), F32), pltpu.VMEM((SLOTS, 512), BF16), pltpu.VMEM((8, WIDTH, 128), F32),
                ],
                4 << 30,
            )(grads[0], second, flat, table, accum)
            table = jnp.swapaxes(table, 1, 2)
        else:
            scratch += [held, pltpu.VMEM((1024, WIDTH), F32), pltpu.VMEM((SLOTS, 512), BF16)]
            table, accum, rows = kernel(
                lambda *refs, s=s: update(s, *refs),
                "hvhvv" + "a" * len(arrived),
                outs + [wire],
                "hvh",
                scratch + [pltpu.VMEM((1024, 512), BF16), held, copies(8)],
                5 << 30,
            )(grads[0], flat, table, accum, named, *arrived)
        own = relation_gather_y(at, own)
        mine, other = relation_gather_x(at, own)
        rel_table, rel_state = kernel(
            relation_update,
            "svvvv",
            [shape((WIDTH, rel_count) if last else (REL, WIDTH), F32), shape((8, 128), F32)],
            "vv",
        )(at, mine, other, rel_table, rel_state)
    return table, accum.reshape(1, 1024), rel_table.T, rel_state.reshape(REL)[:rel_count]


def solution(mesh):
    in_specs = (
        P("rep", "edge", None),
        P("rep", "edge"),
        P(),
        P(),
        P("rep", None, "edge"),
        P("rep", None, "edge"),
        P("rep", None, "edge"),
        P("rep", None, "edge"),
    )
    out_specs = (P("rep", "edge", None), P("rep", "edge"), P(), P())
    return jax.shard_map(shards, mesh=mesh, in_specs=in_specs, out_specs=out_specs, check_vma=False)
```
